32 devices in a mesh: dp: 16 (over z, x, core), tensor: 2 (over y).
Axes of the slice: x: 2, y: 2, z: 4, core: 2. Of those that a mesh axis runs over, the one named last changes fastest.
Arguments:
- tokens: bfloat16 [16384, 768], P('dp'), may hold values from -6 to 6
- conditioning: bfloat16 [16, 128], P('dp'), may hold values from -6 to 6
- lengths: int32 [16, 8], P('dp'), may hold values from 0 to 1024, as said below
- input_weight: bfloat16 [3, 768, 768], P(None, None, 'tensor'), may hold values from -0.21875 to 0.21875
- output_weight: bfloat16 [768, 768], P('tensor'), may hold values from -0.875 to 0.875
- up_weight: bfloat16 [768, 3072], P(None, 'tensor'), may hold values from -0.21875 to 0.21875
- up_bias: bfloat16 [3072], P('tensor'), may hold values from -3 to 3
- down_weight: bfloat16 [3072, 768], P('tensor'), may hold values from -0.109375 to 0.109375
- down_bias: bfloat16 [768], replicated, may hold values from -3 to 3
- attention_gain: bfloat16 [768], replicated, may hold values from 0.5 to 1.5
- feed_gain: bfloat16 [768], replicated, may hold values from 0.5 to 1.5
- adaptive_weight: bfloat16 [128, 4608], replicated, may hold values from -0.25 to 0.25
- adaptive_bias: bfloat16 [4608], replicated, may hold values from -1.796875 to 1.796875
- cotangent: bfloat16 [16384, 768], P('dp'), may hold values from -8 to 8
Outputs:
- mixed: bfloat16 [16384, 768], P(('dp', 'tensor'))
- tokens_grad: float32 [16384, 768], P(('dp', 'tensor'))
- input_weight_grad: float32 [3, 768, 768], P(None, 'dp', 'tensor')
- output_weight_grad: float32 [768, 768], P('tensor', 'dp')
- up_weight_grad: float32 [768, 3072], P('dp', 'tensor')
- up_bias_grad: float32 [3072], P('tensor')
- down_weight_grad: float32 [3072, 768], P('tensor', 'dp')
- down_bias_grad: float32 [768], replicated
- attention_gain_grad: float32 [768], replicated
- feed_gain_grad: float32 [768], replicated
- adaptive_weight_grad: float32 [128, 4608], replicated
- adaptive_bias_grad: float32 [4608], replicated
The draws below stay inside these ranges and needn't reach their ends.
Inputs may be any that keep to these rules, and one draw needn't show every extreme that they name: Each row lists the lengths of the sequences packed into it, in order, each 128, 512 or 1024, followed by zeros; a row's lengths sum to at most 1024, and the slots beyond the sum are padding. Every row has a sequence that holds both slot 511 and slot 512, and every draw has a row that is one sequence of 1024.
All inputs are finite; a program needn't handle non-finite values.
Results may differ from the reference program's by a relative error of at most 0.012.
The reference program's roundings to bfloat16 on the way count: a program that leaves them out, or rounds other values in their place, can miss the bound.
Values may be sent and summed in bfloat16 or wider, within the bound.
No kernel may reach another device: no remote copies, remote signals or barrier semaphores. Data moves between devices by JAX's collectives and lax.ppermute only.
A program may use at most 256 MiB of HBM per device.

```python
import jax
import jax.numpy as jnp
import numpy as np
from jax import lax

D = 768
H = 12
HD = 64
FF = 3072
COND = 128
ROW_LEN = 1024
NSEG = 8
ROWS = 16
TOKENS = 16384


def draw_lengths(key, part):
    key = jax.random.fold_in(key, 7)
    pick_key, forced_key = jax.random.split(key)
    table = np.array([[8, 0, 0, 0, 0, 0, 0, 0], [1, 4, 1, 1, 0, 0, 0, 0], [1, 1, 4, 1, 0, 0, 0, 0], [1, 1, 1, 4, 0, 0, 0, 0], [1, 4, 1, 1, 1, 0, 0, 0], [1, 1, 4, 0, 0, 0, 0, 0]], dtype=np.int32)
    patterns = jnp.array(table, dtype=jnp.int32) * (ROW_LEN // 8)
    row_kinds = jax.random.randint(pick_key, (ROWS,), 0, 6, dtype=jnp.int32)
    forced = jax.random.randint(forced_key, (), 0, ROWS, dtype=jnp.int32)
    row_kinds = jnp.where(jnp.arange(ROWS, dtype=jnp.int32) == forced, 0, row_kinds)
    return jnp.take(patterns, row_kinds, axis=0).astype(jnp.int32)


def strengthened(values, rng, source, target, parts, factor):
    def block_of(axis_at):
        return (jnp.arange(values.shape[axis_at]) // (values.shape[axis_at] // parts)).reshape((-1,) + (1,) * (values.ndim - 1 - axis_at))

    first = jax.random.permutation(rng, parts)[block_of(target)]
    other_side = (block_of(target) + parts // 2) % parts
    return jnp.where((block_of(source) == first) | (block_of(source) == other_side), factor * values, values)


def block_levels(rng, extent, cuts, smallest, high):
    level, own = 1.0, jax.random.fold_in(rng, 6)
    for dim, shards_of in cuts:
        heights = jnp.exp(jax.random.uniform(jax.random.fold_in(own, dim), (shards_of,), jnp.float32, smallest / len(cuts), high / len(cuts)))
        level = level * jnp.repeat(heights, extent[dim] // shards_of).reshape([-1 if axis == dim else 1 for axis in range(len(extent))])
    return level


def bell_draw(stream_key, extent, spread, most, cuts=(), kind=jnp.bfloat16):
    factor_of = block_levels(stream_key, extent, cuts, -0.22, 0.18) if cuts else 1.0
    drawn = jax.random.normal(stream_key, extent, jnp.float32) * spread * factor_of
    return jnp.minimum(jnp.maximum(drawn, -most), most).astype(kind)


def heavy_noise(key, dims, spread, reach, shards, heavy, kind=jnp.bfloat16):
    values = spread * jax.random.normal(key, dims, jnp.float32)
    if shards:
        values = values * block_levels(key, dims, shards, -0.22, 0.18)
    return jnp.clip(strengthened(values, jax.random.fold_in(key, 3), *heavy), -reach, reach).astype(kind)


def setup_inputs(seed: int = 0) -> dict:
    seeds = jax.random.split(jax.random.key(seed), 15)
    return {
        "tokens": bell_draw(seeds[0], (TOKENS, D), 1.0, 6.0, ((0, 16),)),
        "conditioning": bell_draw(seeds[1], (ROWS, COND), 1.0, 6.0, ((0, 16),)),
        "lengths": draw_lengths(jax.random.fold_in(seeds[14], 71), 0),
        "input_weight": bell_draw(seeds[3], (3, D, D), D ** -0.5, 0.21875, ((2, 2),)),
        "output_weight": bell_draw(seeds[4], (D, D), (D // 16) ** -0.5, 0.875, ((0, 2),)),
        "up_weight": bell_draw(seeds[5], (D, FF), D ** -0.5, 0.21875, ((1, 2),)),
        "up_bias": bell_draw(seeds[6], (FF,), 0.5, 3.0, ((0, 2),)),
        "down_weight": bell_draw(seeds[7], (FF, D), FF ** -0.5, 0.109375, ((0, 2),)),
        "down_bias": bell_draw(seeds[8], (D,), 0.5, 3.0),
        "attention_gain": jnp.clip(1.0 + 0.1 * jax.random.normal(seeds[9], (D,), jnp.float32), 0.5, 1.5).astype(jnp.bfloat16),
        "feed_gain": jnp.clip(1.0 + 0.1 * jax.random.normal(seeds[10], (D,), jnp.float32), 0.5, 1.5).astype(jnp.bfloat16),
        "adaptive_weight": bell_draw(seeds[11], (COND, 6 * D), (4 * COND) ** -0.5, 0.25),
        "adaptive_bias": bell_draw(seeds[12], (6 * D,), 0.3, 1.796875),
        "cotangent": heavy_noise(seeds[13], (TOKENS, D), 1.0, 8.0, ((0, 16),), (0, 1, 16, 2.0)),
    }


norm_eps = 1e-05
masked_score = -1000000000.0
precise = lax.Precision.HIGHEST
rotary_base = 10000.0

@jax.custom_vjp
def low(v):
    return lax.optimization_barrier(v.astype(jnp.bfloat16)).astype(jnp.float32)

@jax.custom_vjp
def low_back(v):
    return v

def low_keep(v):
    return (low(v), None)

def low_pass(kept, grad):
    return (grad,)

def back_keep(v):
    return (v, None)

def back_low(kept, grad):
    return (low(grad),)
low.defvjp(low_keep, low_pass)
low_back.defvjp(back_keep, back_low)

def layout(row_lengths):
    bounds = jnp.cumsum(row_lengths, dtype=jnp.int32)
    slot_ids = jnp.arange(ROW_LEN, dtype=jnp.int32)
    passed = (slot_ids[:, None] >= bounds[None, :]).astype(jnp.int32)
    segment = lax.optimization_barrier(jnp.sum(passed, axis=1, dtype=jnp.int32))
    starts = lax.optimization_barrier(jnp.sum(passed * row_lengths[None, :], axis=1, dtype=jnp.int32))
    return (segment, slot_ids - starts)

def rotary(positions):
    half_dim = HD // 2
    frequency = rotary_base ** (-jnp.arange(half_dim, dtype=jnp.float32) * (2.0 / HD))
    angles = positions.astype(jnp.float32)[:, None] * frequency[None, :]
    cosine = jnp.concatenate([jnp.cos(angles), jnp.cos(angles)], axis=1)
    sine_part = jnp.concatenate([jnp.sin(angles), jnp.sin(angles)], axis=1)
    return (cosine, sine_part)

def rotate(vectors, cosine, sine_part):
    half_dim = HD // 2
    turned = jnp.concatenate([-vectors[..., half_dim:], vectors[..., :half_dim]], axis=-1)
    return vectors * cosine[:, None, :] + turned * sine_part[:, None, :]

def norm_forward(values, norm_gain, norm_shift, norm_scale):
    row_mean = lax.optimization_barrier(jnp.mean(values, axis=-1, keepdims=True))
    centered = values - row_mean
    row_var = lax.optimization_barrier(jnp.mean(centered * centered, axis=-1, keepdims=True))
    return centered * lax.rsqrt(row_var + norm_eps) * norm_gain * (1.0 + norm_scale) + norm_shift

def row_layer(weight_set, row_tokens, row_cond, row_lengths):
    input_weight, output_weight, up_weight, up_bias, down_weight, down_bias, attention_gain, feed_gain, adaptive_weight, adaptive_bias = weight_set
    modulation = jnp.dot(row_cond, adaptive_weight, precision=precise) + adaptive_bias
    shift_attention, scale_attention, gate_attention, shift_feed, scale_feed, gate_feed = jnp.split(modulation, 6)
    segment, positions = layout(row_lengths)
    cosine, sine_part = rotary(positions)
    normed = low(norm_forward(row_tokens, attention_gain, shift_attention, scale_attention))
    projected = jnp.einsum('td,jde->jte', normed, input_weight, precision=precise)
    shaped = (ROW_LEN, H, HD)
    queries = low(rotate(low_back(projected[0]).reshape(shaped), cosine, sine_part) * HD ** (-0.5))
    keys_turned = low(rotate(low_back(projected[1]).reshape(shaped), cosine, sine_part))
    values = low(low_back(projected[2])).reshape(shaped)
    scores = low_back(jnp.einsum('qhd,khd->hqk', queries, keys_turned, precision=precise))
    same_doc = segment[:, None] == segment[None, :]
    scores = jnp.where(same_doc[None], scores, masked_score)
    row_peak = lax.optimization_barrier(jnp.max(scores, axis=-1, keepdims=True))
    exponent = jnp.exp(scores - row_peak)
    probability = exponent / lax.optimization_barrier(jnp.sum(exponent, axis=-1, keepdims=True))
    attended = jnp.einsum('hqk,khd->qhd', low(probability), values, precision=precise).reshape(ROW_LEN, D)
    attended = low(low_back(attended))
    branch = low_back(jnp.dot(attended, output_weight, precision=precise))
    middle = row_tokens + gate_attention * branch
    feed_in = low(norm_forward(middle, feed_gain, shift_feed, scale_feed))
    upward = low_back(jnp.dot(feed_in, up_weight, precision=precise) + up_bias)
    active = low(jax.nn.gelu(upward, approximate=True))
    feed_out = low_back(jnp.dot(active, down_weight, precision=precise) + down_bias)
    return middle + gate_feed * feed_out

def reference(tokens, conditioning, lengths, input_weight, output_weight, up_weight, up_bias, down_weight, down_bias, attention_gain, feed_gain, adaptive_weight, adaptive_bias, cotangent):
    weight_set = tuple((argument.astype(jnp.float32) for argument in (input_weight, output_weight, up_weight, up_bias, down_weight, down_bias, attention_gain, feed_gain, adaptive_weight, adaptive_bias)))
    token_rows = tokens.astype(jnp.float32).reshape(ROWS, ROW_LEN, D)
    cond_rows = conditioning.astype(jnp.float32)

    def forward(token_values, weight_values):

        def row_apply(row_item):
            return row_layer(weight_values, row_item[0], row_item[1], row_item[2])
        return lax.map(jax.checkpoint(row_apply), (token_values, cond_rows, lengths))
    result, pullback = jax.vjp(forward, token_rows, weight_set)
    live_slot = (jax.vmap(layout)(lengths)[0] < NSEG).astype(jnp.float32)
    seed_grad = cotangent.astype(jnp.float32).reshape(ROWS, ROW_LEN, D) * live_slot[..., None]
    token_grad, weight_grads = pullback(seed_grad)
    grad_input, grad_output, grad_up, grad_up_bias, grad_down, grad_down_bias, grad_gain_one, grad_gain_two, grad_adaptive, grad_adaptive_bias = weight_grads
    return (result.reshape(TOKENS, D).astype(jnp.bfloat16), token_grad.reshape(TOKENS, D), grad_input, grad_output, grad_up, grad_up_bias, grad_down, grad_down_bias, grad_gain_one, grad_gain_two, grad_adaptive, grad_adaptive_bias)
```

```python
import functools

import jax
import jax.numpy as jnp
from jax import lax
from jax.experimental import pallas as pl
from jax.experimental.pallas import tpu as pltpu
from jax.sharding import PartitionSpec as P

HD = 64
ROW_LEN = 1024
NSEG = 8
BLOCK = 128
PAIR = 2 * HD
RB = 256
QB_FWD = 256
QB_BWD = 512

norm_eps = 1e-05
masked_score = -1000000000.0
rotary_base = 10000.0
gelu_k = 0.7978845608028654
gelu_c = 0.044715

AXES = ("dp", "tensor")
BF = jnp.bfloat16
F32 = jnp.float32
NN = ((1,), (0,))
NT = ((1,), (1,))
TN = ((0,), (0,))
VMEM = pl.BlockSpec(memory_space=pltpu.VMEM)
SMEM = pl.BlockSpec(memory_space=pltpu.SMEM)


def mm(left, right, dims=NN):
    return lax.dot_general(left, right, (dims, ((), ())), preferred_element_type=F32)


def params(mib):
    return pltpu.CompilerParams(vmem_limit_bytes=mib << 20)


def shape(dims, kind=F32):
    return jax.ShapeDtypeStruct(dims, kind)


def normalize(values):
    centered = values - jnp.mean(values, axis=-1, keepdims=True)
    inverse = lax.rsqrt(jnp.mean(centered * centered, axis=-1, keepdims=True) + norm_eps)
    return centered * inverse, inverse


def norm_pull(cotangent, xhat, inverse, weight):
    e = cotangent * weight
    return inverse * (
        e
        - jnp.mean(e, axis=-1, keepdims=True)
        - xhat * jnp.mean(e * xhat, axis=-1, keepdims=True)
    )


def live_rows(total, first_row, rows):
    slots = lax.broadcasted_iota(jnp.int32, (rows, 1), 0) + first_row
    return (slots < total).astype(F32)


def prep_kernel(mine, own_ref, got_ref, mod_ref, gain_ref, tok_ref, normed_ref):
    keep = mine[0] == 1
    tok = jnp.where(keep, own_ref[...], got_ref[...])
    tok_ref[...] = tok
    xhat, _ = normalize(tok.astype(F32))
    mod = mod_ref[0]
    normed_ref[...] = (xhat * (gain_ref[...] * (1.0 + mod[1:2])) + mod[0:1]).astype(BF)


def row_block(width):
    return pl.BlockSpec((RB, width), lambda i, *_: (i, 0))


def whole(dims):
    return pl.BlockSpec(dims, lambda i, *_: (0,) * len(dims))


def mod_block(width):
    return pl.BlockSpec((1, 6, width), lambda i, *_: (i // (ROW_LEN // RB), 0, 0))


def prep(mine, own, got, mod, gain):
    n, d = own.shape
    return pl.pallas_call(
        prep_kernel,
        grid=(n // RB,),
        in_specs=[SMEM, row_block(d), row_block(d), mod_block(d), whole((1, d))],
        out_specs=[row_block(d), row_block(d)],
        out_shape=[shape((n, d), BF), shape((n, d), BF)],
        compiler_params=params(16),
    )(mine, own, got, mod, gain)


def attend_kernel(
    segb, x_ref, w_ref, cos_ref, sin_ref, segrow_ref,
    q_ref, k_ref, v_ref, att_ref, linv_ref, e_ref, vext, qm, kt,
):
    n = ROW_LEN
    lane = lax.broadcasted_iota(jnp.int32, (1, PAIR), 1)
    first = (lane % HD) < HD // 2
    low = (lane < HD).astype(F32)
    high = 1.0 - low
    cos = cos_ref[...]
    sin = sin_ref[...]

    def rotate(u):
        turned = jnp.where(
            first, -pltpu.roll(u, PAIR - HD // 2, 1), pltpu.roll(u, HD // 2, 1)
        )
        return u * cos + turned * sin

    proj = mm(x_ref[...], w_ref[...])
    queries = rotate(proj[:, :PAIR]) * (HD**-0.5)
    keys = rotate(proj[:, PAIR : 2 * PAIR]).astype(BF)
    values = proj[:, 2 * PAIR :]
    q_ref[...] = queries.astype(BF)
    k_ref[...] = keys
    v_ref[...] = values.astype(BF)
    kt[...] = keys.T
    vext[0:n, 0:PAIR] = (values * low).astype(BF)
    vext[n : 2 * n, 0:PAIR] = (values * high).astype(BF)
    vext[0:n, PAIR : 2 * PAIR] = jnp.broadcast_to(low.astype(BF), (n, PAIR))
    vext[n : 2 * n, PAIR : 2 * PAIR] = jnp.broadcast_to(high.astype(BF), (n, PAIR))
    qm[0] = (queries * low).astype(BF)
    qm[1] = (queries * high).astype(BF)
    segrow = segrow_ref[...]
    per = QB_FWD // BLOCK
    for i in range(n // QB_FWD):
        rows = pl.ds(i * QB_FWD, QB_FWD)
        for h in range(2):
            s = mm(qm[h, rows, :], kt[...])
            s = jnp.concatenate(
                [
                    s[b * BLOCK : (b + 1) * BLOCK]
                    + jnp.where(segrow == segb[i * per + b], 0.0, masked_score)
                    for b in range(per)
                ],
                axis=0,
            )
            peak = jnp.max(s, axis=1, keepdims=True)
            e_ref[rows, h * n : (h + 1) * n] = jnp.exp(s - peak).astype(BF)
        o = mm(e_ref[rows, :], vext[...])
        inverse = 1.0 / o[:, PAIR:]
        att_ref[rows, :] = (o[:, :PAIR] * inverse).astype(BF)
        linv_ref[rows, :] = inverse


def attend(segb, x, w, cos, sin, segrow):
    n, d = x.shape
    return pl.pallas_call(
        attend_kernel,
        in_specs=[SMEM] + [VMEM] * 5,
        out_specs=[VMEM] * 6,
        out_shape=[shape((n, PAIR), BF)] * 4
        + [shape((n, PAIR)), shape((n, 2 * n), BF)],
        scratch_shapes=[
            pltpu.VMEM((2 * n, 2 * PAIR), BF),
            pltpu.VMEM((2, n, PAIR), BF),
            pltpu.VMEM((PAIR, n), BF),
        ],
        compiler_params=params(32),
    )(segb, x, w, cos, sin, segrow)


def attend_back_kernel(
    q_ref, k_ref, v_ref, att_ref, linv_ref, do_ref, e_ref, cos_ref, sin_ref, out_ref,
    vx, km, ds, dq, dk, dv,
):
    n = ROW_LEN
    lane = lax.broadcasted_iota(jnp.int32, (1, PAIR), 1)
    first = (lane % HD) < HD // 2
    low = (lane < HD).astype(F32)
    masks = (low, 1.0 - low)
    vx[:, 0:PAIR] = v_ref[...]
    vx[:, PAIR:] = jnp.ones((n, PAIR), BF)
    keys = k_ref[...].astype(F32)
    for h in range(2):
        km[h * n : (h + 1) * n] = (keys * masks[h]).astype(BF)
    for i in range(n // QB_BWD):
        rows = pl.ds(i * QB_BWD, QB_BWD)
        dof = do_ref[rows, :].astype(F32) * linv_ref[rows, :]
        dd = dof * att_ref[rows, :].astype(F32)
        qf = q_ref[rows, :].astype(F32)
        for h in range(2):
            dm = (dof * masks[h]).astype(BF)
            left = jnp.concatenate([dm, (-dd * masks[h]).astype(BF)], axis=1)
            dp = mm(left, vx[...], NT)
            e = e_ref[rows, h * n : (h + 1) * n]
            sg = (dp * e.astype(F32)).astype(BF)
            ds[:, h * n : (h + 1) * n] = sg
            qm = (qf * masks[h]).astype(BF)
            a = mm(qm.T, sg)
            b = mm(dm.T, e)
            if i == 0 and h == 0:
                dk[...] = a
                dv[...] = b
            else:
                dk[...] += a
                dv[...] += b
        dq[rows, :] = mm(ds[...], km[...])
    cos = cos_ref[...]
    sin = sin_ref[...]

    def rotate_back(u):
        w = u * sin
        turned = jnp.where(
            first, pltpu.roll(w, PAIR - HD // 2, 1), -pltpu.roll(w, HD // 2, 1)
        )
        return u * cos + turned

    out_ref[:, 0:PAIR] = (rotate_back(dq[...]) * (HD**-0.5)).astype(BF)
    out_ref[:, PAIR : 2 * PAIR] = rotate_back(dk[...].T).astype(BF)
    out_ref[:, 2 * PAIR :] = dv[...].T.astype(BF)


def attend_back(saved, do, cos, sin):
    q, k, v, att, linv, e = saved
    n = q.shape[0]
    return pl.pallas_call(
        attend_back_kernel,
        in_specs=[VMEM] * 9,
        out_specs=VMEM,
        out_shape=shape((n, 3 * PAIR), BF),
        scratch_shapes=[
            pltpu.VMEM((n, 2 * PAIR), BF),
            pltpu.VMEM((2 * n, PAIR), BF),
            pltpu.VMEM((QB_BWD, 2 * n), BF),
            pltpu.VMEM((n, PAIR), F32),
            pltpu.VMEM((PAIR, n), F32),
            pltpu.VMEM((PAIR, n), F32),
        ],
        compiler_params=params(32),
    )(q, k, v, att, linv, do, e, cos, sin)


def project_kernel(att_ref, w_ref, out_ref):
    out_ref[...] = mm(att_ref[...], w_ref[...]).astype(BF)


def project(att, w):
    n = att.shape[0]
    inner, d = w.shape
    return pl.pallas_call(
        project_kernel,
        grid=(n // RB,),
        in_specs=[row_block(inner), whole((inner, d))],
        out_specs=row_block(d),
        out_shape=shape((n, d), BF),
        compiler_params=params(16),
    )(att, w)


def feed_kernel(
    mine, totals, tok_ref, own_ref, got_ref, cot_ref, cotgot_ref, mod_ref, gain_ref, up_ref,
    ub_ref, down_ref,
    middle_ref, fin_ref, act_ref, ug_ref, fg_ref, fo_ref, fng_ref, seed_ref, ubg_ref, dbg_ref,
):
    i = pl.program_id(0)
    per = ROW_LEN // RB
    mod = mod_ref[0]
    branch = own_ref[...].astype(F32) + got_ref[...].astype(F32)
    middle = tok_ref[...].astype(F32) + mod[2:3] * branch
    middle_ref[...] = middle
    xhat, _ = normalize(middle)
    fin = (xhat * (gain_ref[...] * (1.0 + mod[4:5])) + mod[3:4]).astype(BF)
    fin_ref[...] = fin
    live = live_rows(totals[i // per], (i % per) * RB, RB)
    cot = jnp.where(mine[0] == 1, cot_ref[...], cotgot_ref[...])
    seed = cot.astype(F32) * live
    seed_ref[...] = seed.astype(BF)
    fgf = mod[5:6] * seed
    fg = fgf.astype(BF)
    fg_ref[...] = fg
    u = mm(fin, up_ref[...]) + ub_ref[...]
    u2 = u * u
    t = jnp.tanh(u * (gelu_k + (gelu_k * gelu_c) * u2))
    half = 0.5 * (1.0 + t)
    act = (u * half).astype(BF)
    act_ref[...] = act
    slope = half + (0.5 * u) * (1.0 - t * t) * (gelu_k + (3.0 * gelu_k * gelu_c) * u2)
    ugf = mm(fg, down_ref[...], NT) * slope
    ug = ugf.astype(BF)
    ug_ref[...] = ug
    fo_ref[...] = mm(act, down_ref[...]).astype(BF)
    fng_ref[...] = mm(ug, up_ref[...], NT).astype(BF)
    ubs = jnp.sum(ugf, axis=0, keepdims=True)
    dbs = jnp.sum(fgf, axis=0, keepdims=True)

    @pl.when(i == 0)
    def _():
        ubg_ref[...] = ubs
        dbg_ref[...] = dbs

    @pl.when(i > 0)
    def _():
        ubg_ref[...] += ubs
        dbg_ref[...] += dbs


def feed(mine, totals, tok, own, got, cot, cotgot, mod, gain, up, ub, down):
    n, d = tok.shape
    f = up.shape[1]
    return pl.pallas_call(
        feed_kernel,
        grid=(n // RB,),
        in_specs=[SMEM, SMEM]
        + [row_block(d)] * 5
        + [mod_block(d), whole((1, d)), whole((d, f)), whole((1, f)), whole((f, d))],
        out_specs=[
            row_block(d), row_block(d), row_block(f), row_block(f), row_block(d),
            row_block(d), row_block(d), row_block(d), whole((1, f)), whole((1, d)),
        ],
        out_shape=[
            shape((n, d)), shape((n, d), BF), shape((n, f), BF), shape((n, f), BF),
            shape((n, d), BF), shape((n, d), BF), shape((n, d), BF), shape((n, d), BF),
            shape((1, f)), shape((1, d)),
        ],
        compiler_params=params(44),
    )(mine, totals, tok, own, got, cot, cotgot, mod, gain, up, ub, down)


def middle_kernel(
    middle_ref, own_ref, got_ref, seed_ref, bown_ref, bgot_ref, mod_ref, gain_ref, w_ref,
    mg_ref, bg_ref, do_ref, sums_ref,
):
    i = pl.program_id(0)
    mod = mod_ref[0]
    xhat, inverse = normalize(middle_ref[...])
    c = own_ref[...].astype(F32) + got_ref[...].astype(F32)
    mg = seed_ref[...].astype(F32) + norm_pull(
        c, xhat, inverse, gain_ref[...] * (1.0 + mod[4:5])
    )
    mg_ref[...] = mg
    bg = (mod[2:3] * mg).astype(BF)
    bg_ref[...] = bg
    do_ref[...] = mm(bg, w_ref[...], NT).astype(BF)
    branch = bown_ref[...].astype(F32) + bgot_ref[...].astype(F32)
    sums = jnp.concatenate(
        [
            jnp.sum(mg * branch, axis=0, keepdims=True),
            jnp.sum(c, axis=0, keepdims=True),
            jnp.sum(c * xhat, axis=0, keepdims=True),
        ],
        axis=0,
    )[None]

    @pl.when(i % (ROW_LEN // RB) == 0)
    def _():
        sums_ref[...] = sums

    @pl.when(i % (ROW_LEN // RB) > 0)
    def _():
        sums_ref[...] += sums


def middle_back(middle, own, got, seed, bown, bgot, mod, gain, w):
    n, d = middle.shape
    inner = w.shape[0]
    per = ROW_LEN // RB
    return pl.pallas_call(
        middle_kernel,
        grid=(n // RB,),
        in_specs=[row_block(d)] * 6 + [mod_block(d), whole((1, d)), whole((inner, d))],
        out_specs=[
            row_block(d), row_block(d), row_block(inner),
            pl.BlockSpec((1, 3, d), lambda i: (i // per, 0, 0)),
        ],
        out_shape=[
            shape((n, d)), shape((n, d), BF), shape((n, inner), BF),
            shape((n // ROW_LEN, 3, d)),
        ],
        compiler_params=params(24),
    )(middle, own, got, seed, bown, bgot, mod, gain, w)


def half_block(width, per_half):
    return pl.BlockSpec(
        (RB, width),
        lambda i, core: ((i // per_half) * 2 * per_half + core[0] * per_half + i % per_half, 0),
    )


def other_block(width, per_half):
    return pl.BlockSpec(
        (RB, width),
        lambda i, core: (
            (i // per_half) * 2 * per_half + (1 - core[0]) * per_half + i % per_half,
            0,
        ),
    )


def mix_kernel(core, middle_ref, own_ref, got_ref, seed_ref, mod_ref, bias_ref, out_ref, sums_ref):
    i = pl.program_id(0)
    fo = own_ref[...].astype(F32) + got_ref[...].astype(F32) + bias_ref[...]
    out_ref[...] = (middle_ref[...] + mod_ref[0][5:6] * fo).astype(BF)
    sums = jnp.sum(seed_ref[...].astype(F32) * fo, axis=0, keepdims=True)[None]

    @pl.when(i % (ROW_LEN // RB // 2) == 0)
    def _():
        sums_ref[...] = sums

    @pl.when(i % (ROW_LEN // RB // 2) > 0)
    def _():
        sums_ref[...] += sums


def mix(core, middle, own, got, seed, mod, bias):
    n, d = middle.shape
    ph = ROW_LEN // RB // 2
    half = half_block(d, ph)
    return pl.pallas_call(
        mix_kernel,
        grid_spec=pltpu.PrefetchScalarGridSpec(
            num_scalar_prefetch=1,
            grid=(n // RB // 2,),
            in_specs=[
                half, half, row_block(d), half,
                pl.BlockSpec((1, 6, d), lambda i, core: (i // ph, 0, 0)), whole((1, d)),
            ],
            out_specs=[
                row_block(d),
                pl.BlockSpec((1, 1, d), lambda i, core: (i // ph, 0, 0)),
            ],
        ),
        out_shape=[shape((n // 2, d), BF), shape((n // ROW_LEN, 1, d))],
        compiler_params=params(16),
    )(core, middle, own, got, seed, mod, bias)


def input_back_kernel(core, *refs):
    out_ref = refs[-1]
    pairs = (len(refs) - 1) // 2
    total = mm(refs[0][...], refs[pairs][...], NT)
    for p in range(1, pairs):
        total += mm(refs[p][...], refs[pairs + p][...], NT)
    out_ref[...] = total.astype(out_ref.dtype)


def input_back(core, grads, weights, block, kind):
    n, w3 = grads[0].shape
    d = weights[0].shape[0]
    ph = ROW_LEN // RB // 2
    return pl.pallas_call(
        input_back_kernel,
        grid_spec=pltpu.PrefetchScalarGridSpec(
            num_scalar_prefetch=1,
            grid=(n // RB // 2,),
            in_specs=[block(w3, ph)] * len(grads) + [whole((d, w3))] * len(weights),
            out_specs=row_block(d),
        ),
        out_shape=shape((n // 2, d), kind),
        compiler_params=params(24),
    )(core, *grads, *weights)


def final_kernel(core, tok_ref, own_ref, got_ref, mg_ref, mod_ref, gain_ref, out_ref, sums_ref):
    i = pl.program_id(0)
    mod = mod_ref[0]
    xhat, inverse = normalize(tok_ref[...].astype(F32))
    c = own_ref[...] + got_ref[...].astype(F32)
    out_ref[...] = mg_ref[...] + norm_pull(c, xhat, inverse, gain_ref[...] * (1.0 + mod[1:2]))
    sums = jnp.concatenate(
        [jnp.sum(c, axis=0, keepdims=True), jnp.sum(c * xhat, axis=0, keepdims=True)], axis=0
    )[None]

    @pl.when(i % (ROW_LEN // RB // 2) == 0)
    def _():
        sums_ref[...] = sums

    @pl.when(i % (ROW_LEN // RB // 2) > 0)
    def _():
        sums_ref[...] += sums


def final(core, tok, own, got, mg, mod, gain):
    n, d = tok.shape
    ph = ROW_LEN // RB // 2
    half = half_block(d, ph)
    return pl.pallas_call(
        final_kernel,
        grid_spec=pltpu.PrefetchScalarGridSpec(
            num_scalar_prefetch=1,
            grid=(n // RB // 2,),
            in_specs=[
                half, row_block(d), row_block(d), half,
                pl.BlockSpec((1, 6, d), lambda i, core: (i // ph, 0, 0)), whole((1, d)),
            ],
            out_specs=[
                row_block(d),
                pl.BlockSpec((1, 2, d), lambda i, core: (i // ph, 0, 0)),
            ],
        ),
        out_shape=[shape((n // 2, d)), shape((n // ROW_LEN, 2, d))],
        compiler_params=params(16),
    )(core, tok, own, got, mg, mod, gain)


def perm(dp_size, move):
    pairs = []
    for index in range(dp_size):
        for y in range(2):
            to = move(index >> 2, (index >> 1) & 1, y, index & 1)
            if to is not None:
                pairs.append((index * 2 + y, ((to[0] * 2 + to[1]) * 2 + to[3]) * 2 + to[2]))
    return pairs


def unxor(stack, me, bits):
    for b in range(bits):
        shaped = stack.reshape((-1, 2, 1 << b) + stack.shape[1:])
        flipped = jnp.concatenate([shaped[:, 1:], shaped[:, :1]], axis=1)
        stack = jnp.where(((me >> b) & 1) == 1, flipped, shaped).reshape(stack.shape)
    return stack


def per_device(
    tokens,
    conditioning,
    lengths,
    input_weight,
    output_weight,
    up_weight,
    up_bias,
    down_weight,
    down_bias,
    attention_gain,
    feed_gain,
    adaptive_weight,
    adaptive_bias,
    cotangent,
):
    n, d = tokens.shape
    rows = lengths.shape[0]
    inner = input_weight.shape[2]
    pairs = inner // PAIR
    dp_size = lax.axis_size("dp")
    planes = dp_size // 4
    zbits = planes.bit_length() - 1
    index = lax.axis_index("dp")
    y = lax.axis_index("tensor")
    c = index % 2
    x = (index // 2) % 2
    z = index // 4
    mine = (y == c)
    mine_s = mine.astype(jnp.int32).reshape(1)
    core_s = c.astype(jnp.int32).reshape(1)

    make = functools.partial(perm, dp_size)
    from_owner = make(lambda z, x, y, c: (z, x, y, 1 - c) if y == c else None)
    core_swap = make(lambda z, x, y, c: (z, x, y, 1 - c))
    turn = make(lambda z, x, y, c: (z, x, c, y))

    def send(value, how):
        return lax.ppermute(value, AXES, how)

    small = jnp.concatenate([lengths.astype(F32), conditioning.astype(F32)], axis=1)
    small = jnp.where(mine, small, send(small, from_owner))
    lens = small[:, :NSEG].astype(jnp.int32)
    cond = small[:, NSEG:]
    tok_got = send(tokens, from_owner)
    pair_w = []
    for p in range(pairs):
        cols = slice(p * PAIR, (p + 1) * PAIR)
        pair_w.append(
            send(jnp.concatenate([input_weight[j][:, cols] for j in range(3)], axis=1), turn)
        )
    out_w = send(output_weight, turn)
    up_w = send(up_weight, turn)
    up_b = send(up_bias.reshape(1, -1), turn).astype(F32)
    down_w = send(down_weight, turn)
    cot_got = send(cotangent, from_owner)

    ids = jnp.arange(NSEG, dtype=jnp.int32)
    upto = (ids[:, None] <= ids[None, :]).astype(jnp.int32)
    bounds = jnp.sum(lens[:, :, None] * upto[None], axis=1)
    slots = jnp.arange(ROW_LEN, dtype=jnp.int32)
    passed = (slots[None, :, None] >= bounds[:, None, :]).astype(jnp.int32)
    segment = jnp.sum(passed, axis=2)
    positions = slots[None] - jnp.sum(passed * lens[:, None, :], axis=2)
    segb = segment[:, ::BLOCK]
    totals = bounds[:, NSEG - 1]
    lanes = jnp.arange(PAIR, dtype=jnp.int32) % (HD // 2)
    frequency = rotary_base ** (-lanes.astype(F32) * (2.0 / HD))
    angles = positions.astype(F32)[:, :, None] * frequency[None, None, :]
    cosine = jnp.cos(angles)
    sine = jnp.sin(angles)
    modulation = jnp.dot(
        cond.astype(BF), adaptive_weight, preferred_element_type=F32
    ) + adaptive_bias.astype(F32)
    mod = modulation.reshape(rows, 6, d)
    gain_a = attention_gain.astype(F32).reshape(1, d)
    gain_f = feed_gain.astype(F32).reshape(1, d)

    tok, normed = prep(mine_s, tokens, tok_got, mod, gain_a)
    saved = [
        [
            attend(
                segb[r],
                normed[r * ROW_LEN : (r + 1) * ROW_LEN],
                pair_w[p],
                cosine[r],
                sine[r],
                segment[r][None],
            )
            for p in range(pairs)
        ]
        for r in range(rows)
    ]
    att = jnp.concatenate(
        [jnp.concatenate([s[3] for s in of_row], axis=1) for of_row in saved], axis=0
    )
    branch = project(att, out_w)
    branch_got = send(branch, core_swap)

    middle, fin, act, ug, fg, fo, fng, seed, ubg, dbg = feed(
        mine_s, totals, tok, branch, branch_got, cotangent, cot_got, mod, gain_f, up_w, up_b, down_w
    )
    fng_got = send(fng, core_swap)

    def other_half(value):
        blocks = value.reshape(rows, 2, ROW_LEN // 2, -1)
        return lax.dynamic_index_in_dim(blocks, 1 - c, 1, keepdims=False).reshape(n // 2, -1)

    fo_got = send(other_half(fo), core_swap)

    r_out = d // dp_size

    def scatter(grad):
        width = grad.shape[1]
        blocks = grad.reshape(planes, 2, 2, r_out, width)
        total = None
        for dx in range(2):
            for t in range(2):
                piece = lax.dynamic_index_in_dim(blocks, x ^ dx, 1, keepdims=False)
                piece = lax.dynamic_index_in_dim(piece, y ^ t, 1, keepdims=False)
                got = send(piece, make(lambda z, x, y, c: (z, x ^ dx, c, y ^ t))).astype(F32)
                total = got if total is None else total + got
        mine_part = lax.dynamic_index_in_dim(total, z, 0, keepdims=False)
        sent = total.astype(BF)
        for k in range(1, planes):
            piece = lax.dynamic_index_in_dim(sent, z ^ k, 0, keepdims=False)
            mine_part = mine_part + send(piece, make(lambda z, x, y, c: (z ^ k, x, y, c))).astype(
                F32
            )
        return mine_part

    down_t = mm(fg, act, TN).astype(BF)
    down_grad = scatter(down_t)
    up_g = mm(fin, ug, TN).astype(BF)
    up_grad = scatter(up_g)

    mg, bg, do, mid_sums = middle_back(
        middle, fng, fng_got, seed, branch, branch_got, mod, gain_f, out_w
    )
    mixed_half, gate_sums = mix(
        core_s, middle, fo, fo_got, seed, mod, down_bias.astype(F32).reshape(1, d)
    )
    mixed = send(mixed_half, turn)

    out_g = mm(bg, att, TN).astype(BF)
    out_grad = scatter(out_g)

    def everywhere(gathered, summed):
        width = gathered.shape[1]
        flat = jnp.concatenate([gathered.reshape(-1), summed.reshape(-1)]).reshape(-1, 128)
        flat = flat + send(flat, core_swap)
        count = gathered.size // 128

        def spread(value, moves, me, bits):
            stack = jnp.stack([value] + [send(value, make(move)) for move in moves])
            return unxor(stack, me, bits)

        moves = [
            (lambda z, x, y, c, k=k: (z, x ^ (k >> 1), y ^ (k & 1), c)) for k in range(1, 4)
        ]
        stack = spread(flat, moves, x * 2 + y, 2)
        flat = jnp.concatenate(
            [stack[:, :count].reshape(-1, 128), jnp.sum(stack[:, count:], axis=0)], axis=0
        )
        moves = [(lambda z, x, y, c, k=k: (z ^ k, x, y, c)) for k in range(1, planes)]
        stack = spread(flat, moves, z, zbits)
        return (
            stack[:, : 4 * count].reshape(-1, width),
            jnp.sum(stack[:, 4 * count :], axis=0).reshape(-1),
        )

    once = (c == 0).astype(F32)
    s_feed = mid_sums[:, 2]
    feed_gain_part = jnp.sum((1.0 + mod[:, 4]) * s_feed, axis=0)
    early = jnp.concatenate(
        [
            cond * once,
            mid_sums[:, 0] * once,
            mid_sums[:, 1] * once,
            s_feed * gain_f * once,
            gate_sums[:, 0],
        ],
        axis=1,
    )
    ub_full = jnp.concatenate(
        [ubg * once, ubg * (1.0 - once)], axis=1
    )
    early_sum = jnp.concatenate(
        [feed_gain_part * once, dbg.reshape(-1) * once, ub_full.reshape(-1)]
    )
    early_all, early_total = everywhere(early, early_sum)
    cond_dim = cond.shape[1]
    cond_all = early_all[:, :cond_dim]
    feed_gain_grad = early_total[:d]
    down_bias_grad = early_total[d : 2 * d]
    up_bias_grad = lax.dynamic_index_in_dim(
        early_total[2 * d :].reshape(2, -1), y, 0, keepdims=False
    )

    grads = []
    for p in range(pairs):
        cols = slice(p * PAIR, (p + 1) * PAIR)
        parts = [
            attend_back(
                saved[r][p], do[r * ROW_LEN : (r + 1) * ROW_LEN, cols], cosine[r], sine[r]
            )
            for r in range(rows)
        ]
        grads.append(parts[0] if rows == 1 else jnp.concatenate(parts, axis=0))
    in_grads = [scatter(mm(normed, g, TN).astype(BF)) for g in grads]
    ang_other = input_back(core_s, grads, pair_w, other_block, BF)
    ang_got = send(ang_other, core_swap)
    ang_own = input_back(core_s, grads, pair_w, half_block, F32)
    tok_grad_half, att_sums = final(core_s, tok, ang_own, ang_got, mg, mod, gain_a)
    tok_grad = jnp.where(
        mine, tok_grad_half, send(tok_grad_half.astype(BF), turn).astype(F32)
    )

    s_att = att_sums[:, 1]
    late = jnp.concatenate([att_sums[:, 0], s_att * gain_a], axis=1)
    late_sum = jnp.sum((1.0 + mod[:, 1]) * s_att, axis=0)
    late_all, attention_gain_grad = everywhere(late, late_sum)
    mod_all = jnp.concatenate([late_all, early_all[:, cond_dim:]], axis=1)
    adaptive_weight_grad = lax.dot_general(
        cond_all, mod_all, (TN, ((), ())),
        precision=lax.Precision.HIGHEST, preferred_element_type=F32,
    )
    adaptive_bias_grad = jnp.sum(mod_all, axis=0)

    in_stack = jnp.concatenate(
        [g.reshape(r_out, 3, PAIR).transpose(1, 0, 2) for g in in_grads], axis=2
    )
    return (
        mixed,
        tok_grad,
        in_stack,
        out_grad.T,
        up_grad,
        up_bias_grad,
        down_grad.T,
        down_bias_grad,
        attention_gain_grad,
        feed_gain_grad,
        adaptive_weight_grad,
        adaptive_bias_grad,
    )


def solution(mesh):
    placed = (
        P("dp", None),
        P("dp", None),
        P("dp", None),
        P(None, None, "tensor"),
        P("tensor", None),
        P(None, "tensor"),
        P("tensor"),
        P("tensor", None),
        P(),
        P(),
        P(),
        P(),
        P(),
        P("dp", None),
    )
    return jax.shard_map(
        per_device,
        mesh=mesh,
        in_specs=placed,
        out_specs=(
            P(("dp", "tensor"), None),
            P(("dp", "tensor"), None),
            P(None, "dp", "tensor"),
            P("tensor", "dp"),
            P("dp", "tensor"),
            P("tensor"),
            P("tensor", "dp"),
            P(),
            P(),
            P(),
            P(),
            P(),
        ),
        check_vma=False,
    )
```

```python
import functools

import jax
import jax.numpy as jnp
from jax import lax
from jax.experimental import pallas as pl
from jax.experimental.pallas import tpu as pltpu
from jax.sharding import PartitionSpec as P

HD = 64
ROW_LEN = 1024
NSEG = 8
BLOCK = 128
PAIR = 2 * HD
RB = 256
HALF = ROW_LEN // 2
STEPS = HALF // RB

norm_eps = 1e-05
masked_score = -1000000000.0
rotary_base = 10000.0
gelu_k = 0.7978845608028654
gelu_c = 0.044715

AXES = ("dp", "tensor")
BF = jnp.bfloat16
F32 = jnp.float32
NN = ((1,), (0,))
NT = ((1,), (1,))
TN = ((0,), (0,))
VMEM = pl.BlockSpec(memory_space=pltpu.VMEM)
SMEM = pl.BlockSpec(memory_space=pltpu.SMEM)
ANY = pl.BlockSpec(memory_space=pltpu.HBM)


def mm(left, right, dims=NN):
    return lax.dot_general(left, right, (dims, ((), ())), preferred_element_type=F32)


def params(mib):
    return pltpu.CompilerParams(vmem_limit_bytes=mib << 20)


def cost(us):
    return pl.CostEstimate(flops=int(us * 1.15e9), bytes_accessed=0, transcendentals=0)


def shape(dims, kind=F32):
    return jax.ShapeDtypeStruct(dims, kind)


def hbm(*values):
    return [pltpu.with_memory_space_constraint(v, pltpu.HBM) for v in values]


def normalize(values):
    centered = values - jnp.mean(values, axis=-1, keepdims=True)
    inverse = lax.rsqrt(jnp.mean(centered * centered, axis=-1, keepdims=True) + norm_eps)
    return centered * inverse, inverse


def norm_pull(cotangent, xhat, inverse, weight):
    e = cotangent * weight
    return inverse * (
        e
        - jnp.mean(e, axis=-1, keepdims=True)
        - xhat * jnp.mean(e * xhat, axis=-1, keepdims=True)
    )


def live_rows(total, first_row, rows):
    slots = lax.broadcasted_iota(jnp.int32, (rows, 1), 0) + first_row
    return (slots < total).astype(F32)


def rows_of(width, offset=0):
    return pl.BlockSpec((RB, width), lambda i, *_: (i + offset, 0))


def whole(*dims):
    return pl.BlockSpec(dims, lambda *_: (0,) * len(dims), pipeline_mode=pl.Buffered(1))


def constant(*dims):
    return pl.BlockSpec(dims, lambda *_: (0,) * len(dims))


def head_masks():
    lane = lax.broadcasted_iota(jnp.int32, (1, PAIR), 1)
    low = (lane < HD).astype(F32)
    return (lane % HD) < HD // 2, (low, 1.0 - low)


def project_kernel(
    tok_ref, mod_ref, gain_ref, w_ref, cos_ref, sin_ref,
    normed_ref, q_ref, k_ref, v_ref, kt_ref, vext_ref,
):
    n = ROW_LEN

    @pl.when(pl.program_id(0) == 0)
    def _():
        mod = mod_ref[...]
        for i in range(n // RB):
            rows = slice(i * RB, (i + 1) * RB)
            xhat, _ = normalize(tok_ref[rows, :].astype(F32))
            normed_ref[rows, :] = (
                xhat * (gain_ref[...] * (1.0 + mod[1:2])) + mod[0:1]
            ).astype(BF)

    first, masks = head_masks()
    cos = cos_ref[...]
    sin = sin_ref[...]

    def rotate(u):
        turned = jnp.where(
            first, -pltpu.roll(u, PAIR - HD // 2, 1), pltpu.roll(u, HD // 2, 1)
        )
        return u * cos + turned * sin

    w = jnp.concatenate([w_ref[0], w_ref[1], w_ref[2]], axis=1)
    proj = mm(normed_ref[...], w)
    q_ref[...] = (rotate(proj[:, :PAIR]) * (HD**-0.5)).astype(BF)
    keys = rotate(proj[:, PAIR : 2 * PAIR]).astype(BF)
    values = proj[:, 2 * PAIR :]
    k_ref[...] = keys
    v_ref[...] = values.astype(BF)
    kt_ref[0] = keys.T
    for h in range(2):
        vext_ref[0, h * n : (h + 1) * n, 0:PAIR] = (values * masks[h]).astype(BF)
        vext_ref[0, h * n : (h + 1) * n, PAIR : 2 * PAIR] = jnp.broadcast_to(
            masks[h].astype(BF), (n, PAIR)
        )


def project(tok, mod, gain, w, cos, sin):
    n, d = tok.shape
    inner = w.shape[2]
    pairs = inner // PAIR
    of_pair = pl.BlockSpec((n, PAIR), lambda p: (0, p))
    return pl.pallas_call(
        project_kernel,
        grid=(pairs,),
        in_specs=[
            whole(n, d), whole(6, d), whole(1, d), pl.BlockSpec((3, d, PAIR), lambda p: (0, 0, p)),
            whole(n, PAIR), whole(n, PAIR),
        ],
        out_specs=[
            constant(n, d), of_pair, of_pair, of_pair,
            pl.BlockSpec((1, PAIR, n), lambda p: (p, 0, 0)),
            pl.BlockSpec((1, 2 * n, 2 * PAIR), lambda p: (p, 0, 0)),
        ],
        out_shape=[pltpu.HBM((n, d), BF)]
        + [pltpu.HBM((n, inner), BF)] * 3
        + [shape((pairs, PAIR, n), BF), shape((pairs, 2 * n, 2 * PAIR), BF)],
        compiler_params=params(24),
        cost_estimate=cost(5),
    )(*hbm(tok), mod, gain, *hbm(w), cos, sin)


def attend_kernel(
    segb, q_ref, kt_ref, vext_ref, segrow_ref, w_ref, att_ref, linv_ref, e_ref, out_ref, *, first_row
):
    n = ROW_LEN
    step = pl.program_id(0)
    pairs = kt_ref.shape[0]
    _, masks = head_masks()
    segrow = segrow_ref[...]
    per = RB // BLOCK
    biases = [
        jnp.where(segrow == segb[0, first_row // BLOCK + step * per + b], 0.0, masked_score)
        for b in range(per)
    ]
    for p in range(pairs):
        cols = slice(p * PAIR, (p + 1) * PAIR)
        q = q_ref[:, cols].astype(F32)
        for h in range(2):
            s = mm((q * masks[h]).astype(BF), kt_ref[p])
            s = jnp.concatenate(
                [s[b * BLOCK : (b + 1) * BLOCK] + biases[b] for b in range(per)], axis=0
            )
            peak = jnp.max(s, axis=1, keepdims=True)
            e_ref[p, :, h * n : (h + 1) * n] = jnp.exp(s - peak).astype(BF)
        o = mm(e_ref[p], vext_ref[p])
        inverse = 1.0 / o[:, PAIR:]
        att_ref[:, cols] = (o[:, :PAIR] * inverse).astype(BF)
        linv_ref[:, cols] = inverse
    out_ref[...] = mm(att_ref[...], w_ref[...]).astype(BF)


def attend(half, segb, q, kt, vext, segrow, w):
    n, inner = q.shape
    d = w.shape[1]
    pairs = inner // PAIR
    return pl.pallas_call(
        functools.partial(attend_kernel, first_row=half * HALF),
        grid=(STEPS,),
        in_specs=[
            SMEM, rows_of(inner, half * STEPS), whole(pairs, PAIR, n), whole(pairs, 2 * n, 2 * PAIR),
            whole(1, n), whole(inner, d),
        ],
        out_specs=[
            rows_of(inner), rows_of(inner), pl.BlockSpec((pairs, RB, 2 * n), lambda i: (0, i, 0)),
            rows_of(d),
        ],
        out_shape=[
            pltpu.HBM((HALF, inner), BF), pltpu.HBM((HALF, inner), F32),
            pltpu.HBM((pairs, HALF, 2 * n), BF), shape((HALF, d), BF),
        ],
        compiler_params=params(28),
        cost_estimate=cost(8),
    )(segb, *hbm(q), kt, vext, segrow, w)


def attend_back_kernel(q_ref, k_ref, v_ref, att_ref, linv_ref, do_ref, e_ref, cos_ref, sin_ref, *refs, last):
    n = ROW_LEN
    if last:
        dk0_ref, dv0_ref, dq_ref, dkout_ref, dvout_ref, vx, km, ds, dk, dv = refs
    else:
        dq_ref, dkout_ref, dvout_ref, vx, km, ds, dk, dv = refs
    step = pl.program_id(1)
    first, masks = head_masks()

    @pl.when(step == 0)
    def _():
        vx[:, 0:PAIR] = v_ref[...]
        vx[:, PAIR:] = jnp.ones((n, PAIR), BF)
        keys = k_ref[...].astype(F32)
        for h in range(2):
            km[h * n : (h + 1) * n] = (keys * masks[h]).astype(BF)
        if last:
            dk[...] = dk0_ref[0]
            dv[...] = dv0_ref[0]
        else:
            dk[...] = jnp.zeros_like(dk)
            dv[...] = jnp.zeros_like(dv)

    def rotate_back(u, rows):
        w = u * sin_ref[rows, :]
        turned = jnp.where(
            first, pltpu.roll(w, PAIR - HD // 2, 1), -pltpu.roll(w, HD // 2, 1)
        )
        return u * cos_ref[rows, :] + turned

    dof = do_ref[...].astype(F32) * linv_ref[...]
    dd = dof * att_ref[...].astype(F32)
    qf = q_ref[...].astype(F32)
    for h in range(2):
        dm = (dof * masks[h]).astype(BF)
        left = jnp.concatenate([dm, (-dd * masks[h]).astype(BF)], axis=1)
        dp = mm(left, vx[...], NT)
        e = e_ref[0, :, h * n : (h + 1) * n]
        sg = (dp * e.astype(F32)).astype(BF)
        ds[:, h * n : (h + 1) * n] = sg
        qm = (qf * masks[h]).astype(BF)
        dk[...] += mm(qm.T, sg)
        dv[...] += mm(dm.T, e)
    start = (HALF if last else 0) + step * RB
    rows = pl.ds(pl.multiple_of(start, RB), RB)
    dq_ref[...] = (rotate_back(mm(ds[...], km[...]), rows) * (HD**-0.5)).astype(BF)

    @pl.when(step == STEPS - 1)
    def _():
        if last:
            dkout_ref[...] = rotate_back(dk[...].T, slice(None)).astype(BF)
            dvout_ref[...] = dv[...].T.astype(BF)
        else:
            dkout_ref[0] = dk[...]
            dvout_ref[0] = dv[...]


def attend_back(half, q, k, v, att, linv, e, do, cos, sin, before=()):
    n, inner = q.shape
    pairs = inner // PAIR
    part = pl.BlockSpec((RB, PAIR), lambda p, i: (i, p))
    of_pair = pl.BlockSpec((n, PAIR), lambda p, i: (0, p))
    sums = pl.BlockSpec((1, PAIR, n), lambda p, i: (p, 0, 0))
    last = half == 1
    return pl.pallas_call(
        functools.partial(attend_back_kernel, last=last),
        grid=(pairs, STEPS),
        in_specs=[
            pl.BlockSpec((RB, PAIR), lambda p, i: (half * STEPS + i, p)), of_pair, of_pair,
            part, part, part, pl.BlockSpec((1, RB, 2 * n), lambda p, i: (p, i, 0)),
            whole(n, PAIR), whole(n, PAIR),
        ]
        + [sums] * len(before),
        out_specs=[part] + ([of_pair] * 2 if last else [sums] * 2),
        out_shape=[shape((HALF, inner), BF)]
        + ([shape((n, inner), BF)] * 2 if last else [shape((pairs, PAIR, n))] * 2),
        scratch_shapes=[
            pltpu.VMEM((n, 2 * PAIR), BF),
            pltpu.VMEM((2 * n, PAIR), BF),
            pltpu.VMEM((RB, 2 * n), BF),
            pltpu.VMEM((PAIR, n), F32),
            pltpu.VMEM((PAIR, n), F32),
        ],
        compiler_params=params(28),
        cost_estimate=cost(30),
    )(*hbm(q, k, v, att, linv), do, *hbm(e), cos, sin, *before)


def feed_kernel(
    total, tok_ref, own_ref, got_ref, cot_ref, mod_ref, gain_ref, ub_ref, up_ref, down_ref,
    middle_ref, fin_ref, act_ref, ug_ref, fg_ref, fo_ref, fng_ref, ubg_ref, dbg_ref, *, first_row,
):
    i = pl.program_id(0)
    mod = mod_ref[...]
    branch = own_ref[...].astype(F32) + got_ref[...].astype(F32)
    middle = tok_ref[...].astype(F32) + mod[2:3] * branch
    middle_ref[...] = middle
    xhat, _ = normalize(middle)
    fin = (xhat * (gain_ref[...] * (1.0 + mod[4:5])) + mod[3:4]).astype(BF)
    fin_ref[...] = fin
    seed = cot_ref[...].astype(F32) * live_rows(total[0], first_row + i * RB, RB)
    fgf = mod[5:6] * seed
    fg = fgf.astype(BF)
    fg_ref[...] = fg
    u = mm(fin, up_ref[...]) + ub_ref[...]
    u2 = u * u
    t = jnp.tanh(u * (gelu_k + (gelu_k * gelu_c) * u2))
    half = 0.5 * (1.0 + t)
    act = (u * half).astype(BF)
    act_ref[...] = act
    slope = half + (0.5 * u) * (1.0 - t * t) * (gelu_k + (3.0 * gelu_k * gelu_c) * u2)
    ugf = mm(fg, down_ref[...], NT) * slope
    ug = ugf.astype(BF)
    ug_ref[...] = ug
    fng_ref[...] = mm(ug, up_ref[...], NT).astype(BF)
    fo_ref[...] = mm(act, down_ref[...]).astype(BF)
    ubs = jnp.sum(ugf, axis=0, keepdims=True)
    dbs = jnp.sum(fgf, axis=0, keepdims=True)

    @pl.when(i == 0)
    def _():
        ubg_ref[...] = ubs
        dbg_ref[...] = dbs

    @pl.when(i > 0)
    def _():
        ubg_ref[...] += ubs
        dbg_ref[...] += dbs


def feed(half, total, tok, own, got, cot, mod, gain, ub, up, down):
    d, f = up.shape
    here = rows_of(d, half * STEPS)
    return pl.pallas_call(
        functools.partial(feed_kernel, first_row=half * HALF),
        grid=(STEPS,),
        in_specs=[
            SMEM, here, rows_of(d), rows_of(d), here, whole(6, d), whole(1, d), whole(1, f),
            whole(d, f), whole(f, d),
        ],
        out_specs=[
            rows_of(d), rows_of(d), rows_of(f), rows_of(f), rows_of(d), rows_of(d), rows_of(d),
            constant(1, f), constant(1, d),
        ],
        out_shape=[
            shape((HALF, d)), shape((HALF, d), BF), shape((HALF, f), BF), shape((HALF, f), BF),
            shape((HALF, d), BF), shape((HALF, d), BF), shape((HALF, d), BF),
            shape((1, f)), shape((1, d)),
        ],
        compiler_params=params(36),
        cost_estimate=cost(9),
    )(total, *hbm(tok), own, got, *hbm(cot), mod, gain, ub, up, down)


def middle_kernel(
    total, middle_ref, own_ref, got_ref, cot_ref, bown_ref, bgot_ref, mod_ref, gain_ref, w_ref,
    mg_ref, bg_ref, do_ref, sums_ref, *, first_row,
):
    i = pl.program_id(0)
    mod = mod_ref[...]
    xhat, inverse = normalize(middle_ref[...])
    c = own_ref[...].astype(F32) + got_ref[...].astype(F32)
    seed = cot_ref[...].astype(F32) * live_rows(total[0], first_row + i * RB, RB)
    mg = seed + norm_pull(c, xhat, inverse, gain_ref[...] * (1.0 + mod[4:5]))
    mg_ref[...] = mg
    bg = (mod[2:3] * mg).astype(BF)
    bg_ref[...] = bg
    do_ref[...] = mm(bg, w_ref[...], NT).astype(BF)
    branch = bown_ref[...].astype(F32) + bgot_ref[...].astype(F32)
    sums = jnp.concatenate(
        [
            jnp.sum(mg * branch, axis=0, keepdims=True),
            jnp.sum(c, axis=0, keepdims=True),
            jnp.sum(c * xhat, axis=0, keepdims=True),
        ],
        axis=0,
    )

    @pl.when(i == 0)
    def _():
        sums_ref[...] = sums

    @pl.when(i > 0)
    def _():
        sums_ref[...] += sums


def middle_back(half, total, middle, own, got, cot, bown, bgot, mod, gain, w):
    inner, d = w.shape
    return pl.pallas_call(
        functools.partial(middle_kernel, first_row=half * HALF),
        grid=(STEPS,),
        in_specs=[
            SMEM, rows_of(d), rows_of(d), rows_of(d), rows_of(d, half * STEPS), rows_of(d),
            rows_of(d), whole(6, d), whole(1, d), whole(inner, d),
        ],
        out_specs=[rows_of(d), rows_of(d), rows_of(inner), constant(3, d)],
        out_shape=[
            pltpu.HBM((HALF, d), F32), shape((HALF, d), BF), shape((HALF, inner), BF), shape((3, d)),
        ],
        compiler_params=params(24),
        cost_estimate=cost(8),
    )(total, middle, own, got, *hbm(cot), bown, bgot, mod, gain, w)


def weight_grad_kernel(starts, *refs, plan, outs, blocks):
    ins, rest = refs[: plan["ins"]], refs[plan["ins"] :]
    out = rest[:outs]
    lt, g = rest[outs:]
    j = pl.program_id(0)
    begin = 0
    for lefts, rights in plan["couples"]:

        @pl.when(j == begin)
        def _(lefts=lefts):
            row = 0
            for i in lefts:
                size = ins[i].shape[0]
                lt[:, row : row + size] = ins[i][...].T
                row += size

        for parts, chunks in rights:

            @pl.when((j >= begin) & (j < begin + chunks))
            def _(parts=parts):
                total, row = None, 0
                for i in parts:
                    size = ins[i].shape[0]
                    term = mm(lt[:, row : row + size], ins[i][...])
                    total = term if total is None else total + term
                    row += size
                g[...] = total

            begin += chunks
    size = out[0].shape[1]
    for k in range(outs):
        for m in range(blocks):
            rows = pl.ds(pl.multiple_of(starts[k * blocks + m], 16), size)
            out[k][m] = g[rows, :].astype(BF)


def weight_grad(couples, starts, outs, blocks, size, chunk=384):
    ins, specs, plan, begin = [], [], [], 0
    for lefts, rights in couples:
        left_ids = []
        for part in lefts:
            left_ids.append(len(ins))
            ins.append(part)
            specs.append(whole(*part.shape))
        right_ids = []
        for parts in rights:
            chunks = parts[0].shape[1] // chunk
            ids = []
            for part in parts:
                ids.append(len(ins))
                ins.append(part)
                specs.append(
                    pl.BlockSpec(
                        (part.shape[0], chunk),
                        lambda j, b=begin, w=chunks: (0, jnp.clip(j - b, 0, w - 1)),
                    )
                )
            right_ids.append((ids, chunks))
            begin += chunks
        plan.append((left_ids, right_ids))
    d = couples[0][0][0].shape[1]
    n = sum(part.shape[0] for part in couples[0][0])
    return pl.pallas_call(
        functools.partial(
            weight_grad_kernel, plan={"ins": len(ins), "couples": plan}, outs=outs, blocks=blocks
        ),
        grid=(begin,),
        in_specs=[SMEM] + specs,
        out_specs=[pl.BlockSpec((blocks, size, chunk), lambda j: (0, 0, j))] * outs,
        out_shape=[shape((blocks, size, begin * chunk), BF)] * outs,
        scratch_shapes=[pltpu.VMEM((d, n), BF), pltpu.VMEM((d, chunk), F32)],
        compiler_params=params(24),
        cost_estimate=cost(2 * begin),
    )(starts, *ins)


def mix_kernel(side, m0_ref, m1_ref, f0_ref, f1_ref, got_ref, cot_ref, mod_ref, bias_ref, total, out_ref, sums_ref):
    i = pl.program_id(0)
    second = side[0] == 1
    own = jnp.where(second, f1_ref[...], f0_ref[...])
    fo = own.astype(F32) + got_ref[...].astype(F32) + bias_ref[...]
    middle = jnp.where(second, m1_ref[...], m0_ref[...])
    out_ref[...] = (middle + mod_ref[5:6] * fo).astype(BF)
    seed = cot_ref[...].astype(F32) * live_rows(total[0], side[0] * HALF + i * RB, RB)
    sums = jnp.sum(seed * fo, axis=0, keepdims=True)

    @pl.when(i == 0)
    def _():
        sums_ref[...] = sums

    @pl.when(i > 0)
    def _():
        sums_ref[...] += sums


def here_rows(width):
    return pl.BlockSpec((RB, width), lambda i, side: (side[0] * STEPS + i, 0))


def there_rows(width):
    return pl.BlockSpec((RB, width), lambda i, side: ((1 - side[0]) * STEPS + i, 0))


def mix(side, total, middles, outs, got, cot, mod, bias):
    d = got.shape[1]
    return pl.pallas_call(
        mix_kernel,
        grid_spec=pltpu.PrefetchScalarGridSpec(
            num_scalar_prefetch=1,
            grid=(STEPS,),
            in_specs=[rows_of(d)] * 5 + [here_rows(d), whole(6, d), whole(1, d), SMEM],
            out_specs=[rows_of(d), constant(1, d)],
        ),
        out_shape=[shape((HALF, d), BF), shape((1, d))],
        compiler_params=params(24),
        cost_estimate=cost(1),
    )(side, *middles, *outs, got, *hbm(cot), mod, bias, total)


def input_back_kernel(side, q0_ref, q1_ref, k_ref, v_ref, w_ref, out_ref, *, mine):
    second = (side[0] == 1) if mine else (side[0] == 0)
    dq = jnp.where(second, q1_ref[...], q0_ref[...])
    total = mm(dq, w_ref[0], NT)
    total += mm(k_ref[...], w_ref[1], NT)
    total += mm(v_ref[...], w_ref[2], NT)
    out_ref[...] = total.astype(out_ref.dtype)


def input_back(side, dqs, dk, dv, w, mine, kind):
    _, d, inner = w.shape
    block = here_rows if mine else there_rows
    return pl.pallas_call(
        functools.partial(input_back_kernel, mine=mine),
        grid_spec=pltpu.PrefetchScalarGridSpec(
            num_scalar_prefetch=1,
            grid=(STEPS,),
            in_specs=[rows_of(inner), rows_of(inner), block(inner), block(inner), whole(3, d, inner)],
            out_specs=rows_of(d),
        ),
        out_shape=shape((HALF, d), kind),
        compiler_params=params(24),
        cost_estimate=cost(2),
    )(side, *dqs, dk, dv, w)


def final_kernel(side, tok_ref, own_ref, got_ref, mg0_ref, mg1_ref, mod_ref, gain_ref, out_ref, sums_ref):
    i = pl.program_id(0)
    xhat, inverse = normalize(tok_ref[...].astype(F32))
    c = own_ref[...] + got_ref[...].astype(F32)
    mg = jnp.where(side[0] == 1, mg1_ref[...], mg0_ref[...])
    out_ref[...] = mg + norm_pull(c, xhat, inverse, gain_ref[...] * (1.0 + mod_ref[1:2]))
    sums = jnp.concatenate(
        [jnp.sum(c, axis=0, keepdims=True), jnp.sum(c * xhat, axis=0, keepdims=True)], axis=0
    )

    @pl.when(i == 0)
    def _():
        sums_ref[...] = sums

    @pl.when(i > 0)
    def _():
        sums_ref[...] += sums


def final(side, tok, own, got, mgs, mod, gain):
    d = tok.shape[1]
    return pl.pallas_call(
        final_kernel,
        grid_spec=pltpu.PrefetchScalarGridSpec(
            num_scalar_prefetch=1,
            grid=(STEPS,),
            in_specs=[here_rows(d)] + [rows_of(d)] * 4 + [whole(6, d), whole(1, d)],
            out_specs=[rows_of(d), constant(2, d)],
        ),
        out_shape=[shape((HALF, d)), shape((2, d))],
        compiler_params=params(24),
        cost_estimate=cost(1),
    )(side, *hbm(tok), own, got, *hbm(*mgs), mod, gain)


def collect_kernel(
    half_ref, got_ref, mid0_ref, mid1_ref, mod_ref, ga_ref, gf_ref, cond_ref, d0_ref, d1_ref,
    u0_ref, u1_ref, out_ref,
):
    half = half_ref[...] + got_ref[...]
    mid = mid0_ref[...] + mid1_ref[...]
    d = half.shape[1]
    s_att, s_feed = half[1:2], mid[2:3]
    out_ref[...] = jnp.zeros_like(out_ref)
    out_ref[0:1, : cond_ref.shape[1]] = cond_ref[...]
    rows = (
        half[0:1], s_att * ga_ref[...], mid[0:1], mid[1:2], s_feed * gf_ref[...], half[2:3],
        (1.0 + mod_ref[1:2]) * s_att, (1.0 + mod_ref[4:5]) * s_feed, d0_ref[...] + d1_ref[...],
    )
    for i, row in enumerate(rows):
        out_ref[i + 1 : i + 2, :] = row
    for i in range(u0_ref.shape[1] // d):
        cols = slice(i * d, (i + 1) * d)
        out_ref[10 + i : 11 + i, :] = u0_ref[:, cols] + u1_ref[:, cols]


def collect(half, got, mids, mod, ga, gf, cond, d0, d1, u0, u1):
    d = half.shape[1]
    rows = 10 + u0.shape[1] // d
    return pl.pallas_call(
        collect_kernel,
        in_specs=[VMEM] * 12,
        out_specs=VMEM,
        out_shape=shape((-(-rows // 8) * 8, d)),
        compiler_params=params(4),
        cost_estimate=cost(1),
    )(half, got, *mids, mod, ga, gf, cond, d0, d1, u0, u1)


def together(*values):
    return lax.optimization_barrier(values)


def perm(dp_size, move):
    pairs = []
    for index in range(dp_size):
        for y in range(2):
            to = move(index >> 2, (index >> 1) & 1, y, index & 1)
            pairs.append((index * 2 + y, ((to[0] * 2 + to[1]) * 2 + to[3]) * 2 + to[2]))
    return pairs


def xor_order(stack, me, bits):
    for b in range(bits):
        shaped = stack.reshape((-1, 2, 1 << b) + stack.shape[1:])
        flipped = jnp.concatenate([shaped[:, 1:], shaped[:, :1]], axis=1)
        stack = jnp.where(((me >> b) & 1) == 1, flipped, shaped).reshape(stack.shape)
    return stack


def per_device(
    tokens,
    conditioning,
    lengths,
    input_weight,
    output_weight,
    up_weight,
    up_bias,
    down_weight,
    down_bias,
    attention_gain,
    feed_gain,
    adaptive_weight,
    adaptive_bias,
    cotangent,
):
    n, d = tokens.shape
    assert lengths.shape[0] == 1
    inner = input_weight.shape[2]
    f = up_weight.shape[1]
    dp_size = lax.axis_size("dp")
    planes = dp_size // 4
    zbits = planes.bit_length() - 1
    index = lax.axis_index("dp")
    y = lax.axis_index("tensor")
    c = index % 2
    x = (index // 2) % 2
    z = index // 4
    side = y.astype(jnp.int32).reshape(1)

    make = functools.partial(perm, dp_size)
    y_swap = make(lambda z, x, y, c: (z, x, 1 - y, c))
    core_swap = make(lambda z, x, y, c: (z, x, y, 1 - c))
    x_swap = make(lambda z, x, y, c: (z, 1 - x, y, c))

    def send(value, how):
        return lax.ppermute(value, AXES, how)

    ids = jnp.arange(NSEG, dtype=jnp.int32)
    upto = (ids[:, None] <= ids[None, :]).astype(jnp.int32)
    bounds = jnp.sum(lengths[:, :, None] * upto[None], axis=1)
    slots = jnp.arange(ROW_LEN, dtype=jnp.int32)
    passed = (slots[None, :, None] >= bounds[:, None, :]).astype(jnp.int32)
    segment = jnp.sum(passed, axis=2)
    positions = slots[None] - jnp.sum(passed * lengths[:, None, :], axis=2)
    segb = segment[:, ::BLOCK]
    total = bounds[:, NSEG - 1]
    lanes = jnp.arange(PAIR, dtype=jnp.int32) % (HD // 2)
    frequency = rotary_base ** (-lanes.astype(F32) * (2.0 / HD))
    angles = positions[0].astype(F32)[:, None] * frequency[None, :]
    cosine = jnp.cos(angles)
    sine = jnp.sin(angles)
    modulation = jnp.dot(
        conditioning, adaptive_weight, preferred_element_type=F32
    ) + adaptive_bias.astype(F32)
    mod = modulation.reshape(6, d)
    gain_a = attention_gain.astype(F32).reshape(1, d)
    gain_f = feed_gain.astype(F32).reshape(1, d)
    up_b = up_bias.astype(F32).reshape(1, f)

    normed, q, k, v, kt, vext = project(tokens, mod, gain_a, input_weight, cosine, sine)
    halves = (0, 1)
    att, linv, e, branch, branch_got = [], [], [], [], []
    for h in halves:
        got = attend(h, segb, q, kt, vext, segment, output_weight)
        for store, value in zip((att, linv, e, branch), got):
            store.append(value)
        branch_got.append(send(branch[h], y_swap))
    fed, fng_got = [], []
    for h in halves:
        fed.append(
            feed(
                h, total, tokens, branch[h], branch_got[h], cotangent, mod, gain_f, up_b,
                up_weight, down_weight,
            )
        )
        fng_got.append(send(fed[h][6], y_swap))
    middle, fin, act, ug, fg, fo, fng, ubg, dbg = zip(*fed)
    r_out = d // dp_size

    def cut(couples):
        if r_out % 16 == 0:
            place = [
                (((z ^ m) * 2 + (x ^ dx)) * 2 + (c ^ s)) * r_out
                for s in range(2)
                for dx in range(2)
                for m in range(planes)
            ]
            starts = jnp.stack([p.astype(jnp.int32) for p in place])
            outs = weight_grad(couples, starts, 2, 2 * planes, r_out)
        else:
            grad = jnp.concatenate(
                [
                    mm(jnp.concatenate(a), jnp.concatenate(b), TN).astype(BF)
                    for a, bs in couples
                    for b in bs
                ],
                axis=1,
            )
            blocks = grad.reshape(planes, 2, 2, r_out, grad.shape[1])
            blocks = xor_order(blocks, z, zbits).transpose(2, 1, 0, 3, 4)
            blocks = xor_order(blocks, c, 1)
            outs = [xor_order(b, x, 1) for b in blocks]
        return [o.reshape(2, planes, r_out, -1) for o in outs]

    def over_z(near, got):
        total = near + got.astype(F32)
        result = total[0]
        for m in range(1, planes):
            came = send(total[m].astype(BF), make(lambda z, x, y, c: (z ^ m, x, y, c)))
            result = result + came.astype(F32)
        return result

    feed_own, feed_far = cut([(fg, [act]), (fin, [ug])])
    feed_core_got = send(feed_far, core_swap)
    fng_got[0], feed_own = together(fng_got[0], feed_own)

    mids, backs = [], []
    for h in halves:
        mids.append(
            middle_back(
                h, total, middle[h], fng[h], fng_got[h], cotangent, branch[h], branch_got[h],
                mod, gain_f, output_weight,
            )
        )
        backs.append(
            attend_back(
                h, q, k, v, att[h], linv[h], e[h], mids[h][2], cosine, sine,
                backs[0][1:] if h else (),
            )
        )
        if h == 0:
            feed_near = feed_own[0].astype(F32) + feed_core_got[0].astype(F32)
            feed_far = (feed_own[1].astype(F32) + feed_core_got[1].astype(F32)).astype(BF)
            feed_x_got = send(feed_far, x_swap)
            fng_got[1], fo_sent, feed_near = together(
                fng_got[1], jnp.where(y == 0, fo[1], fo[0]), feed_near
            )
            fo_got = send(fo_sent, y_swap)
    mg, bg, _, mid_sums = zip(*mids)
    dqs, (dk, dv) = (backs[0][0], backs[1][0]), backs[1][1:]

    attn_own, attn_far = cut([(bg, [att]), ([normed], [dqs, [dk], [dv]])])
    attn_core_got = send(attn_far, core_swap)
    dk, feed_x_got, attn_own = together(dk, feed_x_got, attn_own)
    ang_got = send(input_back(side, dqs, dk, dv, input_weight, False, BF), y_swap)
    feed_grads = over_z(feed_near, feed_x_got)
    down_grad, up_grad = feed_grads[:, :f], feed_grads[:, f:]
    attn_near = attn_own[0].astype(F32) + attn_core_got[0].astype(F32)
    attn_far = (attn_own[1].astype(F32) + attn_core_got[1].astype(F32)).astype(BF)
    attn_x_got = send(attn_far, x_swap)
    ang_own = input_back(side, dqs, dk, dv, input_weight, True, F32)
    mixed, gate_sums = mix(
        side, total, middle, fo, fo_got, cotangent, mod, down_bias.astype(F32).reshape(1, d)
    )
    tok_grad, att_sums = final(side, tokens, ang_own, ang_got, mg, mod, gain_a)
    attn_grads = over_z(attn_near, attn_x_got)
    out_grad, in_grad = attn_grads[:, :inner], attn_grads[:, inner:]

    half_sums = jnp.concatenate([att_sums, gate_sums], axis=0)
    flat = collect(
        half_sums, send(half_sums, y_swap), mid_sums, mod, gain_a, gain_f,
        conditioning.astype(F32), *dbg, *ubg,
    )
    got = send(flat, core_swap)
    both = jnp.where(c == 0, jnp.stack([flat, got]), jnp.stack([got, flat]))
    groups = [[i for i in range(dp_size) if i % 2 == s] for s in range(2)]
    every = lax.all_to_all(
        jnp.broadcast_to(both[None], (dp_size // 2,) + both.shape),
        "dp", 0, 0, axis_index_groups=groups, tiled=True,
    ).reshape((dp_size,) + flat.shape)
    sums = jnp.sum(every[:, 7:], axis=0)
    cond_all = every[:, 0, : conditioning.shape[1]]
    mod_all = every[:, 1:7].reshape(dp_size, 6 * d)
    adaptive_weight_grad = lax.dot_general(
        cond_all, mod_all, (TN, ((), ())),
        precision=lax.Precision.HIGHEST, preferred_element_type=F32,
    )
    adaptive_bias_grad = jnp.sum(mod_all, axis=0)
    return (
        mixed,
        tok_grad,
        in_grad.reshape(r_out, 3, inner).transpose(1, 0, 2),
        out_grad.T,
        up_grad,
        sums[3 : 3 + f // d].reshape(f),
        down_grad.T,
        sums[2],
        sums[0],
        sums[1],
        adaptive_weight_grad,
        adaptive_bias_grad,
    )


def solution(mesh):
    placed = (
        P("dp", None),
        P("dp", None),
        P("dp", None),
        P(None, None, "tensor"),
        P("tensor", None),
        P(None, "tensor"),
        P("tensor"),
        P("tensor", None),
        P(),
        P(),
        P(),
        P(),
        P(),
        P("dp", None),
    )
    return jax.shard_map(
        per_device,
        mesh=mesh,
        in_specs=placed,
        out_specs=(
            P(("dp", "tensor"), None),
            P(("dp", "tensor"), None),
            P(None, "dp", "tensor"),
            P("tensor", "dp"),
            P("dp", "tensor"),
            P("tensor"),
            P("tensor", "dp"),
            P(),
            P(),
            P(),
            P(),
            P(),
        ),
        check_vma=False,
    )
```

```python
import functools

import jax
import jax.numpy as jnp
import numpy as np
from jax import lax
from jax.experimental import pallas as pl
from jax.experimental.pallas import tpu as pltpu
from jax.sharding import PartitionSpec as P

HD = 64
ROW_LEN = 1024
NSEG = 8
BLOCK = 128
PAIR = 2 * HD
RB = 256
HALF = ROW_LEN // 2
STEPS = HALF // RB

norm_eps = 1e-05
masked_score = -1000000000.0
rotary_base = 10000.0
gelu_k = 0.7978845608028654
gelu_c = 0.044715

AXES = ("dp", "tensor")
BF = jnp.bfloat16
F32 = jnp.float32
NN = ((1,), (0,))
NT = ((1,), (1,))
TN = ((0,), (0,))
VMEM = pl.BlockSpec(memory_space=pltpu.VMEM)
SMEM = pl.BlockSpec(memory_space=pltpu.SMEM)


def mm(left, right, dims=NN):
    return lax.dot_general(left, right, (dims, ((), ())), preferred_element_type=F32)


def params(mib):
    return pltpu.CompilerParams(vmem_limit_bytes=mib << 20)


def cost(us):
    return pl.CostEstimate(flops=int(us * 1.15e9), bytes_accessed=0, transcendentals=0)


def shape(dims, kind=F32):
    return jax.ShapeDtypeStruct(dims, kind)


def hbm(*values):
    return [pltpu.with_memory_space_constraint(v, pltpu.HBM) for v in values]


def normalize(values):
    centered = values - jnp.mean(values, axis=-1, keepdims=True)
    inverse = lax.rsqrt(jnp.mean(centered * centered, axis=-1, keepdims=True) + norm_eps)
    return centered * inverse, inverse


def norm_pull(cotangent, xhat, inverse, weight):
    e = cotangent * weight
    return inverse * (
        e
        - jnp.mean(e, axis=-1, keepdims=True)
        - xhat * jnp.mean(e * xhat, axis=-1, keepdims=True)
    )


def live_rows(total, first_row, rows):
    slots = lax.broadcasted_iota(jnp.int32, (rows, 1), 0) + first_row
    return (slots < total).astype(F32)


def rows_of(width, offset=0):
    return pl.BlockSpec((RB, width), lambda i, *_: (i + offset, 0))


def turned_rows(width):
    return pl.BlockSpec((width, RB), lambda i, *_: (0, i))


def whole(*dims):
    return pl.BlockSpec(dims, lambda *_: (0,) * len(dims), pipeline_mode=pl.Buffered(1))


def constant(*dims):
    return pl.BlockSpec(dims, lambda *_: (0,) * len(dims))


def head_masks():
    lane = lax.broadcasted_iota(jnp.int32, (1, PAIR), 1)
    low = (lane < HD).astype(F32)
    return (lane % HD) < HD // 2, (low, 1.0 - low)


def rotary_tables():
    lanes = np.arange(PAIR) % (HD // 2)
    frequency = (rotary_base ** (-lanes * (2.0 / HD))).astype(np.float32)
    angles = np.arange(ROW_LEN, dtype=np.float32)[:, None] * frequency[None, :]
    return np.cos(angles), np.sin(angles)


def place_of(lens, slot):
    segment, start, bound = 0, 0, 0
    for j in range(NSEG):
        bound = bound + lens[0, j]
        passed = bound <= slot
        segment = segment + jnp.where(passed, 1, 0)
        start = start + jnp.where(passed, lens[0, j], 0)
    return segment, start


def total_of(lens):
    total = lens[0, 0]
    for j in range(1, NSEG):
        total = total + lens[0, j]
    return total


def project_kernel(
    lens, tok_ref, cond_ref, aw_ref, ab_ref, gain_ref, w_ref, cost_ref, sint_ref,
    mod_ref, normed_t_ref, q_ref, k_ref, v_ref, cos_ref, sin_ref, normed,
):
    n, d = tok_ref.shape

    @pl.when(pl.program_id(0) == 0)
    def _():
        cond = jnp.broadcast_to(cond_ref[...], (8, cond_ref.shape[1]))
        row = mm(cond, aw_ref[...])[0:1] + ab_ref[...].astype(F32)
        for j in range(6):
            mod_ref[j : j + 1, :] = row[:, j * d : (j + 1) * d]
        weight = gain_ref[...].astype(F32) * (1.0 + row[:, d : 2 * d])
        for i in range(n // RB):
            rows = slice(i * RB, (i + 1) * RB)
            xhat, _ = normalize(tok_ref[rows, :].astype(F32))
            part = (xhat * weight + row[:, :d]).astype(BF)
            normed[rows, :] = part
            normed_t_ref[:, rows] = part.T
        for i in range(n // BLOCK):
            _, start = place_of(lens, i * BLOCK)
            rows = slice(i * BLOCK, (i + 1) * BLOCK)
            at = pl.ds(pl.multiple_of(i * BLOCK - start, BLOCK), BLOCK)
            cos_ref[rows, :] = cost_ref[at, :]
            sin_ref[rows, :] = sint_ref[at, :]

    first, _ = head_masks()
    cos = cos_ref[...]
    sin = sin_ref[...]

    def rotate(u):
        turned = jnp.where(
            first, -pltpu.roll(u, PAIR - HD // 2, 1), pltpu.roll(u, HD // 2, 1)
        )
        return u * cos + turned * sin

    w = jnp.concatenate([w_ref[0], w_ref[1], w_ref[2]], axis=1)
    proj = mm(normed[...], w)
    cols = pl.ds(pl.multiple_of(pl.program_id(0) * PAIR, PAIR), PAIR)
    q_ref[...] = (rotate(proj[:, :PAIR]) * (HD**-0.5)).astype(BF)
    k_ref[:, cols] = rotate(proj[:, PAIR : 2 * PAIR]).astype(BF)
    v_ref[:, cols] = proj[:, 2 * PAIR :].astype(BF)


def project(lens, tok, cond, aw, ab, gain, w):
    n, d = tok.shape
    inner = w.shape[2]
    of_pair = pl.BlockSpec((n, PAIR), lambda p: (0, p))
    tables = [jnp.asarray(t) for t in rotary_tables()]
    return pl.pallas_call(
        project_kernel,
        grid=(inner // PAIR,),
        in_specs=[
            SMEM, whole(n, d), whole(*cond.shape), whole(*aw.shape), VMEM, VMEM,
            pl.BlockSpec((3, d, PAIR), lambda p: (0, 0, p)), whole(n, PAIR), whole(n, PAIR),
        ],
        out_specs=[
            VMEM, constant(d, n), of_pair, VMEM, VMEM, VMEM, VMEM,
        ],
        out_shape=[
            shape((6, d)), pltpu.HBM((d, n), BF), pltpu.HBM((n, inner), BF), shape((n, inner), BF),
            shape((n, inner), BF), shape((n, PAIR)), shape((n, PAIR)),
        ],
        scratch_shapes=[pltpu.VMEM((n, d), BF)],
        compiler_params=params(24),
        cost_estimate=cost(5),
    )(lens, *hbm(tok), cond, *hbm(aw), ab, gain, *hbm(w), *hbm(*tables))


def attend_kernel(
    lens, q_ref, k_ref, v_ref, w_ref, att_ref, linv_ref, e_ref, out_ref, vx, *, first_row
):
    n = ROW_LEN
    step = pl.program_id(0)
    pairs = vx.shape[0]
    _, masks = head_masks()

    @pl.when(step == 0)
    def _():
        for p in range(pairs):
            vx[p, :, 0:PAIR] = v_ref[:, p * PAIR : (p + 1) * PAIR]
            vx[p, :, PAIR:] = jnp.ones((n, PAIR), BF)

    segments = [place_of(lens, i * BLOCK)[0] for i in range(n // BLOCK)]

    def bias_of(block):
        here, _ = place_of(lens, block * BLOCK)
        return jnp.concatenate(
            [
                jnp.full((1, BLOCK), jnp.where(here == there, 0.0, masked_score), F32)
                for there in segments
            ],
            axis=1,
        )

    per = RB // BLOCK
    biases = [bias_of(first_row // BLOCK + step * per + b) for b in range(per)]
    low = masks[0] > 0.5
    for p in range(pairs):
        cols = slice(p * PAIR, (p + 1) * PAIR)
        q = q_ref[:, cols].astype(F32)
        keys = k_ref[:, cols]
        outs = []
        for h in range(2):
            s = mm((q * masks[h]).astype(BF), keys, NT)
            s = jnp.concatenate(
                [s[b * BLOCK : (b + 1) * BLOCK] + biases[b] for b in range(per)], axis=0
            )
            peak = jnp.max(s, axis=1, keepdims=True)
            e = jnp.exp(s - peak).astype(BF)
            e_ref[p, h] = e
            outs.append(mm(e, vx[p]))
        inverse = 1.0 / jnp.where(low, outs[0][:, PAIR:], outs[1][:, PAIR:])
        att_ref[:, cols] = (
            jnp.where(low, outs[0][:, :PAIR], outs[1][:, :PAIR]) * inverse
        ).astype(BF)
        linv_ref[:, cols] = inverse
    rows = pl.ds(pl.multiple_of(step * RB, RB), RB)
    out_ref[rows, :] = mm(att_ref[...], w_ref[...]).astype(BF)


def attend(half, lens, q, k, v, w):
    n, inner = q.shape
    d = w.shape[1]
    pairs = inner // PAIR
    return pl.pallas_call(
        functools.partial(attend_kernel, first_row=half * HALF),
        grid=(STEPS,),
        in_specs=[SMEM, rows_of(inner, half * STEPS), VMEM, VMEM, VMEM],
        out_specs=[
            rows_of(inner), rows_of(inner),
            pl.BlockSpec((pairs, 2, RB, n), lambda i: (0, 0, i, 0)), VMEM,
        ],
        out_shape=[
            pltpu.HBM((HALF, inner), BF), pltpu.HBM((HALF, inner), F32),
            pltpu.HBM((pairs, 2, HALF, n), BF), shape((HALF, d), BF),
        ],
        scratch_shapes=[pltpu.VMEM((pairs, n, 2 * PAIR), BF)],
        compiler_params=params(18),
        cost_estimate=cost(8),
    )(lens, *hbm(q), k, v, w)


def attend_back_kernel(
    q_ref, k_ref, v_ref, att_ref, linv_ref, do_ref, e_ref, cos_ref, sin_ref, *refs, last
):
    n = ROW_LEN
    if last:
        dk0_ref, dv0_ref, dq_ref, dkout_ref, dvout_ref, vx, km, ds, dk, dv = refs
    else:
        dq_ref, dk, dv, vx, km, ds = refs
    pairs = vx.shape[0]
    step = pl.program_id(0)
    first, masks = head_masks()

    @pl.when(step == 0)
    def _():
        for p in range(pairs):
            cols = slice(p * PAIR, (p + 1) * PAIR)
            vx[p, :, 0:PAIR] = v_ref[:, cols]
            vx[p, :, PAIR:] = jnp.ones((n, PAIR), BF)
            keys = k_ref[:, cols].astype(F32)
            for h in range(2):
                km[p, h] = (keys * masks[h]).astype(BF)

    def rotate_back(u, rows):
        w = u * sin_ref[rows, :]
        turned = jnp.where(
            first, pltpu.roll(w, PAIR - HD // 2, 1), -pltpu.roll(w, HD // 2, 1)
        )
        return u * cos_ref[rows, :] + turned

    start = (HALF if last else 0) + step * RB
    rows = pl.ds(pl.multiple_of(start, RB), RB)
    here = pl.ds(pl.multiple_of(step * RB, RB), RB)
    for p in range(pairs):
        cols = slice(p * PAIR, (p + 1) * PAIR)
        dof = do_ref[here, cols].astype(F32) * linv_ref[:, cols]
        dd = dof * att_ref[:, cols].astype(F32)
        qf = q_ref[:, cols].astype(F32)
        qs, dms, dq = [], [], None
        for h in range(2):
            dm = (dof * masks[h]).astype(BF)
            left = jnp.concatenate([dm, (-dd * masks[h]).astype(BF)], axis=1)
            dp = mm(left, vx[p], NT)
            sg = (dp * e_ref[p, h].astype(F32)).astype(BF)
            ds[h * RB : (h + 1) * RB, :] = sg
            part = mm(sg, km[p, h])
            dq = part if dq is None else dq + part
            qs.append((qf * masks[h]).astype(BF))
            dms.append(dm)
        dq_ref[here, cols] = (rotate_back(dq, rows) * (HD**-0.5)).astype(BF)
        a = mm(jnp.concatenate(qs, axis=0).T, ds[...])
        b = mm(jnp.concatenate(dms, axis=0).T, e_ref[p].reshape(2 * RB, n))

        @pl.when(step == 0)
        def _(p=p, a=a, b=b):
            if last:
                dk[p] = dk0_ref[p] + a
                dv[p] = dv0_ref[p] + b
            else:
                dk[p] = a
                dv[p] = b

        @pl.when(step > 0)
        def _(p=p, a=a, b=b):
            dk[p] += a
            dv[p] += b

    if last:

        @pl.when(step == STEPS - 1)
        def _():
            for p in range(pairs):
                cols = slice(p * PAIR, (p + 1) * PAIR)
                dkout_ref[:, cols] = rotate_back(dk[p].T, slice(None)).astype(BF)
                dvout_ref[:, cols] = dv[p].T.astype(BF)


def attend_back(half, q, k, v, att, linv, e, do, cos, sin, before=()):
    n, inner = q.shape
    pairs = inner // PAIR
    last = half == 1
    sums = [pltpu.VMEM((pairs, PAIR, n), F32)] * 2
    return pl.pallas_call(
        functools.partial(attend_back_kernel, last=last),
        grid=(STEPS,),
        in_specs=[
            rows_of(inner, half * STEPS), VMEM, VMEM, rows_of(inner), rows_of(inner),
            VMEM, pl.BlockSpec((pairs, 2, RB, n), lambda i: (0, 0, i, 0)), VMEM, VMEM,
        ]
        + [VMEM] * len(before),
        out_specs=[VMEM] * 3,
        out_shape=[shape((HALF, inner), BF)]
        + ([shape((n, inner), BF)] * 2 if last else [shape((pairs, PAIR, n))] * 2),
        scratch_shapes=[
            pltpu.VMEM((pairs, n, 2 * PAIR), BF),
            pltpu.VMEM((pairs, 2, n, PAIR), BF),
            pltpu.VMEM((2 * RB, n), BF),
        ]
        + (sums if last else []),
        compiler_params=params(24),
        cost_estimate=cost(30),
    )(*hbm(q), k, v, *hbm(att, linv), do, *hbm(e), cos, sin, *before)


def feed_kernel(
    lens, tok_ref, own_ref, got_ref, cot_ref, mod_ref, gain_ref, ub_ref, up_ref, down_ref,
    middle_ref, fin_t_ref, act_ref, ug_ref, fg_t_ref, fo_ref, fng_ref, ubg_ref, sums_ref,
    *, first_row,
):
    i = pl.program_id(0)
    rows = pl.ds(pl.multiple_of(i * RB, RB), RB)
    mod = mod_ref[...]
    branch = own_ref[rows, :].astype(F32) + got_ref[...].astype(F32)
    middle = tok_ref[...].astype(F32) + mod[2:3] * branch
    middle_ref[rows, :] = middle
    xhat, _ = normalize(middle)
    fin = (xhat * (gain_ref[...].astype(F32) * (1.0 + mod[4:5])) + mod[3:4]).astype(BF)
    fin_t_ref[:, rows] = fin.T
    seed = cot_ref[...].astype(F32) * live_rows(total_of(lens), first_row + i * RB, RB)
    fg = (mod[5:6] * seed).astype(BF)
    fg_t_ref[:, rows] = fg.T
    u = mm(fin, up_ref[...]) + ub_ref[...].astype(F32)
    u2 = u * u
    t = jnp.tanh(u * (gelu_k + (gelu_k * gelu_c) * u2))
    half = 0.5 * (1.0 + t)
    act = (u * half).astype(BF)
    act_ref[rows, :] = act
    slope = half + (0.5 * u) * (1.0 - t * t) * (gelu_k + (3.0 * gelu_k * gelu_c) * u2)
    ugf = mm(fg, down_ref[...], NT) * slope
    ug = ugf.astype(BF)
    ug_ref[rows, :] = ug
    fng_ref[rows, :] = mm(ug, up_ref[...], NT).astype(BF)
    fo = mm(act, down_ref[...])
    fo_ref[rows, :] = fo.astype(BF)
    ubs = jnp.sum(ugf, axis=0, keepdims=True)
    sums = jnp.concatenate(
        [jnp.sum(seed, axis=0, keepdims=True), jnp.sum(seed * fo, axis=0, keepdims=True)], axis=0
    )

    @pl.when(i == 0)
    def _():
        ubg_ref[...] = ubs
        sums_ref[...] = sums

    @pl.when(i > 0)
    def _():
        ubg_ref[...] += ubs
        sums_ref[...] += sums


def feed(half, lens, tok, own, got, cot, mod, gain, ub, up, down):
    d, f = up.shape
    here = rows_of(d, half * STEPS)
    return pl.pallas_call(
        functools.partial(feed_kernel, first_row=half * HALF),
        grid=(STEPS,),
        in_specs=[
            SMEM, here, VMEM, rows_of(d), here, VMEM, VMEM, VMEM, VMEM, VMEM,
        ],
        out_specs=[VMEM] * 9,
        out_shape=[
            shape((HALF, d)), shape((d, HALF), BF), shape((HALF, f), BF),
            shape((HALF, f), BF), shape((d, HALF), BF), shape((HALF, d), BF),
            shape((HALF, d), BF), shape((1, f)), shape((2, d)),
        ],
        compiler_params=params(16),
        cost_estimate=cost(9),
    )(lens, *hbm(tok), own, got, *hbm(cot), mod, gain, ub, up, down)


def middle_kernel(
    lens, middle_ref, own_ref, got_ref, cot_ref, bown_ref, bgot_ref, mod_ref, gain_ref, w_ref,
    mg_ref, bg_t_ref, do_ref, sums_ref, *, first_row,
):
    i = pl.program_id(0)
    rows = pl.ds(pl.multiple_of(i * RB, RB), RB)
    mod = mod_ref[...]
    xhat, inverse = normalize(middle_ref[rows, :])
    c = own_ref[rows, :].astype(F32) + got_ref[...].astype(F32)
    seed = cot_ref[...].astype(F32) * live_rows(total_of(lens), first_row + i * RB, RB)
    mg = seed + norm_pull(c, xhat, inverse, gain_ref[...].astype(F32) * (1.0 + mod[4:5]))
    mg_ref[...] = mg
    bg = (mod[2:3] * mg).astype(BF)
    bg_t_ref[:, rows] = bg.T
    do_ref[rows, :] = mm(bg, w_ref[...], NT).astype(BF)
    branch = bown_ref[rows, :].astype(F32) + bgot_ref[...].astype(F32)
    sums = jnp.concatenate(
        [
            jnp.sum(mg * branch, axis=0, keepdims=True),
            jnp.sum(c, axis=0, keepdims=True),
            jnp.sum(c * xhat, axis=0, keepdims=True),
        ],
        axis=0,
    )

    @pl.when(i == 0)
    def _():
        sums_ref[...] = sums

    @pl.when(i > 0)
    def _():
        sums_ref[...] += sums


def middle_back(half, lens, middle, own, got, cot, bown, bgot, mod, gain, w):
    inner, d = w.shape
    return pl.pallas_call(
        functools.partial(middle_kernel, first_row=half * HALF),
        grid=(STEPS,),
        in_specs=[
            SMEM, VMEM, VMEM, rows_of(d), rows_of(d, half * STEPS), VMEM, rows_of(d), VMEM, VMEM,
            VMEM,
        ],
        out_specs=[rows_of(d), VMEM, VMEM, VMEM],
        out_shape=[
            pltpu.HBM((HALF, d), F32), shape((d, HALF), BF), shape((HALF, inner), BF), shape((3, d)),
        ],
        compiler_params=params(14),
        cost_estimate=cost(40),
    )(lens, middle, own, got, *hbm(cot), bown, bgot, mod, gain, w)


def weight_grad_kernel(starts, *refs, ins, plan, outs, blocks, chunk):
    out, g = refs[ins : ins + outs], refs[ins + outs]
    j = pl.program_id(0)
    begin = 0
    for chunks, parts in plan:

        @pl.when((j >= begin) & (j < begin + chunks))
        def _(parts=parts, begin=begin):
            cols = pl.ds(pl.multiple_of((j - begin) * chunk, 128), chunk)
            total = None
            for left, column, part in parts:
                size = refs[part].shape[0]
                term = mm(refs[left][:, column : column + size], refs[part][:, cols])
                total = term if total is None else total + term
            g[...] = total

        begin += chunks
    size = out[0].shape[1]
    cols = pl.ds(pl.multiple_of(j * chunk, 128), chunk)
    for k in range(outs):
        for m in range(blocks):
            rows = pl.ds(pl.multiple_of(starts[k * blocks + m], 16), size)
            out[k][m, :, cols] = g[rows, :].astype(BF)


def weight_grad(couples, starts, outs, blocks, size, chunk):
    ins, specs, plan, begin = [], [], [], 0
    for lefts, rights in couples:
        columns = []
        for part in lefts:
            columns += [(len(ins), i) for i in range(0, part.shape[1], HALF)]
            ins.append(part)
            specs.append(VMEM)
        for parts in rights:
            chunks = parts[0].shape[1] // chunk
            entries, row = [], 0
            for part in parts:
                left, column = columns[row // HALF]
                entries.append((left, column, len(ins)))
                row += part.shape[0]
                ins.append(part)
                specs.append(VMEM)
            plan.append((chunks, entries))
            begin += chunks
    d = couples[0][0][0].shape[0]
    return pl.pallas_call(
        functools.partial(
            weight_grad_kernel, ins=len(ins), plan=plan, outs=outs, blocks=blocks, chunk=chunk
        ),
        grid=(begin,),
        in_specs=[SMEM] + specs,
        out_specs=[VMEM] * outs,
        out_shape=[shape((blocks, size, begin * chunk), BF)] * outs,
        scratch_shapes=[pltpu.VMEM((d, chunk), F32)],
        compiler_params=params(12),
        cost_estimate=cost(4),
    )(starts, *ins)


def mix_kernel(side, m0_ref, m1_ref, f0_ref, f1_ref, got_ref, mod_ref, bias_ref, out_ref):
    second = side[0] == 1
    own = jnp.where(second, f1_ref[...], f0_ref[...])
    fo = own.astype(F32) + got_ref[...].astype(F32) + bias_ref[...].astype(F32)
    middle = jnp.where(second, m1_ref[...], m0_ref[...])
    out_ref[...] = (middle + mod_ref[5:6] * fo).astype(BF)


def here_rows(width):
    return pl.BlockSpec((RB, width), lambda i, side: (side[0] * STEPS + i, 0))


def mix(side, middles, outs, got, mod, bias):
    d = got.shape[1]
    return pl.pallas_call(
        mix_kernel,
        grid_spec=pltpu.PrefetchScalarGridSpec(
            num_scalar_prefetch=1,
            grid=(STEPS,),
            in_specs=[rows_of(d)] * 5 + [VMEM, VMEM],
            out_specs=rows_of(d),
        ),
        out_shape=shape((HALF, d), BF),
        compiler_params=params(16),
        cost_estimate=cost(1),
    )(side, *hbm(*middles, *outs), got, mod, bias)


def input_back_kernel(side, q0_ref, q1_ref, k_ref, v_ref, w_ref, out_ref, *, mine):
    second = (side[0] == 1) if mine else (side[0] == 0)
    here = pl.ds(pl.multiple_of(pl.program_id(0) * RB, RB), RB)
    dq = jnp.where(second, q1_ref[here, :], q0_ref[here, :])
    start = (side[0] if mine else 1 - side[0]) * HALF + pl.program_id(0) * RB
    rows = pl.ds(pl.multiple_of(start, RB), RB)
    total = mm(dq, w_ref[0], NT)
    total += mm(k_ref[rows, :], w_ref[1], NT)
    total += mm(v_ref[rows, :], w_ref[2], NT)
    out_ref[here, :] = total.astype(out_ref.dtype)


def input_back(side, dqs, dk, dv, w, mine, kind):
    _, d, inner = w.shape
    return pl.pallas_call(
        functools.partial(input_back_kernel, mine=mine),
        grid_spec=pltpu.PrefetchScalarGridSpec(
            num_scalar_prefetch=1,
            grid=(STEPS,),
            in_specs=[VMEM] * 5,
            out_specs=VMEM,
        ),
        out_shape=shape((HALF, d), kind),
        compiler_params=params(24),
        cost_estimate=cost(1),
    )(side, *dqs, dk, dv, w)


def final_kernel(side, tok_ref, own_ref, got_ref, mg0_ref, mg1_ref, mod_ref, gain_ref, out_ref, sums_ref):
    i = pl.program_id(0)
    xhat, inverse = normalize(tok_ref[...].astype(F32))
    c = own_ref[...] + got_ref[...].astype(F32)
    mg = jnp.where(side[0] == 1, mg1_ref[...], mg0_ref[...])
    out_ref[...] = mg + norm_pull(c, xhat, inverse, gain_ref[...].astype(F32) * (1.0 + mod_ref[1:2]))
    sums = jnp.concatenate(
        [jnp.sum(c, axis=0, keepdims=True), jnp.sum(c * xhat, axis=0, keepdims=True)], axis=0
    )

    @pl.when(i == 0)
    def _():
        sums_ref[...] = sums

    @pl.when(i > 0)
    def _():
        sums_ref[...] += sums


def final(side, tok, own, got, mgs, mod, gain):
    d = tok.shape[1]
    return pl.pallas_call(
        final_kernel,
        grid_spec=pltpu.PrefetchScalarGridSpec(
            num_scalar_prefetch=1,
            grid=(STEPS,),
            in_specs=[here_rows(d)] + [rows_of(d)] * 4 + [whole(6, d), whole(1, d)],
            out_specs=[rows_of(d), constant(2, d)],
        ),
        out_shape=[shape((HALF, d)), shape((2, d))],
        compiler_params=params(24),
        cost_estimate=cost(1),
    )(side, *hbm(tok), own, got, *hbm(*mgs), mod, gain)


def collect_kernel(
    half_ref, got_ref, mid0_ref, mid1_ref, seed0_ref, seed1_ref, mod_ref, ga_ref, gf_ref, db_ref,
    cond_ref, u0_ref, u1_ref, out_ref, all_ref,
):
    half = half_ref[...] + got_ref[...]
    mid = mid0_ref[...] + mid1_ref[...]
    seeds = seed0_ref[0:1, :] + seed1_ref[0:1, :]
    d = half.shape[1]
    s_att, s_feed = half[1:2], mid[2:3]
    all_ref[...] = jnp.zeros_like(all_ref)
    all_ref[0:1, : cond_ref.shape[1]] = cond_ref[...].astype(F32)
    rows = (
        half[0:1], s_att * ga_ref[...].astype(F32), mid[0:1], mid[1:2],
        s_feed * gf_ref[...].astype(F32), half[2:3] + seeds * db_ref[...].astype(F32),
        (1.0 + mod_ref[1:2]) * s_att, (1.0 + mod_ref[4:5]) * s_feed, mod_ref[5:6] * seeds,
    )
    for i, row in enumerate(rows):
        all_ref[i + 1 : i + 2, :] = row
    for i in range(u0_ref.shape[1] // d):
        cols = slice(i * d, (i + 1) * d)
        all_ref[10 + i : 11 + i, :] = u0_ref[:, cols] + u1_ref[:, cols]
    out_ref[...] = all_ref[...].astype(BF)


def collect(half, got, mids, seeds, mod, ga, gf, db, cond, ubs):
    d = half.shape[1]
    rows = -(-(10 + ubs[0].shape[1] // d) // 16) * 16
    return pl.pallas_call(
        collect_kernel,
        in_specs=[VMEM] * 13,
        out_specs=VMEM,
        out_shape=shape((rows, d), BF),
        scratch_shapes=[pltpu.VMEM((rows, d), F32)],
        compiler_params=params(4),
        cost_estimate=cost(1),
    )(half, got, *mids, *seeds, mod, ga, gf, db, cond, *ubs)


def finish_kernel(every_ref, weight_ref, bias_ref, sums_ref):
    d = every_ref.shape[2]
    cond = every_ref[:, 0, :]
    for j in range(6):
        rows = every_ref[:, 1 + j, :]
        weight_ref[:, j * d : (j + 1) * d] = mm(cond[:, : weight_ref.shape[0]], rows, TN)
        bias_ref[j : j + 1, :] = jnp.sum(rows.astype(F32), axis=0, keepdims=True)
    sums_ref[...] = jnp.zeros_like(sums_ref)
    for j in range(every_ref.shape[1] - 7):
        rows = every_ref[:, 7 + j, :].astype(F32)
        sums_ref[j : j + 1, :] = jnp.sum(rows, axis=0, keepdims=True)


def finish(every, cond_dim):
    rows, kinds, d = every.shape
    return pl.pallas_call(
        finish_kernel,
        in_specs=[VMEM],
        out_specs=[VMEM] * 3,
        out_shape=[shape((cond_dim, 6 * d)), shape((6, d)), shape((kinds, d))],
        compiler_params=params(12),
        cost_estimate=cost(2),
    )(every)


def together(*values):
    return lax.optimization_barrier(values)


def perm(dp_size, move):
    pairs = []
    for index in range(dp_size):
        for y in range(2):
            to = move(index >> 2, (index >> 1) & 1, y, index & 1)
            pairs.append((index * 2 + y, ((to[0] * 2 + to[1]) * 2 + to[3]) * 2 + to[2]))
    return pairs


def xor_order(stack, me, bits):
    for b in range(bits):
        shaped = stack.reshape((-1, 2, 1 << b) + stack.shape[1:])
        flipped = jnp.concatenate([shaped[:, 1:], shaped[:, :1]], axis=1)
        stack = jnp.where(((me >> b) & 1) == 1, flipped, shaped).reshape(stack.shape)
    return stack


def per_device(
    tokens,
    conditioning,
    lengths,
    input_weight,
    output_weight,
    up_weight,
    up_bias,
    down_weight,
    down_bias,
    attention_gain,
    feed_gain,
    adaptive_weight,
    adaptive_bias,
    cotangent,
):
    n, d = tokens.shape
    assert lengths.shape[0] == 1
    inner = input_weight.shape[2]
    f = up_weight.shape[1]
    dp_size = lax.axis_size("dp")
    planes = dp_size // 4
    zbits = planes.bit_length() - 1
    index = lax.axis_index("dp")
    y = lax.axis_index("tensor")
    c = index % 2
    x = (index // 2) % 2
    z = index // 4
    side = y.astype(jnp.int32).reshape(1)

    make = functools.partial(perm, dp_size)
    y_swap = make(lambda z, x, y, c: (z, x, 1 - y, c))
    core_swap = make(lambda z, x, y, c: (z, x, y, 1 - c))
    x_swap = make(lambda z, x, y, c: (z, 1 - x, y, c))

    def send(value, how):
        return lax.ppermute(value, AXES, how)

    gain_a = attention_gain.reshape(1, d)
    gain_f = feed_gain.reshape(1, d)
    up_b = up_bias.reshape(1, f)

    mod, normed_t, q, k, v, cosine, sine = project(
        lengths, tokens, conditioning, adaptive_weight, adaptive_bias.reshape(1, -1), gain_a,
        input_weight,
    )
    halves = (0, 1)
    att, linv, e, branch, branch_got = [], [], [], [], []
    for h in halves:
        got = attend(h, lengths, q, k, v, output_weight)
        for store, value in zip((att, linv, e, branch), got):
            store.append(value)
        if h == 0:
            branch[0], k = together(branch[0], k)
        branch_got.append(send(branch[h], y_swap))
    fed, fng_got = [], []
    for h in halves:
        fed.append(
            feed(
                h, lengths, tokens, branch[h], branch_got[h], cotangent, mod, gain_f, up_b,
                up_weight, down_weight,
            )
        )
        fng_sent = fed[h][6]
        if h == 0:
            fng_sent, branch_got[1] = together(fng_sent, branch_got[1])
        fng_got.append(send(fng_sent, y_swap))
    middle, fin_t, act, ug, fg_t, fo, fng, ubg, seed_sums = zip(*fed)

    r_out = d // dp_size

    def cut(couples, chunk):
        if r_out % 16 == 0:
            place = [
                (((z ^ m) * 2 + (x ^ dx)) * 2 + (c ^ s)) * r_out
                for s in range(2)
                for dx in range(2)
                for m in range(planes)
            ]
            starts = jnp.stack([p.astype(jnp.int32) for p in place])
            outs = weight_grad(couples, starts, 2, 2 * planes, r_out, chunk)
        else:
            grad = jnp.concatenate(
                [
                    mm(jnp.concatenate(a, axis=1), jnp.concatenate(b)).astype(BF)
                    for a, bs in couples
                    for b in bs
                ],
                axis=1,
            )
            blocks = grad.reshape(planes, 2, 2, r_out, grad.shape[1])
            blocks = xor_order(blocks, z, zbits).transpose(2, 1, 0, 3, 4)
            blocks = xor_order(blocks, c, 1)
            outs = [xor_order(b, x, 1) for b in blocks]
        return [o.reshape(2, planes, r_out, -1) for o in outs]

    def send_z(total):
        return [
            send(total[m].astype(BF), make(lambda z, x, y, c: (z ^ m, x, y, c)))
            for m in range(1, planes)
        ]

    def sum_z(total, got):
        return sum((v.astype(F32) for v in got), total[0])

    feed_own, feed_far = cut([(fg_t, [act]), (fin_t, [ug])], f // 2)
    feed_core_got = send(feed_far, core_swap)
    fng_got[0], feed_own = together(fng_got[0], feed_own)

    mids, backs = [], []
    for h in halves:
        mids.append(
            middle_back(
                h, lengths, middle[h], fng[h], fng_got[h], cotangent, branch[h], branch_got[h],
                mod, gain_f, output_weight,
            )
        )
        if h == 0:
            feed_core_got, do = together(feed_core_got, mids[0][2])
            feed_near = feed_own[0].astype(F32) + feed_core_got[0].astype(F32)
            feed_far = (feed_own[1].astype(F32) + feed_core_got[1].astype(F32)).astype(BF)
            do, feed_far = together(do, feed_far)
            feed_x_got = send(feed_far, x_swap)
        else:
            do = mids[1][2]
        backs.append(
            attend_back(
                h, q, k, v, att[h], linv[h], e[h], do, cosine, sine, backs[0][1:] if h else ()
            )
        )
        if h == 0:
            fng_got[1], fo_sent, _ = together(
                fng_got[1], jnp.where(y == 0, fo[1], fo[0]), backs[0][0]
            )
            fo_got = send(fo_sent, y_swap)
    mg, bg_t, _, mid_sums = zip(*mids)
    dqs, (dk, dv) = (backs[0][0], backs[1][0]), backs[1][1:]

    fo_got, dk = together(fo_got, dk)
    ang_other = input_back(side, dqs, dk, dv, input_weight, False, BF)
    dk, ang_other = together(dk, ang_other)
    ang_got = send(ang_other, y_swap)
    attn_own, attn_far = cut([(bg_t, [att]), ([normed_t], [dqs, [dk], [dv]])], inner)
    attn_core_got = send(attn_far, core_swap)
    dk, feed_x_got, attn_own = together(dk, feed_x_got, attn_own)
    feed_total = feed_near + feed_x_got.astype(F32)
    feed_total, attn_core_got = together(feed_total, attn_core_got)
    feed_z_got = send_z(feed_total)
    attn_near = attn_own[0].astype(F32) + attn_core_got[0].astype(F32)
    attn_far = (attn_own[1].astype(F32) + attn_core_got[1].astype(F32)).astype(BF)
    attn_far, dk = together(attn_far, dk)
    attn_x_got = send(attn_far, x_swap)
    ang_own = input_back(side, dqs, dk, dv, input_weight, True, F32)
    tok_grad, att_sums = final(side, tokens, ang_own, ang_got, mg, mod, gain_a)

    half_sums = jnp.concatenate([att_sums, seed_sums[0][1:] + seed_sums[1][1:]], axis=0)
    flat = collect(
        half_sums, send(half_sums, y_swap), mid_sums, seed_sums, mod, gain_a, gain_f,
        down_bias.reshape(1, d), conditioning, ubg,
    )
    flat, attn_x_got, fo_got = together(flat, attn_x_got, fo_got)
    every = lax.all_to_all(
        jnp.broadcast_to(flat[None], (dp_size,) + flat.shape), "dp", 0, 0, tiled=True
    )
    attn_total = attn_near + attn_x_got.astype(F32)
    attn_z_got = send_z(attn_total)
    mixed = mix(side, middle, fo, fo_got, mod, down_bias.reshape(1, d))
    mixed, *feed_z_got = together(mixed, *feed_z_got)
    feed_grads = sum_z(feed_total, feed_z_got)
    down_grad, up_grad = feed_grads[:, :f], feed_grads[:, f:]
    attn_grads = sum_z(attn_total, attn_z_got)
    out_grad, in_grad = attn_grads[:, :inner], attn_grads[:, inner:]
    adaptive_weight_grad, adaptive_bias_grad, sums = finish(
        every.reshape(dp_size, flat.shape[0], d), conditioning.shape[1]
    )
    return (
        mixed,
        tok_grad,
        in_grad.reshape(r_out, 3, inner).transpose(1, 0, 2),
        out_grad.T,
        up_grad,
        sums[3 : 3 + f // d].reshape(f),
        down_grad.T,
        sums[2],
        sums[0],
        sums[1],
        adaptive_weight_grad,
        adaptive_bias_grad.reshape(-1),
    )


def solution(mesh):
    placed = (
        P("dp", None),
        P("dp", None),
        P("dp", None),
        P(None, None, "tensor"),
        P("tensor", None),
        P(None, "tensor"),
        P("tensor"),
        P("tensor", None),
        P(),
        P(),
        P(),
        P(),
        P(),
        P("dp", None),
    )
    return jax.shard_map(
        per_device,
        mesh=mesh,
        in_specs=placed,
        out_specs=(
            P(("dp", "tensor"), None),
            P(("dp", "tensor"), None),
            P(None, "dp", "tensor"),
            P("tensor", "dp"),
            P("dp", "tensor"),
            P("tensor"),
            P("tensor", "dp"),
            P(),
            P(),
            P(),
            P(),
            P(),
        ),
        check_vma=False,
    )
```

```python
import functools

import jax
import jax.numpy as jnp
import numpy as np
from jax import lax
from jax.experimental import pallas as pl
from jax.experimental.pallas import tpu as pltpu
from jax.sharding import PartitionSpec as P

HD = 64
ROW_LEN = 1024
NSEG = 8
BLOCK = 128
PAIR = 2 * HD
RB = 256
HALF = ROW_LEN // 2
STEPS = HALF // RB

norm_eps = 1e-05
masked_score = -1000000000.0
rotary_base = 10000.0
gelu_k = 0.7978845608028654
gelu_c = 0.044715

AXES = ("dp", "tensor")
BF = jnp.bfloat16
F32 = jnp.float32
NN = ((1,), (0,))
NT = ((1,), (1,))
TN = ((0,), (0,))
VMEM = pl.BlockSpec(memory_space=pltpu.VMEM)
SMEM = pl.BlockSpec(memory_space=pltpu.SMEM)
FAR = pl.BlockSpec(memory_space=pltpu.HBM)


def mm(left, right, dims=NN):
    return lax.dot_general(left, right, (dims, ((), ())), preferred_element_type=F32)


def params(mib):
    return pltpu.CompilerParams(vmem_limit_bytes=mib << 20)


def cost(us):
    return pl.CostEstimate(flops=int(us * 1.15e9), bytes_accessed=0, transcendentals=0)


def shape(dims, kind=F32):
    return jax.ShapeDtypeStruct(dims, kind)


def hbm(*values):
    return [pltpu.with_memory_space_constraint(v, pltpu.HBM) for v in values]


def normalize(values):
    centered = values - jnp.mean(values, axis=-1, keepdims=True)
    inverse = lax.rsqrt(jnp.mean(centered * centered, axis=-1, keepdims=True) + norm_eps)
    return centered * inverse, inverse


def norm_pull(cotangent, xhat, inverse, weight):
    e = cotangent * weight
    return inverse * (
        e
        - jnp.mean(e, axis=-1, keepdims=True)
        - xhat * jnp.mean(e * xhat, axis=-1, keepdims=True)
    )


def live_rows(total, first_row, rows):
    slots = lax.broadcasted_iota(jnp.int32, (rows, 1), 0) + first_row
    return (slots < total).astype(F32)


def rows_of(width, offset=0):
    return pl.BlockSpec((RB, width), lambda i, *_: (i + offset, 0))


def turned_rows(width):
    return pl.BlockSpec((width, RB), lambda i, *_: (0, i))


def whole(*dims):
    return pl.BlockSpec(dims, lambda *_: (0,) * len(dims), pipeline_mode=pl.Buffered(1))


def constant(*dims):
    return pl.BlockSpec(dims, lambda *_: (0,) * len(dims))


def head_masks():
    lane = lax.broadcasted_iota(jnp.int32, (1, PAIR), 1)
    low = (lane < HD).astype(F32)
    return (lane % HD) < HD // 2, (low, 1.0 - low)


def rotary_tables():
    lanes = np.arange(PAIR) % (HD // 2)
    frequency = (rotary_base ** (-lanes * (2.0 / HD))).astype(np.float32)
    angles = np.arange(ROW_LEN, dtype=np.float32)[:, None] * frequency[None, :]
    return np.cos(angles), np.sin(angles)


def place_of(lens, slot):
    segment, start, bound = 0, 0, 0
    for j in range(NSEG):
        bound = bound + lens[0, j]
        passed = bound <= slot
        segment = segment + jnp.where(passed, 1, 0)
        start = start + jnp.where(passed, lens[0, j], 0)
    return segment, start


def total_of(lens):
    total = lens[0, 0]
    for j in range(1, NSEG):
        total = total + lens[0, j]
    return total


def project_kernel(
    lens, tokfar_ref, cond_ref, awfar_ref, ab_ref, gain_ref, wfar_ref, cosfar_ref, sinfar_ref,
    mod_ref, turnedfar_ref, q_ref, k_ref, v_ref, cos_ref, sin_ref,
    tok, aw, w, cos_table, sin_table, normed, turned, sems,
):
    n, d = tok.shape
    pairs = k_ref.shape[1] // PAIR
    copies = [
        pltpu.make_async_copy(source, target, sems.at[i])
        for i, (source, target) in enumerate(
            (
                (awfar_ref, aw), (tokfar_ref, tok), (wfar_ref, w), (cosfar_ref, cos_table),
                (sinfar_ref, sin_table), (turned, turnedfar_ref),
            )
        )
    ]
    for copy in copies[:5]:
        copy.start()
    copies[0].wait()
    cond = jnp.broadcast_to(cond_ref[...], (8, cond_ref.shape[1]))
    row = mm(cond, aw[...])[0:1] + ab_ref[...].astype(F32).reshape(1, 6 * d)
    for j in range(6):
        mod_ref[j : j + 1, :] = row[:, j * d : (j + 1) * d]
    weight = gain_ref[...].astype(F32).reshape(1, d) * (1.0 + row[:, d : 2 * d])
    copies[1].wait()
    for i in range(n // RB):
        rows = slice(i * RB, (i + 1) * RB)
        xhat, _ = normalize(tok[rows, :].astype(F32))
        part = (xhat * weight + row[:, :d]).astype(BF)
        normed[rows, :] = part
        turned[:, rows] = part.T
    copies[5].start()
    copies[3].wait()
    copies[4].wait()
    for i in range(n // BLOCK):
        _, start = place_of(lens, i * BLOCK)
        rows = slice(i * BLOCK, (i + 1) * BLOCK)
        at = pl.ds(pl.multiple_of(i * BLOCK - start, BLOCK), BLOCK)
        cos_ref[rows, :] = cos_table[at, :]
        sin_ref[rows, :] = sin_table[at, :]
    copies[2].wait()
    first, _ = head_masks()

    def rotate(u, rows):
        turned_u = jnp.where(
            first, -pltpu.roll(u, PAIR - HD // 2, 1), pltpu.roll(u, HD // 2, 1)
        )
        return u * cos_ref[rows, :] + turned_u * sin_ref[rows, :]

    for i in range(n // HALF):
        rows = slice(i * HALF, (i + 1) * HALF)
        left = normed[rows, :]
        queries, keys, values = (mm(left, w[j]) for j in range(3))
        for p in range(pairs):
            cols = slice(p * PAIR, (p + 1) * PAIR)
            q_ref[rows, cols] = (rotate(queries[:, cols], rows) * (HD**-0.5)).astype(BF)
            k_ref[rows, cols] = rotate(keys[:, cols], rows).astype(BF)
        v_ref[rows, :] = values.astype(BF)
    copies[5].wait()


def project(lens, tok, cond, aw, ab, gain, w):
    n, d = tok.shape
    inner = w.shape[2]
    tables = [jnp.asarray(t) for t in rotary_tables()]
    return pl.pallas_call(
        project_kernel,
        in_specs=[SMEM, FAR, VMEM, FAR, VMEM, VMEM, FAR, FAR, FAR],
        out_specs=[VMEM, FAR, VMEM, VMEM, VMEM, VMEM, VMEM],
        out_shape=[
            shape((6, d)), pltpu.HBM((d, n), BF), shape((n, inner), BF), shape((n, inner), BF),
            shape((n, inner), BF), shape((n, PAIR)), shape((n, PAIR)),
        ],
        scratch_shapes=[
            pltpu.VMEM((n, d), BF), pltpu.VMEM(aw.shape, BF), pltpu.VMEM(w.shape, BF),
            pltpu.VMEM((n, PAIR), F32), pltpu.VMEM((n, PAIR), F32), pltpu.VMEM((n, d), BF),
            pltpu.VMEM((d, n), BF), pltpu.SemaphoreType.DMA((6,)),
        ],
        compiler_params=params(24),
        cost_estimate=cost(5),
    )(lens, *hbm(tok), cond, *hbm(aw), ab, gain, *hbm(w, *tables))


def attend_kernel(
    lens, q_ref, k_ref, v_ref, w_ref, attfar_ref, linvfar_ref, efar_ref, out_ref,
    vx, att, linv, es, sems, *, first_row,
):
    n = ROW_LEN
    pairs = vx.shape[0]
    _, masks = head_masks()
    low = masks[0] > 0.5
    segments = [place_of(lens, i * BLOCK)[0] for i in range(n // BLOCK)]
    biases = [
        jnp.concatenate(
            [
                jnp.full((1, BLOCK), jnp.where(here == there, 0.0, masked_score), F32)
                for there in segments
            ],
            axis=1,
        )
        for here in segments[first_row // BLOCK : (first_row + HALF) // BLOCK]
    ]
    for p in range(pairs):
        vx[p, :, 0:PAIR] = v_ref[:, p * PAIR : (p + 1) * PAIR]
        vx[p, :, PAIR:] = jnp.ones((n, PAIR), BF)
    per = RB // BLOCK
    copies = []

    def leave(source, target):
        copies.append(pltpu.make_async_copy(source, target, sems.at[len(copies)]))
        copies[-1].start()

    for step in range(STEPS):
        rows = slice(step * RB, (step + 1) * RB)
        for p in range(pairs):
            cols = slice(p * PAIR, (p + 1) * PAIR)
            q = q_ref[first_row + step * RB : first_row + (step + 1) * RB, cols].astype(F32)
            keys = k_ref[:, cols]
            outs = []
            for h in range(2):
                s = mm((q * masks[h]).astype(BF), keys, NT)
                s = jnp.concatenate(
                    [
                        s[b * BLOCK : (b + 1) * BLOCK] + biases[step * per + b]
                        for b in range(per)
                    ],
                    axis=0,
                )
                peak = jnp.max(s, axis=1, keepdims=True)
                e = jnp.exp(s - peak).astype(BF)
                es[step * pairs + p, h] = e
                outs.append(mm(e, vx[p]))
            leave(es.at[step * pairs + p], efar_ref.at[step * pairs + p])
            inverse = 1.0 / jnp.where(low, outs[0][:, PAIR:], outs[1][:, PAIR:])
            att[rows, cols] = (
                jnp.where(low, outs[0][:, :PAIR], outs[1][:, :PAIR]) * inverse
            ).astype(BF)
            linv[rows, cols] = inverse
        leave(att.at[rows], attfar_ref.at[rows])
        leave(linv.at[rows], linvfar_ref.at[rows])
        out_ref[rows, :] = mm(att[rows, :], w_ref[...]).astype(BF)
    for copy in copies:
        copy.wait()


def attend(half, lens, q, k, v, w):
    n, inner = q.shape
    d = w.shape[1]
    pairs = inner // PAIR
    parts = STEPS * pairs
    return pl.pallas_call(
        functools.partial(attend_kernel, first_row=half * HALF),
        in_specs=[SMEM, VMEM, VMEM, VMEM, VMEM],
        out_specs=[FAR, FAR, FAR, VMEM],
        out_shape=[
            pltpu.HBM((HALF, inner), BF), pltpu.HBM((HALF, inner), F32),
            pltpu.HBM((parts, 2, RB, n), BF), shape((HALF, d), BF),
        ],
        scratch_shapes=[
            pltpu.VMEM((pairs, n, 2 * PAIR), BF), pltpu.VMEM((HALF, inner), BF),
            pltpu.VMEM((HALF, inner), F32), pltpu.VMEM((parts, 2, RB, n), BF),
            pltpu.SemaphoreType.DMA((parts + 2 * STEPS,)),
        ],
        compiler_params=params(20),
        cost_estimate=cost(8),
    )(lens, q, k, v, w)


def attend_back_kernel(
    q_ref, k_ref, v_ref, attfar_ref, linvfar_ref, do_ref, efar_ref, cos_ref, sin_ref, *refs, last
):
    n = ROW_LEN
    if last:
        dk0_ref, dv0_ref, dq_ref, dkout_ref, dvout_ref, vx, km, ds, att, linv, es, sems, dk, dv = refs
    else:
        dq_ref, dk, dv, vx, km, ds, att, linv, es, sems = refs
    pairs = vx.shape[0]
    first, masks = head_masks()
    parts = STEPS * pairs
    copies = [
        pltpu.make_async_copy(attfar_ref, att, sems.at[parts]),
        pltpu.make_async_copy(linvfar_ref, linv, sems.at[parts + 1]),
    ] + [
        pltpu.make_async_copy(efar_ref.at[i], es.at[i], sems.at[i]) for i in range(parts)
    ]
    for copy in copies:
        copy.start()
    for p in range(pairs):
        cols = slice(p * PAIR, (p + 1) * PAIR)
        vx[p, :, 0:PAIR] = v_ref[:, cols]
        vx[p, :, PAIR:] = jnp.ones((n, PAIR), BF)
        keys = k_ref[:, cols].astype(F32)
        for h in range(2):
            km[p, h] = (keys * masks[h]).astype(BF)

    def rotate_back(u, rows):
        w = u * sin_ref[rows, :]
        turned = jnp.where(
            first, pltpu.roll(w, PAIR - HD // 2, 1), -pltpu.roll(w, HD // 2, 1)
        )
        return u * cos_ref[rows, :] + turned

    copies[0].wait()
    copies[1].wait()
    for step in range(STEPS):
        here = slice(step * RB, (step + 1) * RB)
        start = (HALF if last else 0) + step * RB
        rows = slice(start, start + RB)
        for p in range(pairs):
            part = step * pairs + p
            cols = slice(p * PAIR, (p + 1) * PAIR)
            dof = do_ref[here, cols].astype(F32) * linv[here, cols]
            dd = dof * att[here, cols].astype(F32)
            qf = q_ref[rows, cols].astype(F32)
            qs, dms, dq = [], [], None
            copies[2 + part].wait()
            for h in range(2):
                dm = (dof * masks[h]).astype(BF)
                left = jnp.concatenate([dm, (-dd * masks[h]).astype(BF)], axis=1)
                dp = mm(left, vx[p], NT)
                sg = (dp * es[part, h].astype(F32)).astype(BF)
                ds[h * RB : (h + 1) * RB, :] = sg
                term = mm(sg, km[p, h])
                dq = term if dq is None else dq + term
                qs.append((qf * masks[h]).astype(BF))
                dms.append(dm)
            dq_ref[here, cols] = (rotate_back(dq, rows) * (HD**-0.5)).astype(BF)
            a = mm(jnp.concatenate(qs, axis=0).T, ds[...])
            b = mm(jnp.concatenate(dms, axis=0).T, es[part].reshape(2 * RB, n))
            if step == 0:
                dk[p] = dk0_ref[p] + a if last else a
                dv[p] = dv0_ref[p] + b if last else b
            else:
                dk[p] += a
                dv[p] += b
    if last:
        for p in range(pairs):
            cols = slice(p * PAIR, (p + 1) * PAIR)
            dkout_ref[:, cols] = rotate_back(dk[p].T, slice(None)).astype(BF)
            dvout_ref[:, cols] = dv[p].T.astype(BF)


def attend_back(half, q, k, v, att, linv, e, do, cos, sin, before=()):
    n, inner = q.shape
    pairs = inner // PAIR
    last = half == 1
    sums = [pltpu.VMEM((pairs, PAIR, n), F32)] * 2
    return pl.pallas_call(
        functools.partial(attend_back_kernel, last=last),
        in_specs=[VMEM, VMEM, VMEM, FAR, FAR, VMEM, FAR, VMEM, VMEM] + [VMEM] * len(before),
        out_specs=[VMEM] * 3,
        out_shape=[shape((HALF, inner), BF)]
        + ([shape((n, inner), BF)] * 2 if last else [shape((pairs, PAIR, n))] * 2),
        scratch_shapes=[
            pltpu.VMEM((pairs, n, 2 * PAIR), BF),
            pltpu.VMEM((pairs, 2, n, PAIR), BF),
            pltpu.VMEM((2 * RB, n), BF),
            pltpu.VMEM((HALF, inner), BF),
            pltpu.VMEM((HALF, inner), F32),
            pltpu.VMEM(e.shape, BF),
            pltpu.SemaphoreType.DMA((e.shape[0] + 2,)),
        ]
        + (sums if last else []),
        compiler_params=params(28),
        cost_estimate=cost(30),
    )(q, k, v, *hbm(att, linv), do, *hbm(e), cos, sin, *before)


def feed_kernel(
    lens, tok_ref, own_ref, got_ref, cot_ref, mod_ref, gain_ref, ub_ref, up_ref, down_ref,
    middle_ref, fin_t_ref, act_ref, ug_ref, fg_t_ref, fo_ref, fng_ref, ubg_ref, sums_ref,
    *, first_row,
):
    i = pl.program_id(0)
    rows = pl.ds(pl.multiple_of(i * RB, RB), RB)
    mod = mod_ref[...]
    branch = own_ref[rows, :].astype(F32) + got_ref[...].astype(F32)
    middle = tok_ref[...].astype(F32) + mod[2:3] * branch
    middle_ref[rows, :] = middle
    xhat, _ = normalize(middle)
    fin = (xhat * (gain_ref[...].astype(F32) * (1.0 + mod[4:5])) + mod[3:4]).astype(BF)
    fin_t_ref[:, rows] = fin.T
    seed = cot_ref[...].astype(F32) * live_rows(total_of(lens), first_row + i * RB, RB)
    fg = (mod[5:6] * seed).astype(BF)
    fg_t_ref[:, rows] = fg.T
    u = mm(fin, up_ref[...]) + ub_ref[...].astype(F32)
    u2 = u * u
    t = jnp.tanh(u * (gelu_k + (gelu_k * gelu_c) * u2))
    half = 0.5 * (1.0 + t)
    act = (u * half).astype(BF)
    act_ref[rows, :] = act
    slope = half + (0.5 * u) * (1.0 - t * t) * (gelu_k + (3.0 * gelu_k * gelu_c) * u2)
    ugf = mm(fg, down_ref[...], NT) * slope
    ug = ugf.astype(BF)
    ug_ref[rows, :] = ug
    fng_ref[rows, :] = mm(ug, up_ref[...], NT).astype(BF)
    fo = mm(act, down_ref[...])
    fo_ref[rows, :] = fo.astype(BF)
    ubs = jnp.sum(ugf, axis=0, keepdims=True)
    sums = jnp.concatenate(
        [jnp.sum(seed, axis=0, keepdims=True), jnp.sum(seed * fo, axis=0, keepdims=True)], axis=0
    )

    @pl.when(i == 0)
    def _():
        ubg_ref[...] = ubs
        sums_ref[...] = sums

    @pl.when(i > 0)
    def _():
        ubg_ref[...] += ubs
        sums_ref[...] += sums


def feed(half, lens, tok, own, got, cot, mod, gain, ub, up, down):
    d, f = up.shape
    here = rows_of(d, half * STEPS)
    return pl.pallas_call(
        functools.partial(feed_kernel, first_row=half * HALF),
        grid=(STEPS,),
        in_specs=[
            SMEM, here, VMEM, rows_of(d), here, VMEM, VMEM, VMEM, VMEM, VMEM,
        ],
        out_specs=[VMEM] * 9,
        out_shape=[
            shape((HALF, d)), shape((d, HALF), BF), shape((HALF, f), BF),
            shape((HALF, f), BF), shape((d, HALF), BF), shape((HALF, d), BF),
            shape((HALF, d), BF), shape((1, f)), shape((2, d)),
        ],
        compiler_params=params(16),
        cost_estimate=cost(9),
    )(lens, *hbm(tok), own, got, *hbm(cot), mod, gain, ub, up, down)


def middle_kernel(
    lens, middle_ref, own_ref, got_ref, cot_ref, bown_ref, bgot_ref, mod_ref, gain_ref, w_ref,
    mg_ref, bg_t_ref, do_ref, sums_ref, *, first_row,
):
    i = pl.program_id(0)
    rows = pl.ds(pl.multiple_of(i * RB, RB), RB)
    mod = mod_ref[...]
    xhat, inverse = normalize(middle_ref[rows, :])
    c = own_ref[rows, :].astype(F32) + got_ref[...].astype(F32)
    seed = cot_ref[...].astype(F32) * live_rows(total_of(lens), first_row + i * RB, RB)
    mg = seed + norm_pull(c, xhat, inverse, gain_ref[...].astype(F32) * (1.0 + mod[4:5]))
    mg_ref[...] = mg
    bg = (mod[2:3] * mg).astype(BF)
    bg_t_ref[:, rows] = bg.T
    do_ref[rows, :] = mm(bg, w_ref[...], NT).astype(BF)
    branch = bown_ref[rows, :].astype(F32) + bgot_ref[...].astype(F32)
    sums = jnp.concatenate(
        [
            jnp.sum(mg * branch, axis=0, keepdims=True),
            jnp.sum(c, axis=0, keepdims=True),
            jnp.sum(c * xhat, axis=0, keepdims=True),
        ],
        axis=0,
    )

    @pl.when(i == 0)
    def _():
        sums_ref[...] = sums

    @pl.when(i > 0)
    def _():
        sums_ref[...] += sums


def middle_back(half, lens, middle, own, got, cot, bown, bgot, mod, gain, w):
    inner, d = w.shape
    return pl.pallas_call(
        functools.partial(middle_kernel, first_row=half * HALF),
        grid=(STEPS,),
        in_specs=[
            SMEM, VMEM, VMEM, rows_of(d), rows_of(d, half * STEPS), VMEM, rows_of(d), VMEM, VMEM,
            VMEM,
        ],
        out_specs=[rows_of(d), VMEM, VMEM, VMEM],
        out_shape=[
            pltpu.HBM((HALF, d), F32), shape((d, HALF), BF), shape((HALF, inner), BF), shape((3, d)),
        ],
        compiler_params=params(14),
        cost_estimate=cost(40),
    )(lens, middle, own, got, *hbm(cot), bown, bgot, mod, gain, w)


def weight_grad_kernel(starts, *refs, ins, plan, outs, blocks, chunk):
    out, g = refs[ins : ins + outs], refs[ins + outs]
    j = pl.program_id(0)
    begin = 0
    for chunks, parts in plan:

        @pl.when((j >= begin) & (j < begin + chunks))
        def _(parts=parts, begin=begin):
            cols = pl.ds(pl.multiple_of((j - begin) * chunk, 128), chunk)
            total = None
            for left, column, part in parts:
                size = refs[part].shape[0]
                term = mm(refs[left][:, column : column + size], refs[part][:, cols])
                total = term if total is None else total + term
            g[...] = total

        begin += chunks
    size = out[0].shape[1]
    cols = pl.ds(pl.multiple_of(j * chunk, 128), chunk)
    for k in range(outs):
        for m in range(blocks):
            rows = pl.ds(pl.multiple_of(starts[k * blocks + m], 16), size)
            out[k][m, :, cols] = g[rows, :].astype(BF)


def weight_grad(couples, starts, outs, blocks, size, chunk):
    ins, specs, plan, begin = [], [], [], 0
    for lefts, rights in couples:
        columns = []
        for part in lefts:
            columns += [(len(ins), i) for i in range(0, part.shape[1], HALF)]
            ins.append(part)
            specs.append(VMEM)
        for parts in rights:
            chunks = parts[0].shape[1] // chunk
            entries, row = [], 0
            for part in parts:
                left, column = columns[row // HALF]
                entries.append((left, column, len(ins)))
                row += part.shape[0]
                ins.append(part)
                specs.append(VMEM)
            plan.append((chunks, entries))
            begin += chunks
    d = couples[0][0][0].shape[0]
    return pl.pallas_call(
        functools.partial(
            weight_grad_kernel, ins=len(ins), plan=plan, outs=outs, blocks=blocks, chunk=chunk
        ),
        grid=(begin,),
        in_specs=[SMEM] + specs,
        out_specs=[VMEM] * outs,
        out_shape=[shape((blocks, size, begin * chunk), BF)] * outs,
        scratch_shapes=[pltpu.VMEM((d, chunk), F32)],
        compiler_params=params(12),
        cost_estimate=cost(4),
    )(starts, *ins)


def mix_kernel(side, m0_ref, m1_ref, f0_ref, f1_ref, got_ref, mod_ref, bias_ref, out_ref):
    second = side[0] == 1
    own = jnp.where(second, f1_ref[...], f0_ref[...])
    fo = own.astype(F32) + got_ref[...].astype(F32) + bias_ref[...].astype(F32)
    middle = jnp.where(second, m1_ref[...], m0_ref[...])
    out_ref[...] = (middle + mod_ref[5:6] * fo).astype(BF)


def here_rows(width):
    return pl.BlockSpec((RB, width), lambda i, side: (side[0] * STEPS + i, 0))


def mix(side, middles, outs, got, mod, bias):
    d = got.shape[1]
    return pl.pallas_call(
        mix_kernel,
        grid_spec=pltpu.PrefetchScalarGridSpec(
            num_scalar_prefetch=1,
            grid=(STEPS,),
            in_specs=[rows_of(d)] * 5 + [VMEM, VMEM],
            out_specs=rows_of(d),
        ),
        out_shape=shape((HALF, d), BF),
        compiler_params=params(16),
        cost_estimate=cost(1),
    )(side, *hbm(*middles, *outs), got, mod, bias)


def input_back_kernel(side, q0_ref, q1_ref, k_ref, v_ref, w_ref, out_ref, *, mine):
    second = (side[0] == 1) if mine else (side[0] == 0)
    here = pl.ds(pl.multiple_of(pl.program_id(0) * RB, RB), RB)
    dq = jnp.where(second, q1_ref[here, :], q0_ref[here, :])
    start = (side[0] if mine else 1 - side[0]) * HALF + pl.program_id(0) * RB
    rows = pl.ds(pl.multiple_of(start, RB), RB)
    total = mm(dq, w_ref[0], NT)
    total += mm(k_ref[rows, :], w_ref[1], NT)
    total += mm(v_ref[rows, :], w_ref[2], NT)
    out_ref[here, :] = total.astype(out_ref.dtype)


def input_back(side, dqs, dk, dv, w, mine, kind):
    _, d, inner = w.shape
    return pl.pallas_call(
        functools.partial(input_back_kernel, mine=mine),
        grid_spec=pltpu.PrefetchScalarGridSpec(
            num_scalar_prefetch=1,
            grid=(STEPS,),
            in_specs=[VMEM] * 5,
            out_specs=VMEM,
        ),
        out_shape=shape((HALF, d), kind),
        compiler_params=params(24),
        cost_estimate=cost(1),
    )(side, *dqs, dk, dv, w)


def final_kernel(side, tok_ref, own_ref, got_ref, mg0_ref, mg1_ref, mod_ref, gain_ref, out_ref, sums_ref):
    i = pl.program_id(0)
    xhat, inverse = normalize(tok_ref[...].astype(F32))
    c = own_ref[...] + got_ref[...].astype(F32)
    mg = jnp.where(side[0] == 1, mg1_ref[...], mg0_ref[...])
    out_ref[...] = mg + norm_pull(c, xhat, inverse, gain_ref[...].astype(F32) * (1.0 + mod_ref[1:2]))
    sums = jnp.concatenate(
        [jnp.sum(c, axis=0, keepdims=True), jnp.sum(c * xhat, axis=0, keepdims=True)], axis=0
    )

    @pl.when(i == 0)
    def _():
        sums_ref[...] = sums

    @pl.when(i > 0)
    def _():
        sums_ref[...] += sums


def final(side, tok, own, got, mgs, mod, gain):
    d = tok.shape[1]
    return pl.pallas_call(
        final_kernel,
        grid_spec=pltpu.PrefetchScalarGridSpec(
            num_scalar_prefetch=1,
            grid=(STEPS,),
            in_specs=[here_rows(d)] + [rows_of(d)] * 4 + [whole(6, d), whole(1, d)],
            out_specs=[rows_of(d), constant(2, d)],
        ),
        out_shape=[shape((HALF, d)), shape((2, d))],
        compiler_params=params(24),
        cost_estimate=cost(1),
    )(side, *hbm(tok), own, got, *hbm(*mgs), mod, gain)


def collect_kernel(
    half_ref, got_ref, mid0_ref, mid1_ref, seed0_ref, seed1_ref, mod_ref, ga_ref, gf_ref, db_ref,
    cond_ref, u0_ref, u1_ref, out_ref, all_ref,
):
    half = half_ref[...] + got_ref[...]
    mid = mid0_ref[...] + mid1_ref[...]
    seeds = seed0_ref[0:1, :] + seed1_ref[0:1, :]
    d = half.shape[1]
    s_att, s_feed = half[1:2], mid[2:3]
    all_ref[...] = jnp.zeros_like(all_ref)
    all_ref[0:1, : cond_ref.shape[1]] = cond_ref[...].astype(F32)
    rows = (
        half[0:1], s_att * ga_ref[...].astype(F32), mid[0:1], mid[1:2],
        s_feed * gf_ref[...].astype(F32), half[2:3] + seeds * db_ref[...].astype(F32),
        (1.0 + mod_ref[1:2]) * s_att, (1.0 + mod_ref[4:5]) * s_feed, mod_ref[5:6] * seeds,
    )
    for i, row in enumerate(rows):
        all_ref[i + 1 : i + 2, :] = row
    for i in range(u0_ref.shape[1] // d):
        cols = slice(i * d, (i + 1) * d)
        all_ref[10 + i : 11 + i, :] = u0_ref[:, cols] + u1_ref[:, cols]
    out_ref[...] = all_ref[...].astype(BF)


def collect(half, got, mids, seeds, mod, ga, gf, db, cond, ubs):
    d = half.shape[1]
    rows = -(-(10 + ubs[0].shape[1] // d) // 16) * 16
    return pl.pallas_call(
        collect_kernel,
        in_specs=[VMEM] * 13,
        out_specs=VMEM,
        out_shape=shape((rows, d), BF),
        scratch_shapes=[pltpu.VMEM((rows, d), F32)],
        compiler_params=params(4),
        cost_estimate=cost(1),
    )(half, got, *mids, *seeds, mod, ga, gf, db, cond, *ubs)


def finish_kernel(every_ref, weight_ref, bias_ref, sums_ref):
    d = every_ref.shape[2]
    cond = every_ref[:, 0, :]
    for j in range(6):
        rows = every_ref[:, 1 + j, :]
        weight_ref[:, j * d : (j + 1) * d] = mm(cond[:, : weight_ref.shape[0]], rows, TN)
        bias_ref[j : j + 1, :] = jnp.sum(rows.astype(F32), axis=0, keepdims=True)
    sums_ref[...] = jnp.zeros_like(sums_ref)
    for j in range(every_ref.shape[1] - 7):
        rows = every_ref[:, 7 + j, :].astype(F32)
        sums_ref[j : j + 1, :] = jnp.sum(rows, axis=0, keepdims=True)


def finish(every, cond_dim):
    rows, kinds, d = every.shape
    return pl.pallas_call(
        finish_kernel,
        in_specs=[VMEM],
        out_specs=[VMEM] * 3,
        out_shape=[shape((cond_dim, 6 * d)), shape((6, d)), shape((kinds, d))],
        compiler_params=params(12),
        cost_estimate=cost(2),
    )(every)


def together(*values):
    return lax.optimization_barrier(values)


def perm(dp_size, move):
    pairs = []
    for index in range(dp_size):
        for y in range(2):
            to = move(index >> 2, (index >> 1) & 1, y, index & 1)
            pairs.append((index * 2 + y, ((to[0] * 2 + to[1]) * 2 + to[3]) * 2 + to[2]))
    return pairs


def xor_order(stack, me, bits):
    for b in range(bits):
        shaped = stack.reshape((-1, 2, 1 << b) + stack.shape[1:])
        flipped = jnp.concatenate([shaped[:, 1:], shaped[:, :1]], axis=1)
        stack = jnp.where(((me >> b) & 1) == 1, flipped, shaped).reshape(stack.shape)
    return stack


def per_device(
    tokens,
    conditioning,
    lengths,
    input_weight,
    output_weight,
    up_weight,
    up_bias,
    down_weight,
    down_bias,
    attention_gain,
    feed_gain,
    adaptive_weight,
    adaptive_bias,
    cotangent,
):
    n, d = tokens.shape
    assert lengths.shape[0] == 1
    inner = input_weight.shape[2]
    f = up_weight.shape[1]
    dp_size = lax.axis_size("dp")
    planes = dp_size // 4
    zbits = planes.bit_length() - 1
    index = lax.axis_index("dp")
    y = lax.axis_index("tensor")
    c = index % 2
    x = (index // 2) % 2
    z = index // 4
    side = y.astype(jnp.int32).reshape(1)

    make = functools.partial(perm, dp_size)
    y_swap = make(lambda z, x, y, c: (z, x, 1 - y, c))
    core_swap = make(lambda z, x, y, c: (z, x, y, 1 - c))
    x_swap = make(lambda z, x, y, c: (z, 1 - x, y, c))

    def send(value, how):
        return lax.ppermute(value, AXES, how)

    gain_a = attention_gain.reshape(1, d)
    gain_f = feed_gain.reshape(1, d)
    up_b = up_bias.reshape(1, f)

    mod, normed_t, q, k, v, cosine, sine = project(
        lengths, tokens, conditioning, adaptive_weight, adaptive_bias, attention_gain,
        input_weight,
    )
    halves = (0, 1)
    att, linv, e, branch, branch_got = [], [], [], [], []
    for h in halves:
        got = attend(h, lengths, q, k, v, output_weight)
        for store, value in zip((att, linv, e, branch), got):
            store.append(value)
        if h == 0:
            branch[0], k = together(branch[0], k)
        branch_got.append(send(branch[h], y_swap))
    fed, fng_got = [], []
    for h in halves:
        fed.append(
            feed(
                h, lengths, tokens, branch[h], branch_got[h], cotangent, mod, gain_f, up_b,
                up_weight, down_weight,
            )
        )
        fng_sent = fed[h][6]
        if h == 0:
            fng_sent, branch_got[1] = together(fng_sent, branch_got[1])
        fng_got.append(send(fng_sent, y_swap))
    middle, fin_t, act, ug, fg_t, fo, fng, ubg, seed_sums = zip(*fed)

    r_out = d // dp_size

    def cut(couples, chunk):
        if r_out % 16 == 0:
            place = [
                (((z ^ m) * 2 + (x ^ dx)) * 2 + (c ^ s)) * r_out
                for s in range(2)
                for dx in range(2)
                for m in range(planes)
            ]
            starts = jnp.stack([p.astype(jnp.int32) for p in place])
            outs = weight_grad(couples, starts, 2, 2 * planes, r_out, chunk)
        else:
            grad = jnp.concatenate(
                [
                    mm(jnp.concatenate(a, axis=1), jnp.concatenate(b)).astype(BF)
                    for a, bs in couples
                    for b in bs
                ],
                axis=1,
            )
            blocks = grad.reshape(planes, 2, 2, r_out, grad.shape[1])
            blocks = xor_order(blocks, z, zbits).transpose(2, 1, 0, 3, 4)
            blocks = xor_order(blocks, c, 1)
            outs = [xor_order(b, x, 1) for b in blocks]
        return [o.reshape(2, planes, r_out, -1) for o in outs]

    def send_z(total):
        return [
            send(total[m].astype(BF), make(lambda z, x, y, c: (z ^ m, x, y, c)))
            for m in range(1, planes)
        ]

    def sum_z(total, got):
        return sum((v.astype(F32) for v in got), total[0])

    feed_own, feed_far = cut([(fg_t, [act]), (fin_t, [ug])], f // 2)
    feed_core_got = send(feed_far, core_swap)
    fng_got[0], feed_own = together(fng_got[0], feed_own)

    mids, backs = [], []
    for h in halves:
        mids.append(
            middle_back(
                h, lengths, middle[h], fng[h], fng_got[h], cotangent, branch[h], branch_got[h],
                mod, gain_f, output_weight,
            )
        )
        if h == 0:
            feed_core_got, do = together(feed_core_got, mids[0][2])
            feed_near = feed_own[0].astype(F32) + feed_core_got[0].astype(F32)
            feed_far = (feed_own[1].astype(F32) + feed_core_got[1].astype(F32)).astype(BF)
            do, feed_far = together(do, feed_far)
            feed_x_got = send(feed_far, x_swap)
        else:
            do = mids[1][2]
        backs.append(
            attend_back(
                h, q, k, v, att[h], linv[h], e[h], do, cosine, sine, backs[0][1:] if h else ()
            )
        )
        if h == 0:
            fng_got[1], fo_sent, _ = together(
                fng_got[1], jnp.where(y == 0, fo[1], fo[0]), backs[0][0]
            )
            fo_got = send(fo_sent, y_swap)
    mg, bg_t, _, mid_sums = zip(*mids)
    dqs, (dk, dv) = (backs[0][0], backs[1][0]), backs[1][1:]

    ang_other = input_back(side, dqs, dk, dv, input_weight, False, BF)
    dk, ang_other, fo_got = together(dk, ang_other, fo_got)
    ang_got = send(ang_other, y_swap)
    attn_own, attn_far = cut([(bg_t, [att]), ([normed_t], [dqs, [dk], [dv]])], inner)
    attn_core_got = send(attn_far, core_swap)
    dk, feed_x_got, attn_own = together(dk, feed_x_got, attn_own)
    feed_total = feed_near + feed_x_got.astype(F32)
    feed_total, attn_core_got = together(feed_total, attn_core_got)
    feed_z_got = send_z(feed_total)
    attn_near = attn_own[0].astype(F32) + attn_core_got[0].astype(F32)
    attn_far = (attn_own[1].astype(F32) + attn_core_got[1].astype(F32)).astype(BF)
    attn_far, dk = together(attn_far, dk)
    attn_x_got = send(attn_far, x_swap)
    ang_own = input_back(side, dqs, dk, dv, input_weight, True, F32)
    tok_grad, att_sums = final(side, tokens, ang_own, ang_got, mg, mod, gain_a)

    half_sums = jnp.concatenate([att_sums, seed_sums[0][1:] + seed_sums[1][1:]], axis=0)
    flat = collect(
        half_sums, send(half_sums, y_swap), mid_sums, seed_sums, mod, gain_a, gain_f,
        down_bias.reshape(1, d), conditioning, ubg,
    )
    flat, attn_x_got, fo_got = together(flat, attn_x_got, fo_got)
    every = lax.all_to_all(
        jnp.broadcast_to(flat[None], (dp_size,) + flat.shape), "dp", 0, 0, tiled=True
    )
    attn_total = attn_near + attn_x_got.astype(F32)
    attn_z_got = send_z(attn_total)
    mixed = mix(side, middle, fo, fo_got, mod, down_bias.reshape(1, d))
    mixed, *feed_z_got = together(mixed, *feed_z_got)
    feed_grads = sum_z(feed_total, feed_z_got)
    down_grad, up_grad = feed_grads[:, :f], feed_grads[:, f:]
    attn_grads = sum_z(attn_total, attn_z_got)
    out_grad, in_grad = attn_grads[:, :inner], attn_grads[:, inner:]
    adaptive_weight_grad, adaptive_bias_grad, sums = finish(
        every.reshape(dp_size, flat.shape[0], d), conditioning.shape[1]
    )
    return (
        mixed,
        tok_grad,
        in_grad.reshape(r_out, 3, inner).transpose(1, 0, 2),
        out_grad.T,
        up_grad,
        sums[3 : 3 + f // d].reshape(f),
        down_grad.T,
        sums[2],
        sums[0],
        sums[1],
        adaptive_weight_grad,
        adaptive_bias_grad.reshape(-1),
    )


def solution(mesh):
    placed = (
        P("dp", None),
        P("dp", None),
        P("dp", None),
        P(None, None, "tensor"),
        P("tensor", None),
        P(None, "tensor"),
        P("tensor"),
        P("tensor", None),
        P(),
        P(),
        P(),
        P(),
        P(),
        P("dp", None),
    )
    return jax.shard_map(
        per_device,
        mesh=mesh,
        in_specs=placed,
        out_specs=(
            P(("dp", "tensor"), None),
            P(("dp", "tensor"), None),
            P(None, "dp", "tensor"),
            P("tensor", "dp"),
            P("dp", "tensor"),
            P("tensor"),
            P("tensor", "dp"),
            P(),
            P(),
            P(),
            P(),
            P(),
        ),
        check_vma=False,
    )
```

```python
import functools

import jax
import jax.numpy as jnp
import numpy as np
from jax import lax
from jax.experimental import pallas as pl
from jax.experimental.pallas import tpu as pltpu
from jax.sharding import PartitionSpec as P

HD = 64
ROW_LEN = 1024
NSEG = 8
BLOCK = 128
PAIR = 2 * HD
RB = 256
HALF = ROW_LEN // 2
STEPS = HALF // RB

norm_eps = 1e-05
masked_score = -1000000000.0
rotary_base = 10000.0
gelu_k = 0.7978845608028654
gelu_c = 0.044715

AXES = ("dp", "tensor")
BF = jnp.bfloat16
F32 = jnp.float32
NN = ((1,), (0,))
NT = ((1,), (1,))
TN = ((0,), (0,))
VMEM = pl.BlockSpec(memory_space=pltpu.VMEM)
SMEM = pl.BlockSpec(memory_space=pltpu.SMEM)
FAR = pl.BlockSpec(memory_space=pltpu.HBM)


def mm(left, right, dims=NN):
    return lax.dot_general(left, right, (dims, ((), ())), preferred_element_type=F32)


def params(mib):
    return pltpu.CompilerParams(vmem_limit_bytes=mib << 20)


def cost(us):
    return pl.CostEstimate(flops=int(us * 1.15e9), bytes_accessed=0, transcendentals=0)


def shape(dims, kind=F32):
    return jax.ShapeDtypeStruct(dims, kind)


def hbm(*values):
    return [pltpu.with_memory_space_constraint(v, pltpu.HBM) for v in values]


def normalize(values):
    centered = values - jnp.mean(values, axis=-1, keepdims=True)
    inverse = lax.rsqrt(jnp.mean(centered * centered, axis=-1, keepdims=True) + norm_eps)
    return centered * inverse, inverse


def norm_pull(cotangent, xhat, inverse, weight):
    e = cotangent * weight
    return inverse * (
        e
        - jnp.mean(e, axis=-1, keepdims=True)
        - xhat * jnp.mean(e * xhat, axis=-1, keepdims=True)
    )


def live_rows(total, first_row, rows):
    slots = lax.broadcasted_iota(jnp.int32, (rows, 1), 0) + first_row
    return (slots < total).astype(F32)


def rows_of(width, offset=0):
    return pl.BlockSpec((RB, width), lambda i, *_: (i + offset, 0))


def turned_rows(width):
    return pl.BlockSpec((width, RB), lambda i, *_: (0, i))


def whole(*dims):
    return pl.BlockSpec(dims, lambda *_: (0,) * len(dims), pipeline_mode=pl.Buffered(1))


def constant(*dims):
    return pl.BlockSpec(dims, lambda *_: (0,) * len(dims))


def head_masks():
    lane = lax.broadcasted_iota(jnp.int32, (1, PAIR), 1)
    low = (lane < HD).astype(F32)
    return (lane % HD) < HD // 2, (low, 1.0 - low)


def rotary_tables():
    lanes = np.arange(PAIR) % (HD // 2)
    frequency = (rotary_base ** (-lanes * (2.0 / HD))).astype(np.float32)
    angles = np.arange(ROW_LEN, dtype=np.float32)[:, None] * frequency[None, :]
    return np.cos(angles), np.sin(angles)


def place_of(lens, slot):
    segment, start, bound = 0, 0, 0
    for j in range(NSEG):
        bound = bound + lens[0, j]
        passed = bound <= slot
        segment = segment + jnp.where(passed, 1, 0)
        start = start + jnp.where(passed, lens[0, j], 0)
    return segment, start


def total_of(lens):
    total = lens[0, 0]
    for j in range(1, NSEG):
        total = total + lens[0, j]
    return total


def project_kernel(
    lens, tokfar_ref, condfar_ref, awfar_ref, abfar_ref, gainfar_ref, wfar_ref, cosfar_ref,
    sinfar_ref,
    mod_ref, turnedfar_ref, q_ref, k_ref, v_ref, cos_ref, sin_ref,
    tok, aw, w, cos_table, sin_table, normed, turned, cond_ref, ab_ref, gain_ref, sems,
):
    n, d = tok.shape
    pairs = k_ref.shape[1] // PAIR
    copies = [
        pltpu.make_async_copy(source, target, sems.at[i])
        for i, (source, target) in enumerate(
            (
                (awfar_ref, aw), (tokfar_ref, tok), (wfar_ref, w), (cosfar_ref, cos_table),
                (sinfar_ref, sin_table), (turned, turnedfar_ref), (condfar_ref, cond_ref),
                (abfar_ref, ab_ref), (gainfar_ref, gain_ref),
            )
        )
    ]
    for copy in copies[6:] + copies[:5]:
        copy.start()
    for copy in copies[6:] + copies[:1]:
        copy.wait()
    cond = jnp.broadcast_to(cond_ref[...], (8, cond_ref.shape[1]))
    row = mm(cond, aw[...])[0:1] + ab_ref[...].astype(F32).reshape(1, 6 * d)
    for j in range(6):
        mod_ref[j : j + 1, :] = row[:, j * d : (j + 1) * d]
    weight = gain_ref[...].astype(F32).reshape(1, d) * (1.0 + row[:, d : 2 * d])
    copies[1].wait()
    for i in range(n // RB):
        rows = slice(i * RB, (i + 1) * RB)
        xhat, _ = normalize(tok[rows, :].astype(F32))
        part = (xhat * weight + row[:, :d]).astype(BF)
        normed[rows, :] = part
        turned[:, rows] = part.T
    copies[5].start()
    copies[3].wait()
    copies[4].wait()
    for i in range(n // BLOCK):
        _, start = place_of(lens, i * BLOCK)
        rows = slice(i * BLOCK, (i + 1) * BLOCK)
        at = pl.ds(pl.multiple_of(i * BLOCK - start, BLOCK), BLOCK)
        cos_ref[rows, :] = cos_table[at, :]
        sin_ref[rows, :] = sin_table[at, :]
    copies[2].wait()
    first, _ = head_masks()

    def rotate(u, rows):
        turned_u = jnp.where(
            first, -pltpu.roll(u, PAIR - HD // 2, 1), pltpu.roll(u, HD // 2, 1)
        )
        return u * cos_ref[rows, :] + turned_u * sin_ref[rows, :]

    for i in range(n // HALF):
        rows = slice(i * HALF, (i + 1) * HALF)
        left = normed[rows, :]
        queries, keys, values = (mm(left, w[j]) for j in range(3))
        for p in range(pairs):
            cols = slice(p * PAIR, (p + 1) * PAIR)
            q_ref[rows, cols] = (rotate(queries[:, cols], rows) * (HD**-0.5)).astype(BF)
            k_ref[rows, cols] = rotate(keys[:, cols], rows).astype(BF)
        v_ref[rows, :] = values.astype(BF)
    copies[5].wait()


def project(lens, tok, cond, aw, ab, gain, w):
    n, d = tok.shape
    inner = w.shape[2]
    tables = [jnp.asarray(t) for t in rotary_tables()]
    return pl.pallas_call(
        project_kernel,
        in_specs=[SMEM] + [FAR] * 8,
        out_specs=[VMEM, FAR, VMEM, VMEM, VMEM, VMEM, VMEM],
        out_shape=[
            shape((6, d)), pltpu.HBM((d, n), BF), shape((n, inner), BF), shape((n, inner), BF),
            shape((n, inner), BF), shape((n, PAIR)), shape((n, PAIR)),
        ],
        scratch_shapes=[
            pltpu.VMEM((n, d), BF), pltpu.VMEM(aw.shape, BF), pltpu.VMEM(w.shape, BF),
            pltpu.VMEM((n, PAIR), F32), pltpu.VMEM((n, PAIR), F32), pltpu.VMEM((n, d), BF),
            pltpu.VMEM((d, n), BF), pltpu.VMEM(cond.shape, BF), pltpu.VMEM(ab.shape, BF),
            pltpu.VMEM(gain.shape, BF), pltpu.SemaphoreType.DMA((9,)),
        ],
        compiler_params=params(24),
        cost_estimate=cost(5),
    )(*hbm(lens, tok, cond, aw, ab, gain, w, *tables))


def attend_kernel(
    lens, q_ref, k_ref, v_ref, w_ref, attfar_ref, linvfar_ref, efar_ref, out_ref,
    vx, att, linv, es, sems, *, first_row,
):
    n = ROW_LEN
    pairs = vx.shape[0]
    _, masks = head_masks()
    low = masks[0] > 0.5
    segments = [place_of(lens, i * BLOCK)[0] for i in range(n // BLOCK)]
    biases = [
        jnp.concatenate(
            [
                jnp.full((1, BLOCK), jnp.where(here == there, 0.0, masked_score), F32)
                for there in segments
            ],
            axis=1,
        )
        for here in segments[first_row // BLOCK : (first_row + HALF) // BLOCK]
    ]
    for p in range(pairs):
        vx[p, :, 0:PAIR] = v_ref[:, p * PAIR : (p + 1) * PAIR]
        vx[p, :, PAIR:] = jnp.ones((n, PAIR), BF)
    per = RB // BLOCK
    copies = []

    def leave(source, target):
        copies.append(pltpu.make_async_copy(source, target, sems.at[len(copies)]))
        copies[-1].start()

    for step in range(STEPS):
        rows = slice(step * RB, (step + 1) * RB)
        for p in range(pairs):
            cols = slice(p * PAIR, (p + 1) * PAIR)
            q = q_ref[first_row + step * RB : first_row + (step + 1) * RB, cols].astype(F32)
            keys = k_ref[:, cols]
            outs = []
            for h in range(2):
                s = mm((q * masks[h]).astype(BF), keys, NT)
                s = jnp.concatenate(
                    [
                        s[b * BLOCK : (b + 1) * BLOCK] + biases[step * per + b]
                        for b in range(per)
                    ],
                    axis=0,
                )
                peak = jnp.max(s, axis=1, keepdims=True)
                e = jnp.exp(s - peak).astype(BF)
                es[step * pairs + p, h] = e
                outs.append(mm(e, vx[p]))
            leave(es.at[step * pairs + p], efar_ref.at[step * pairs + p])
            inverse = 1.0 / jnp.where(low, outs[0][:, PAIR:], outs[1][:, PAIR:])
            att[rows, cols] = (
                jnp.where(low, outs[0][:, :PAIR], outs[1][:, :PAIR]) * inverse
            ).astype(BF)
            linv[rows, cols] = inverse
        leave(att.at[rows], attfar_ref.at[rows])
        leave(linv.at[rows], linvfar_ref.at[rows])
        out_ref[rows, :] = mm(att[rows, :], w_ref[...]).astype(BF)
    for copy in copies:
        copy.wait()


def attend(half, lens, q, k, v, w):
    n, inner = q.shape
    d = w.shape[1]
    pairs = inner // PAIR
    parts = STEPS * pairs
    return pl.pallas_call(
        functools.partial(attend_kernel, first_row=half * HALF),
        in_specs=[SMEM, VMEM, VMEM, VMEM, VMEM],
        out_specs=[FAR, FAR, FAR, VMEM],
        out_shape=[
            pltpu.HBM((HALF, inner), BF), pltpu.HBM((HALF, inner), F32),
            pltpu.HBM((parts, 2, RB, n), BF), shape((HALF, d), BF),
        ],
        scratch_shapes=[
            pltpu.VMEM((pairs, n, 2 * PAIR), BF), pltpu.VMEM((HALF, inner), BF),
            pltpu.VMEM((HALF, inner), F32), pltpu.VMEM((parts, 2, RB, n), BF),
            pltpu.SemaphoreType.DMA((parts + 2 * STEPS,)),
        ],
        compiler_params=params(20),
        cost_estimate=cost(8),
    )(lens, q, k, v, w)


def attend_back_kernel(
    q_ref, k_ref, v_ref, attfar_ref, linvfar_ref, do_ref, efar_ref, cos_ref, sin_ref, *refs, last
):
    n = ROW_LEN
    if last:
        dk0_ref, dv0_ref, dq_ref, dkout_ref, dvout_ref, vx, km, ds, att, linv, es, sems, dk, dv = refs
    else:
        dq_ref, dk, dv, vx, km, ds, att, linv, es, sems = refs
    pairs = vx.shape[0]
    first, masks = head_masks()
    parts = STEPS * pairs
    copies = [
        pltpu.make_async_copy(attfar_ref, att, sems.at[parts]),
        pltpu.make_async_copy(linvfar_ref, linv, sems.at[parts + 1]),
    ] + [
        pltpu.make_async_copy(efar_ref.at[i], es.at[i], sems.at[i]) for i in range(parts)
    ]
    for copy in copies:
        copy.start()
    for p in range(pairs):
        cols = slice(p * PAIR, (p + 1) * PAIR)
        vx[p, :, 0:PAIR] = v_ref[:, cols]
        vx[p, :, PAIR:] = jnp.ones((n, PAIR), BF)
        keys = k_ref[:, cols].astype(F32)
        for h in range(2):
            km[p, h] = (keys * masks[h]).astype(BF)

    def rotate_back(u, rows):
        w = u * sin_ref[rows, :]
        turned = jnp.where(
            first, pltpu.roll(w, PAIR - HD // 2, 1), -pltpu.roll(w, HD // 2, 1)
        )
        return u * cos_ref[rows, :] + turned

    copies[0].wait()
    copies[1].wait()
    for step in range(STEPS):
        here = slice(step * RB, (step + 1) * RB)
        start = (HALF if last else 0) + step * RB
        rows = slice(start, start + RB)
        for p in range(pairs):
            part = step * pairs + p
            cols = slice(p * PAIR, (p + 1) * PAIR)
            dof = do_ref[here, cols].astype(F32) * linv[here, cols]
            dd = dof * att[here, cols].astype(F32)
            qf = q_ref[rows, cols].astype(F32)
            qs, dms, dq = [], [], None
            copies[2 + part].wait()
            for h in range(2):
                dm = (dof * masks[h]).astype(BF)
                left = jnp.concatenate([dm, (-dd * masks[h]).astype(BF)], axis=1)
                dp = mm(left, vx[p], NT)
                sg = (dp * es[part, h].astype(F32)).astype(BF)
                ds[h * RB : (h + 1) * RB, :] = sg
                term = mm(sg, km[p, h])
                dq = term if dq is None else dq + term
                qs.append((qf * masks[h]).astype(BF))
                dms.append(dm)
            dq_ref[here, cols] = (rotate_back(dq, rows) * (HD**-0.5)).astype(BF)
            a = mm(jnp.concatenate(qs, axis=0).T, ds[...])
            b = mm(jnp.concatenate(dms, axis=0).T, es[part].reshape(2 * RB, n))
            if step == 0:
                dk[p] = dk0_ref[p] + a if last else a
                dv[p] = dv0_ref[p] + b if last else b
            else:
                dk[p] += a
                dv[p] += b
    if last:
        for p in range(pairs):
            cols = slice(p * PAIR, (p + 1) * PAIR)
            dkout_ref[:, cols] = rotate_back(dk[p].T, slice(None)).astype(BF)
            dvout_ref[:, cols] = dv[p].T.astype(BF)


def attend_back(half, q, k, v, att, linv, e, do, cos, sin, before=()):
    n, inner = q.shape
    pairs = inner // PAIR
    last = half == 1
    sums = [pltpu.VMEM((pairs, PAIR, n), F32)] * 2
    return pl.pallas_call(
        functools.partial(attend_back_kernel, last=last),
        in_specs=[VMEM, VMEM, VMEM, FAR, FAR, VMEM, FAR, VMEM, VMEM] + [VMEM] * len(before),
        out_specs=[VMEM] * 3,
        out_shape=[shape((HALF, inner), BF)]
        + ([shape((n, inner), BF)] * 2 if last else [shape((pairs, PAIR, n))] * 2),
        scratch_shapes=[
            pltpu.VMEM((pairs, n, 2 * PAIR), BF),
            pltpu.VMEM((pairs, 2, n, PAIR), BF),
            pltpu.VMEM((2 * RB, n), BF),
            pltpu.VMEM((HALF, inner), BF),
            pltpu.VMEM((HALF, inner), F32),
            pltpu.VMEM(e.shape, BF),
            pltpu.SemaphoreType.DMA((e.shape[0] + 2,)),
        ]
        + (sums if last else []),
        compiler_params=params(28),
        cost_estimate=cost(30),
    )(q, k, v, *hbm(att, linv), do, *hbm(e), cos, sin, *before)


def feed_kernel(
    lens, tok_ref, own_ref, got_ref, cot_ref, mod_ref, gain_ref, ub_ref, up_ref, down_ref,
    middle_ref, fin_t_ref, act_ref, ug_ref, fg_t_ref, fo_ref, fng_ref, ubg_ref, sums_ref,
    *, first_row,
):
    i = pl.program_id(0)
    rows = pl.ds(pl.multiple_of(i * RB, RB), RB)
    mod = mod_ref[...]
    branch = own_ref[rows, :].astype(F32) + got_ref[...].astype(F32)
    middle = tok_ref[...].astype(F32) + mod[2:3] * branch
    middle_ref[rows, :] = middle
    xhat, _ = normalize(middle)
    fin = (xhat * (gain_ref[...].astype(F32) * (1.0 + mod[4:5])) + mod[3:4]).astype(BF)
    fin_t_ref[:, rows] = fin.T
    seed = cot_ref[...].astype(F32) * live_rows(total_of(lens), first_row + i * RB, RB)
    fg = (mod[5:6] * seed).astype(BF)
    fg_t_ref[:, rows] = fg.T
    u = mm(fin, up_ref[...]) + ub_ref[...].astype(F32)
    u2 = u * u
    t = jnp.tanh(u * (gelu_k + (gelu_k * gelu_c) * u2))
    half = 0.5 * (1.0 + t)
    act = (u * half).astype(BF)
    act_ref[rows, :] = act
    slope = half + (0.5 * u) * (1.0 - t * t) * (gelu_k + (3.0 * gelu_k * gelu_c) * u2)
    ugf = mm(fg, down_ref[...], NT) * slope
    ug = ugf.astype(BF)
    ug_ref[rows, :] = ug
    fng_ref[rows, :] = mm(ug, up_ref[...], NT).astype(BF)
    fo = mm(act, down_ref[...])
    fo_ref[rows, :] = fo.astype(BF)
    ubs = jnp.sum(ugf, axis=0, keepdims=True)
    sums = jnp.concatenate(
        [jnp.sum(seed, axis=0, keepdims=True), jnp.sum(seed * fo, axis=0, keepdims=True)], axis=0
    )

    @pl.when(i == 0)
    def _():
        ubg_ref[...] = ubs
        sums_ref[...] = sums

    @pl.when(i > 0)
    def _():
        ubg_ref[...] += ubs
        sums_ref[...] += sums


def feed(half, lens, tok, own, got, cot, mod, gain, ub, up, down):
    d, f = up.shape
    here = rows_of(d, half * STEPS)
    return pl.pallas_call(
        functools.partial(feed_kernel, first_row=half * HALF),
        grid=(STEPS,),
        in_specs=[
            SMEM, here, VMEM, rows_of(d), here, VMEM, VMEM, VMEM, VMEM, VMEM,
        ],
        out_specs=[VMEM] * 9,
        out_shape=[
            shape((HALF, d)), shape((d, HALF), BF), shape((HALF, f), BF),
            shape((HALF, f), BF), shape((d, HALF), BF), shape((HALF, d), BF),
            shape((HALF, d), BF), shape((1, f)), shape((2, d)),
        ],
        compiler_params=params(16),
        cost_estimate=cost(9),
    )(lens, *hbm(tok), own, got, *hbm(cot), mod, gain, ub, up, down)


def middle_kernel(
    lens, middle_ref, own_ref, got_ref, cot_ref, bown_ref, bgot_ref, mod_ref, gain_ref, w_ref,
    mg_ref, bg_t_ref, do_ref, sums_ref, *, first_row,
):
    i = pl.program_id(0)
    rows = pl.ds(pl.multiple_of(i * RB, RB), RB)
    mod = mod_ref[...]
    xhat, inverse = normalize(middle_ref[rows, :])
    c = own_ref[rows, :].astype(F32) + got_ref[...].astype(F32)
    seed = cot_ref[...].astype(F32) * live_rows(total_of(lens), first_row + i * RB, RB)
    mg = seed + norm_pull(c, xhat, inverse, gain_ref[...].astype(F32) * (1.0 + mod[4:5]))
    mg_ref[...] = mg
    bg = (mod[2:3] * mg).astype(BF)
    bg_t_ref[:, rows] = bg.T
    do_ref[rows, :] = mm(bg, w_ref[...], NT).astype(BF)
    branch = bown_ref[rows, :].astype(F32) + bgot_ref[...].astype(F32)
    sums = jnp.concatenate(
        [
            jnp.sum(mg * branch, axis=0, keepdims=True),
            jnp.sum(c, axis=0, keepdims=True),
            jnp.sum(c * xhat, axis=0, keepdims=True),
        ],
        axis=0,
    )

    @pl.when(i == 0)
    def _():
        sums_ref[...] = sums

    @pl.when(i > 0)
    def _():
        sums_ref[...] += sums


def middle_back(half, lens, middle, own, got, cot, bown, bgot, mod, gain, w):
    inner, d = w.shape
    return pl.pallas_call(
        functools.partial(middle_kernel, first_row=half * HALF),
        grid=(STEPS,),
        in_specs=[
            SMEM, VMEM, VMEM, rows_of(d), rows_of(d, half * STEPS), VMEM, rows_of(d), VMEM, VMEM,
            VMEM,
        ],
        out_specs=[rows_of(d), VMEM, VMEM, VMEM],
        out_shape=[
            pltpu.HBM((HALF, d), F32), shape((d, HALF), BF), shape((HALF, inner), BF), shape((3, d)),
        ],
        compiler_params=params(14),
        cost_estimate=cost(40),
    )(lens, middle, own, got, *hbm(cot), bown, bgot, mod, gain, w)


def weight_grad_kernel(starts, *refs, ins, plan, outs, blocks, chunk):
    out, g = refs[ins : ins + outs], refs[ins + outs]
    j = pl.program_id(0)
    begin = 0
    for chunks, parts in plan:

        @pl.when((j >= begin) & (j < begin + chunks))
        def _(parts=parts, begin=begin):
            cols = pl.ds(pl.multiple_of((j - begin) * chunk, 128), chunk)
            total = None
            for left, column, part in parts:
                size = refs[part].shape[0]
                term = mm(refs[left][:, column : column + size], refs[part][:, cols])
                total = term if total is None else total + term
            g[...] = total

        begin += chunks
    size = out[0].shape[1]
    cols = pl.ds(pl.multiple_of(j * chunk, 128), chunk)
    for k in range(outs):
        for m in range(blocks):
            rows = pl.ds(pl.multiple_of(starts[k * blocks + m], 16), size)
            out[k][m, :, cols] = g[rows, :].astype(BF)


def weight_grad(couples, starts, outs, blocks, size, chunk):
    ins, specs, plan, begin = [], [], [], 0
    for lefts, rights in couples:
        columns = []
        for part in lefts:
            columns += [(len(ins), i) for i in range(0, part.shape[1], HALF)]
            ins.append(part)
            specs.append(VMEM)
        for parts in rights:
            chunks = parts[0].shape[1] // chunk
            entries, row = [], 0
            for part in parts:
                left, column = columns[row // HALF]
                entries.append((left, column, len(ins)))
                row += part.shape[0]
                ins.append(part)
                specs.append(VMEM)
            plan.append((chunks, entries))
            begin += chunks
    d = couples[0][0][0].shape[0]
    return pl.pallas_call(
        functools.partial(
            weight_grad_kernel, ins=len(ins), plan=plan, outs=outs, blocks=blocks, chunk=chunk
        ),
        grid=(begin,),
        in_specs=[SMEM] + specs,
        out_specs=[VMEM] * outs,
        out_shape=[shape((blocks, size, begin * chunk), BF)] * outs,
        scratch_shapes=[pltpu.VMEM((d, chunk), F32)],
        compiler_params=params(12),
        cost_estimate=cost(4),
    )(starts, *ins)


def mix_kernel(side, m0_ref, m1_ref, f0_ref, f1_ref, got_ref, mod_ref, bias_ref, out_ref):
    second = side[0] == 1
    own = jnp.where(second, f1_ref[...], f0_ref[...])
    fo = own.astype(F32) + got_ref[...].astype(F32) + bias_ref[...].astype(F32)
    middle = jnp.where(second, m1_ref[...], m0_ref[...])
    out_ref[...] = (middle + mod_ref[5:6] * fo).astype(BF)


def here_rows(width):
    return pl.BlockSpec((RB, width), lambda i, side: (side[0] * STEPS + i, 0))


def mix(side, middles, outs, got, mod, bias):
    d = got.shape[1]
    return pl.pallas_call(
        mix_kernel,
        grid_spec=pltpu.PrefetchScalarGridSpec(
            num_scalar_prefetch=1,
            grid=(STEPS,),
            in_specs=[rows_of(d)] * 5 + [VMEM, VMEM],
            out_specs=rows_of(d),
        ),
        out_shape=shape((HALF, d), BF),
        compiler_params=params(16),
        cost_estimate=cost(1),
    )(side, *hbm(*middles, *outs), got, mod, bias)


def input_back_kernel(side, q0_ref, q1_ref, k_ref, v_ref, w_ref, out_ref, *, mine):
    second = (side[0] == 1) if mine else (side[0] == 0)
    here = pl.ds(pl.multiple_of(pl.program_id(0) * RB, RB), RB)
    dq = jnp.where(second, q1_ref[here, :], q0_ref[here, :])
    start = (side[0] if mine else 1 - side[0]) * HALF + pl.program_id(0) * RB
    rows = pl.ds(pl.multiple_of(start, RB), RB)
    total = mm(dq, w_ref[0], NT)
    total += mm(k_ref[rows, :], w_ref[1], NT)
    total += mm(v_ref[rows, :], w_ref[2], NT)
    out_ref[here, :] = total.astype(out_ref.dtype)


def input_back(side, dqs, dk, dv, w, mine, kind):
    _, d, inner = w.shape
    return pl.pallas_call(
        functools.partial(input_back_kernel, mine=mine),
        grid_spec=pltpu.PrefetchScalarGridSpec(
            num_scalar_prefetch=1,
            grid=(STEPS,),
            in_specs=[VMEM] * 5,
            out_specs=VMEM,
        ),
        out_shape=shape((HALF, d), kind),
        compiler_params=params(24),
        cost_estimate=cost(1),
    )(side, *dqs, dk, dv, w)


def final_kernel(side, tok_ref, own_ref, got_ref, mg0_ref, mg1_ref, mod_ref, gain_ref, out_ref, sums_ref):
    i = pl.program_id(0)
    xhat, inverse = normalize(tok_ref[...].astype(F32))
    c = own_ref[...] + got_ref[...].astype(F32)
    mg = jnp.where(side[0] == 1, mg1_ref[...], mg0_ref[...])
    out_ref[...] = mg + norm_pull(c, xhat, inverse, gain_ref[...].astype(F32) * (1.0 + mod_ref[1:2]))
    sums = jnp.concatenate(
        [jnp.sum(c, axis=0, keepdims=True), jnp.sum(c * xhat, axis=0, keepdims=True)], axis=0
    )

    @pl.when(i == 0)
    def _():
        sums_ref[...] = sums

    @pl.when(i > 0)
    def _():
        sums_ref[...] += sums


def final(side, tok, own, got, mgs, mod, gain):
    d = tok.shape[1]
    return pl.pallas_call(
        final_kernel,
        grid_spec=pltpu.PrefetchScalarGridSpec(
            num_scalar_prefetch=1,
            grid=(STEPS,),
            in_specs=[here_rows(d)] + [rows_of(d)] * 4 + [whole(6, d), whole(1, d)],
            out_specs=[rows_of(d), constant(2, d)],
        ),
        out_shape=[shape((HALF, d)), shape((2, d))],
        compiler_params=params(24),
        cost_estimate=cost(1),
    )(side, *hbm(tok), own, got, *hbm(*mgs), mod, gain)


def collect_kernel(
    half_ref, got_ref, mid0_ref, mid1_ref, seed0_ref, seed1_ref, mod_ref, ga_ref, gf_ref, db_ref,
    cond_ref, u0_ref, u1_ref, out_ref, all_ref,
):
    half = half_ref[...] + got_ref[...]
    mid = mid0_ref[...] + mid1_ref[...]
    seeds = seed0_ref[0:1, :] + seed1_ref[0:1, :]
    d = half.shape[1]
    s_att, s_feed = half[1:2], mid[2:3]
    all_ref[...] = jnp.zeros_like(all_ref)
    all_ref[0:1, : cond_ref.shape[1]] = cond_ref[...].astype(F32)
    rows = (
        half[0:1], s_att * ga_ref[...].astype(F32), mid[0:1], mid[1:2],
        s_feed * gf_ref[...].astype(F32), half[2:3] + seeds * db_ref[...].astype(F32),
        (1.0 + mod_ref[1:2]) * s_att, (1.0 + mod_ref[4:5]) * s_feed, mod_ref[5:6] * seeds,
    )
    for i, row in enumerate(rows):
        all_ref[i + 1 : i + 2, :] = row
    for i in range(u0_ref.shape[1] // d):
        cols = slice(i * d, (i + 1) * d)
        all_ref[10 + i : 11 + i, :] = u0_ref[:, cols] + u1_ref[:, cols]
    out_ref[...] = all_ref[...].astype(BF)


def collect(half, got, mids, seeds, mod, ga, gf, db, cond, ubs):
    d = half.shape[1]
    rows = -(-(10 + ubs[0].shape[1] // d) // 16) * 16
    return pl.pallas_call(
        collect_kernel,
        in_specs=[VMEM] * 13,
        out_specs=VMEM,
        out_shape=shape((rows, d), BF),
        scratch_shapes=[pltpu.VMEM((rows, d), F32)],
        compiler_params=params(4),
        cost_estimate=cost(1),
    )(half, got, *mids, *seeds, mod, ga, gf, db, cond, *ubs)


def finish_kernel(every_ref, weight_ref, bias_ref, one_ref, two_ref, down_ref, up_ref):
    d = every_ref.shape[2]
    cond = every_ref[:, 0, :]

    def summed(j):
        return jnp.sum(every_ref[:, j, :].astype(F32), axis=0, keepdims=True)

    for j in range(6):
        rows = every_ref[:, 1 + j, :]
        weight_ref[:, j * d : (j + 1) * d] = mm(cond[:, : weight_ref.shape[0]], rows, TN)
        bias_ref[j * d : (j + 1) * d] = summed(1 + j).reshape(d)
    one_ref[...] = summed(7).reshape(d)
    two_ref[...] = summed(8).reshape(d)
    down_ref[...] = summed(9).reshape(d)
    for j in range(up_ref.shape[0] // d):
        up_ref[j * d : (j + 1) * d] = summed(10 + j).reshape(d)


def finish(every, cond_dim, f):
    d = every.shape[2]
    return pl.pallas_call(
        finish_kernel,
        in_specs=[VMEM],
        out_specs=[VMEM] * 6,
        out_shape=[shape((cond_dim, 6 * d)), shape((6 * d,))]
        + [shape((d,))] * 3
        + [shape((f,))],
        compiler_params=params(12),
        cost_estimate=cost(2),
    )(every)


def together(*values):
    return lax.optimization_barrier(values)


def perm(dp_size, move):
    pairs = []
    for index in range(dp_size):
        for y in range(2):
            to = move(index >> 2, (index >> 1) & 1, y, index & 1)
            pairs.append((index * 2 + y, ((to[0] * 2 + to[1]) * 2 + to[3]) * 2 + to[2]))
    return pairs


def xor_order(stack, me, bits):
    for b in range(bits):
        shaped = stack.reshape((-1, 2, 1 << b) + stack.shape[1:])
        flipped = jnp.concatenate([shaped[:, 1:], shaped[:, :1]], axis=1)
        stack = jnp.where(((me >> b) & 1) == 1, flipped, shaped).reshape(stack.shape)
    return stack


def per_device(
    tokens,
    conditioning,
    lengths,
    input_weight,
    output_weight,
    up_weight,
    up_bias,
    down_weight,
    down_bias,
    attention_gain,
    feed_gain,
    adaptive_weight,
    adaptive_bias,
    cotangent,
):
    n, d = tokens.shape
    assert lengths.shape[0] == 1
    inner = input_weight.shape[2]
    f = up_weight.shape[1]
    dp_size = lax.axis_size("dp")
    planes = dp_size // 4
    zbits = planes.bit_length() - 1
    index = lax.axis_index("dp")
    y = lax.axis_index("tensor")
    c = index % 2
    x = (index // 2) % 2
    z = index // 4
    side = y.astype(jnp.int32).reshape(1)

    make = functools.partial(perm, dp_size)
    y_swap = make(lambda z, x, y, c: (z, x, 1 - y, c))
    core_swap = make(lambda z, x, y, c: (z, x, y, 1 - c))
    x_swap = make(lambda z, x, y, c: (z, 1 - x, y, c))

    def send(value, how):
        return lax.ppermute(value, AXES, how)

    gain_a = attention_gain.reshape(1, d)
    gain_f = feed_gain.reshape(1, d)
    up_b = up_bias.reshape(1, f)

    mod, normed_t, q, k, v, cosine, sine = project(
        lengths, tokens, conditioning, adaptive_weight, adaptive_bias, attention_gain,
        input_weight,
    )
    halves = (0, 1)
    att, linv, e, branch, branch_got = [], [], [], [], []
    for h in halves:
        got = attend(h, lengths, q, k, v, output_weight)
        for store, value in zip((att, linv, e, branch), got):
            store.append(value)
        if h == 0:
            branch[0], k = together(branch[0], k)
        branch_got.append(send(branch[h], y_swap))
    fed, fng_got = [], []
    for h in halves:
        fed.append(
            feed(
                h, lengths, tokens, branch[h], branch_got[h], cotangent, mod, gain_f, up_b,
                up_weight, down_weight,
            )
        )
        fng_sent = fed[h][6]
        if h == 0:
            fng_sent, branch_got[1] = together(fng_sent, branch_got[1])
        fng_got.append(send(fng_sent, y_swap))
    middle, fin_t, act, ug, fg_t, fo, fng, ubg, seed_sums = zip(*fed)

    r_out = d // dp_size

    def cut(couples, chunk):
        if r_out % 16 == 0:
            place = [
                (((z ^ m) * 2 + (x ^ dx)) * 2 + (c ^ s)) * r_out
                for s in range(2)
                for dx in range(2)
                for m in range(planes)
            ]
            starts = jnp.stack([p.astype(jnp.int32) for p in place])
            outs = weight_grad(couples, starts, 2, 2 * planes, r_out, chunk)
        else:
            grad = jnp.concatenate(
                [
                    mm(jnp.concatenate(a, axis=1), jnp.concatenate(b)).astype(BF)
                    for a, bs in couples
                    for b in bs
                ],
                axis=1,
            )
            blocks = grad.reshape(planes, 2, 2, r_out, grad.shape[1])
            blocks = xor_order(blocks, z, zbits).transpose(2, 1, 0, 3, 4)
            blocks = xor_order(blocks, c, 1)
            outs = [xor_order(b, x, 1) for b in blocks]
        return [o.reshape(2, planes, r_out, -1) for o in outs]

    def send_z(total):
        return [
            send(total[m].astype(BF), make(lambda z, x, y, c: (z ^ m, x, y, c)))
            for m in range(1, planes)
        ]

    def sum_z(total, got):
        return sum((v.astype(F32) for v in got), total[0])

    feed_own, feed_far = cut([(fg_t, [act]), (fin_t, [ug])], f // 2)
    feed_core_got = send(feed_far, core_swap)
    fng_got[0], feed_own = together(fng_got[0], feed_own)

    mids, backs = [], []
    for h in halves:
        mids.append(
            middle_back(
                h, lengths, middle[h], fng[h], fng_got[h], cotangent, branch[h], branch_got[h],
                mod, gain_f, output_weight,
            )
        )
        if h == 0:
            feed_core_got, do = together(feed_core_got, mids[0][2])
            feed_near = feed_own[0].astype(F32) + feed_core_got[0].astype(F32)
            feed_far = (feed_own[1].astype(F32) + feed_core_got[1].astype(F32)).astype(BF)
            do, feed_far = together(do, feed_far)
            feed_x_got = send(feed_far, x_swap)
        else:
            do = mids[1][2]
        backs.append(
            attend_back(
                h, q, k, v, att[h], linv[h], e[h], do, cosine, sine, backs[0][1:] if h else ()
            )
        )
        if h == 0:
            fng_got[1], fo_sent, _ = together(
                fng_got[1], jnp.where(y == 0, fo[1], fo[0]), backs[0][0]
            )
            fo_got = send(fo_sent, y_swap)
    mg, bg_t, _, mid_sums = zip(*mids)
    dqs, (dk, dv) = (backs[0][0], backs[1][0]), backs[1][1:]

    ang_other = input_back(side, dqs, dk, dv, input_weight, False, BF)
    dk, ang_other, fo_got = together(dk, ang_other, fo_got)
    ang_got = send(ang_other, y_swap)
    attn_own, attn_far = cut([(bg_t, [att]), ([normed_t], [dqs, [dk], [dv]])], inner)
    attn_core_got = send(attn_far, core_swap)
    dk, feed_x_got, attn_own = together(dk, feed_x_got, attn_own)
    feed_total = feed_near + feed_x_got.astype(F32)
    feed_total, attn_core_got = together(feed_total, attn_core_got)
    feed_z_got = send_z(feed_total)
    attn_near = attn_own[0].astype(F32) + attn_core_got[0].astype(F32)
    attn_far = (attn_own[1].astype(F32) + attn_core_got[1].astype(F32)).astype(BF)
    attn_far, dk = together(attn_far, dk)
    attn_x_got = send(attn_far, x_swap)
    ang_own = input_back(side, dqs, dk, dv, input_weight, True, F32)
    tok_grad, att_sums = final(side, tokens, ang_own, ang_got, mg, mod, gain_a)

    half_sums = jnp.concatenate([att_sums, seed_sums[0][1:] + seed_sums[1][1:]], axis=0)
    flat = collect(
        half_sums, send(half_sums, y_swap), mid_sums, seed_sums, mod, gain_a, gain_f,
        down_bias.reshape(1, d), conditioning, ubg,
    )
    flat, attn_x_got, fo_got = together(flat, attn_x_got, fo_got)
    every = lax.all_to_all(
        jnp.broadcast_to(flat[None], (dp_size,) + flat.shape), "dp", 0, 0, tiled=True
    )
    attn_total = attn_near + attn_x_got.astype(F32)
    attn_z_got = send_z(attn_total)
    mixed = mix(side, middle, fo, fo_got, mod, down_bias.reshape(1, d))
    mixed, *feed_z_got = together(mixed, *feed_z_got)
    feed_grads = sum_z(feed_total, feed_z_got)
    down_grad, up_grad = feed_grads[:, :f], feed_grads[:, f:]
    attn_grads = sum_z(attn_total, attn_z_got)
    out_grad, in_grad = attn_grads[:, :inner], attn_grads[:, inner:]
    (
        adaptive_weight_grad, adaptive_bias_grad, attention_gain_grad, feed_gain_grad,
        down_bias_grad, up_bias_grad,
    ) = finish(every.reshape(dp_size, flat.shape[0], d), conditioning.shape[1], f)
    return (
        mixed,
        tok_grad,
        in_grad.reshape(r_out, 3, inner).transpose(1, 0, 2),
        out_grad.T,
        up_grad,
        up_bias_grad,
        down_grad.T,
        down_bias_grad,
        attention_gain_grad,
        feed_gain_grad,
        adaptive_weight_grad,
        adaptive_bias_grad,
    )


def solution(mesh):
    placed = (
        P("dp", None),
        P("dp", None),
        P("dp", None),
        P(None, None, "tensor"),
        P("tensor", None),
        P(None, "tensor"),
        P("tensor"),
        P("tensor", None),
        P(),
        P(),
        P(),
        P(),
        P(),
        P("dp", None),
    )
    return jax.shard_map(
        per_device,
        mesh=mesh,
        in_specs=placed,
        out_specs=(
            P(("dp", "tensor"), None),
            P(("dp", "tensor"), None),
            P(None, "dp", "tensor"),
            P("tensor", "dp"),
            P("dp", "tensor"),
            P("tensor"),
            P("tensor", "dp"),
            P(),
            P(),
            P(),
            P(),
            P(),
        ),
        check_vma=False,
    )
```

```python
import functools

import jax
import jax.numpy as jnp
import numpy as np
from jax import lax
from jax.experimental import pallas as pl
from jax.experimental.pallas import tpu as pltpu
from jax.sharding import PartitionSpec as P

HD = 64
ROW_LEN = 1024
NSEG = 8
BLOCK = 128
PAIR = 2 * HD
RB = 256
HALF = ROW_LEN // 2
STEPS = HALF // RB

norm_eps = 1e-05
masked_score = -1000000000.0
rotary_base = 10000.0
gelu_k = 0.7978845608028654
gelu_c = 0.044715

AXES = ("dp", "tensor")
BF = jnp.bfloat16
F32 = jnp.float32
NN = ((1,), (0,))
NT = ((1,), (1,))
TN = ((0,), (0,))
VMEM = pl.BlockSpec(memory_space=pltpu.VMEM)
SMEM = pl.BlockSpec(memory_space=pltpu.SMEM)
FAR = pl.BlockSpec(memory_space=pltpu.HBM)


def mm(left, right, dims=NN):
    return lax.dot_general(left, right, (dims, ((), ())), preferred_element_type=F32)


def params(mib):
    return pltpu.CompilerParams(vmem_limit_bytes=mib << 20)


def cost(us):
    return pl.CostEstimate(flops=int(us * 1.15e9), bytes_accessed=0, transcendentals=0)


def shape(dims, kind=F32):
    return jax.ShapeDtypeStruct(dims, kind)


def hbm(*values):
    return [pltpu.with_memory_space_constraint(v, pltpu.HBM) for v in values]


def normalize(values):
    centered = values - jnp.mean(values, axis=-1, keepdims=True)
    inverse = lax.rsqrt(jnp.mean(centered * centered, axis=-1, keepdims=True) + norm_eps)
    return centered * inverse, inverse


def norm_pull(cotangent, xhat, inverse, weight):
    e = cotangent * weight
    return inverse * (
        e
        - jnp.mean(e, axis=-1, keepdims=True)
        - xhat * jnp.mean(e * xhat, axis=-1, keepdims=True)
    )


def live_rows(total, first_row, rows):
    slots = lax.broadcasted_iota(jnp.int32, (rows, 1), 0) + first_row
    return (slots < total).astype(F32)


def rows_of(width, offset=0):
    return pl.BlockSpec((RB, width), lambda i, *_: (i + offset, 0))


def turned_rows(width):
    return pl.BlockSpec((width, RB), lambda i, *_: (0, i))


def whole(*dims):
    return pl.BlockSpec(dims, lambda *_: (0,) * len(dims), pipeline_mode=pl.Buffered(1))


def constant(*dims):
    return pl.BlockSpec(dims, lambda *_: (0,) * len(dims))


def head_masks():
    lane = lax.broadcasted_iota(jnp.int32, (1, PAIR), 1)
    low = (lane < HD).astype(F32)
    return (lane % HD) < HD // 2, (low, 1.0 - low)


def rotary_tables():
    lanes = np.arange(PAIR) % (HD // 2)
    frequency = (rotary_base ** (-lanes * (2.0 / HD))).astype(np.float32)
    angles = np.arange(ROW_LEN, dtype=np.float32)[:, None] * frequency[None, :]
    return np.cos(angles), np.sin(angles)


def place_of(lens, slot):
    segment, start, bound = 0, 0, 0
    for j in range(NSEG):
        bound = bound + lens[0, j]
        passed = bound <= slot
        segment = segment + jnp.where(passed, 1, 0)
        start = start + jnp.where(passed, lens[0, j], 0)
    return segment, start


def total_of(lens):
    total = lens[0, 0]
    for j in range(1, NSEG):
        total = total + lens[0, j]
    return total


def project_kernel(
    lens, tokfar_ref, condfar_ref, awfar_ref, abfar_ref, gainfar_ref, wfar_ref, cosfar_ref,
    sinfar_ref,
    mod_ref, turnedfar_ref, q_ref, k_ref, v_ref, cos_ref, sin_ref,
    tok, aw, w, cos_table, sin_table, normed, turned, cond_ref, ab_ref, gain_ref, sems,
):
    n, d = tok.shape
    pairs = k_ref.shape[1] // PAIR
    copies = [
        pltpu.make_async_copy(source, target, sems.at[i])
        for i, (source, target) in enumerate(
            (
                (awfar_ref, aw), (tokfar_ref, tok), (wfar_ref, w), (cosfar_ref, cos_table),
                (sinfar_ref, sin_table), (turned, turnedfar_ref), (condfar_ref, cond_ref),
                (abfar_ref, ab_ref), (gainfar_ref, gain_ref),
            )
        )
    ]
    for copy in copies[6:] + copies[:5]:
        copy.start()
    for copy in copies[6:] + copies[:1]:
        copy.wait()
    cond = jnp.broadcast_to(cond_ref[...], (8, cond_ref.shape[1]))
    row = mm(cond, aw[...])[0:1] + ab_ref[...].astype(F32).reshape(1, 6 * d)
    for j in range(6):
        mod_ref[j : j + 1, :] = row[:, j * d : (j + 1) * d]
    weight = gain_ref[...].astype(F32).reshape(1, d) * (1.0 + row[:, d : 2 * d])
    copies[1].wait()
    for i in range(n // RB):
        rows = slice(i * RB, (i + 1) * RB)
        xhat, _ = normalize(tok[rows, :].astype(F32))
        part = (xhat * weight + row[:, :d]).astype(BF)
        normed[rows, :] = part
        turned[:, rows] = part.T
    copies[5].start()
    copies[3].wait()
    copies[4].wait()
    for i in range(n // BLOCK):
        _, start = place_of(lens, i * BLOCK)
        rows = slice(i * BLOCK, (i + 1) * BLOCK)
        at = pl.ds(pl.multiple_of(i * BLOCK - start, BLOCK), BLOCK)
        cos_ref[rows, :] = cos_table[at, :]
        sin_ref[rows, :] = sin_table[at, :]
    copies[2].wait()
    first, _ = head_masks()

    def rotate(u, rows):
        turned_u = jnp.where(
            first, -pltpu.roll(u, PAIR - HD // 2, 1), pltpu.roll(u, HD // 2, 1)
        )
        return u * cos_ref[rows, :] + turned_u * sin_ref[rows, :]

    for i in range(n // HALF):
        rows = slice(i * HALF, (i + 1) * HALF)
        left = normed[rows, :]
        queries, keys, values = (mm(left, w[j]) for j in range(3))
        for p in range(pairs):
            cols = slice(p * PAIR, (p + 1) * PAIR)
            q_ref[rows, cols] = (rotate(queries[:, cols], rows) * (HD**-0.5)).astype(BF)
            k_ref[rows, cols] = rotate(keys[:, cols], rows).astype(BF)
        v_ref[rows, :] = values.astype(BF)
    copies[5].wait()


def project(lens, tok, cond, aw, ab, gain, w):
    n, d = tok.shape
    inner = w.shape[2]
    tables = [jnp.asarray(t) for t in rotary_tables()]
    return pl.pallas_call(
        project_kernel,
        in_specs=[SMEM] + [FAR] * 8,
        out_specs=[VMEM, FAR, VMEM, VMEM, VMEM, VMEM, VMEM],
        out_shape=[
            shape((6, d)), pltpu.HBM((d, n), BF), shape((n, inner), BF), shape((n, inner), BF),
            shape((n, inner), BF), shape((n, PAIR)), shape((n, PAIR)),
        ],
        scratch_shapes=[
            pltpu.VMEM((n, d), BF), pltpu.VMEM(aw.shape, BF), pltpu.VMEM(w.shape, BF),
            pltpu.VMEM((n, PAIR), F32), pltpu.VMEM((n, PAIR), F32), pltpu.VMEM((n, d), BF),
            pltpu.VMEM((d, n), BF), pltpu.VMEM(cond.shape, BF), pltpu.VMEM(ab.shape, BF),
            pltpu.VMEM(gain.shape, BF), pltpu.SemaphoreType.DMA((9,)),
        ],
        compiler_params=params(24),
        cost_estimate=cost(5),
    )(*hbm(lens, tok, cond, aw, ab, gain, w, *tables))


def attend_kernel(
    lens, q_ref, k_ref, v_ref, w_ref, attfar_ref, linvfar_ref, efar_ref, out_ref,
    vx, att, linv, es, sems, *, first_row,
):
    n = ROW_LEN
    pairs = vx.shape[0]
    _, masks = head_masks()
    low = masks[0] > 0.5
    segments = [place_of(lens, i * BLOCK)[0] for i in range(n // BLOCK)]
    biases = [
        jnp.concatenate(
            [
                jnp.full((1, BLOCK), jnp.where(here == there, 0.0, masked_score), F32)
                for there in segments
            ],
            axis=1,
        )
        for here in segments[first_row // BLOCK : (first_row + HALF) // BLOCK]
    ]
    for p in range(pairs):
        vx[p, :, 0:PAIR] = v_ref[:, p * PAIR : (p + 1) * PAIR]
        vx[p, :, PAIR:] = jnp.ones((n, PAIR), BF)
    per = RB // BLOCK
    copies = []

    def leave(source, target):
        copies.append(pltpu.make_async_copy(source, target, sems.at[len(copies)]))
        copies[-1].start()

    for step in range(STEPS):
        rows = slice(step * RB, (step + 1) * RB)
        for p in range(pairs):
            cols = slice(p * PAIR, (p + 1) * PAIR)
            q = q_ref[first_row + step * RB : first_row + (step + 1) * RB, cols].astype(F32)
            keys = k_ref[:, cols]
            outs = []
            for h in range(2):
                s = mm((q * masks[h]).astype(BF), keys, NT)
                s = jnp.concatenate(
                    [
                        s[b * BLOCK : (b + 1) * BLOCK] + biases[step * per + b]
                        for b in range(per)
                    ],
                    axis=0,
                )
                peak = jnp.max(s, axis=1, keepdims=True)
                e = jnp.exp(s - peak).astype(BF)
                es[step * pairs + p, h] = e
                outs.append(mm(e, vx[p]))
            leave(es.at[step * pairs + p], efar_ref.at[step * pairs + p])
            inverse = 1.0 / jnp.where(low, outs[0][:, PAIR:], outs[1][:, PAIR:])
            att[rows, cols] = (
                jnp.where(low, outs[0][:, :PAIR], outs[1][:, :PAIR]) * inverse
            ).astype(BF)
            linv[rows, cols] = inverse
        leave(att.at[rows], attfar_ref.at[rows])
        leave(linv.at[rows], linvfar_ref.at[rows])
        out_ref[rows, :] = mm(att[rows, :], w_ref[...]).astype(BF)
    for copy in copies:
        copy.wait()


def attend(half, lens, q, k, v, w):
    n, inner = q.shape
    d = w.shape[1]
    pairs = inner // PAIR
    parts = STEPS * pairs
    return pl.pallas_call(
        functools.partial(attend_kernel, first_row=half * HALF),
        in_specs=[SMEM, VMEM, VMEM, VMEM, VMEM],
        out_specs=[FAR, FAR, FAR, VMEM],
        out_shape=[
            pltpu.HBM((HALF, inner), BF), pltpu.HBM((HALF, inner), F32),
            pltpu.HBM((parts, 2, RB, n), BF), shape((HALF, d), BF),
        ],
        scratch_shapes=[
            pltpu.VMEM((pairs, n, 2 * PAIR), BF), pltpu.VMEM((HALF, inner), BF),
            pltpu.VMEM((HALF, inner), F32), pltpu.VMEM((parts, 2, RB, n), BF),
            pltpu.SemaphoreType.DMA((parts + 2 * STEPS,)),
        ],
        compiler_params=params(20),
        cost_estimate=cost(8),
    )(lens, q, k, v, w)


def attend_back_kernel(
    q_ref, k_ref, v_ref, attfar_ref, linvfar_ref, do_ref, efar_ref, cos_ref, sin_ref, *refs, last
):
    n = ROW_LEN
    if last:
        dk0_ref, dv0_ref, dq_ref, dkout_ref, dvout_ref, vx, km, ds, att, linv, es, sems, dk, dv = refs
    else:
        dq_ref, dk, dv, vx, km, ds, att, linv, es, sems = refs
    pairs = vx.shape[0]
    first, masks = head_masks()
    parts = STEPS * pairs
    copies = [
        pltpu.make_async_copy(attfar_ref, att, sems.at[parts]),
        pltpu.make_async_copy(linvfar_ref, linv, sems.at[parts + 1]),
    ] + [
        pltpu.make_async_copy(efar_ref.at[i], es.at[i], sems.at[i]) for i in range(parts)
    ]
    for copy in copies:
        copy.start()
    for p in range(pairs):
        cols = slice(p * PAIR, (p + 1) * PAIR)
        vx[p, :, 0:PAIR] = v_ref[:, cols]
        vx[p, :, PAIR:] = jnp.ones((n, PAIR), BF)
        keys = k_ref[:, cols].astype(F32)
        for h in range(2):
            km[p, h] = (keys * masks[h]).astype(BF)

    def rotate_back(u, rows):
        w = u * sin_ref[rows, :]
        turned = jnp.where(
            first, pltpu.roll(w, PAIR - HD // 2, 1), -pltpu.roll(w, HD // 2, 1)
        )
        return u * cos_ref[rows, :] + turned

    copies[0].wait()
    copies[1].wait()
    for step in range(STEPS):
        here = slice(step * RB, (step + 1) * RB)
        start = (HALF if last else 0) + step * RB
        rows = slice(start, start + RB)
        for p in range(pairs):
            part = step * pairs + p
            cols = slice(p * PAIR, (p + 1) * PAIR)
            dof = do_ref[here, cols].astype(F32) * linv[here, cols]
            dd = dof * att[here, cols].astype(F32)
            qf = q_ref[rows, cols].astype(F32)
            qs, dms, dq = [], [], None
            copies[2 + part].wait()
            for h in range(2):
                dm = (dof * masks[h]).astype(BF)
                left = jnp.concatenate([dm, (-dd * masks[h]).astype(BF)], axis=1)
                dp = mm(left, vx[p], NT)
                sg = (dp * es[part, h].astype(F32)).astype(BF)
                ds[h * RB : (h + 1) * RB, :] = sg
                term = mm(sg, km[p, h])
                dq = term if dq is None else dq + term
                qs.append((qf * masks[h]).astype(BF))
                dms.append(dm)
            dq_ref[here, cols] = (rotate_back(dq, rows) * (HD**-0.5)).astype(BF)
            a = mm(jnp.concatenate(qs, axis=0).T, ds[...])
            b = mm(jnp.concatenate(dms, axis=0).T, es[part].reshape(2 * RB, n))
            if step == 0:
                dk[p] = dk0_ref[p] + a if last else a
                dv[p] = dv0_ref[p] + b if last else b
            else:
                dk[p] += a
                dv[p] += b
    if last:
        for p in range(pairs):
            cols = slice(p * PAIR, (p + 1) * PAIR)
            dkout_ref[:, cols] = rotate_back(dk[p].T, slice(None)).astype(BF)
            dvout_ref[:, cols] = dv[p].T.astype(BF)


def attend_back(half, q, k, v, att, linv, e, do, cos, sin, before=()):
    n, inner = q.shape
    pairs = inner // PAIR
    last = half == 1
    sums = [pltpu.VMEM((pairs, PAIR, n), F32)] * 2
    return pl.pallas_call(
        functools.partial(attend_back_kernel, last=last),
        in_specs=[VMEM, VMEM, VMEM, FAR, FAR, VMEM, FAR, VMEM, VMEM] + [VMEM] * len(before),
        out_specs=[VMEM] * 3,
        out_shape=[shape((HALF, inner), BF)]
        + ([shape((n, inner), BF)] * 2 if last else [shape((pairs, PAIR, n))] * 2),
        scratch_shapes=[
            pltpu.VMEM((pairs, n, 2 * PAIR), BF),
            pltpu.VMEM((pairs, 2, n, PAIR), BF),
            pltpu.VMEM((2 * RB, n), BF),
            pltpu.VMEM((HALF, inner), BF),
            pltpu.VMEM((HALF, inner), F32),
            pltpu.VMEM(e.shape, BF),
            pltpu.SemaphoreType.DMA((e.shape[0] + 2,)),
        ]
        + (sums if last else []),
        compiler_params=params(28),
        cost_estimate=cost(30),
    )(q, k, v, *hbm(att, linv), do, *hbm(e), cos, sin, *before)


def feed_kernel(
    lens, tok_ref, own_ref, got_ref, cot_ref, mod_ref, gain_ref, ub_ref, up_ref, down_ref,
    middle_ref, fin_t_ref, act_ref, ug_ref, fg_t_ref, fo_ref, fng_ref, ubg_ref, sums_ref,
    *, first_row,
):
    i = pl.program_id(0)
    rows = pl.ds(pl.multiple_of(i * RB, RB), RB)
    mod = mod_ref[...]
    branch = own_ref[rows, :].astype(F32) + got_ref[...].astype(F32)
    middle = tok_ref[...].astype(F32) + mod[2:3] * branch
    middle_ref[rows, :] = middle
    xhat, _ = normalize(middle)
    fin = (xhat * (gain_ref[...].astype(F32) * (1.0 + mod[4:5])) + mod[3:4]).astype(BF)
    fin_t_ref[:, rows] = fin.T
    seed = cot_ref[...].astype(F32) * live_rows(total_of(lens), first_row + i * RB, RB)
    fg = (mod[5:6] * seed).astype(BF)
    fg_t_ref[:, rows] = fg.T
    u = mm(fin, up_ref[...]) + ub_ref[...].astype(F32)
    u2 = u * u
    t = jnp.tanh(u * (gelu_k + (gelu_k * gelu_c) * u2))
    half = 0.5 * (1.0 + t)
    act = (u * half).astype(BF)
    act_ref[rows, :] = act
    slope = half + (0.5 * u) * (1.0 - t * t) * (gelu_k + (3.0 * gelu_k * gelu_c) * u2)
    ugf = mm(fg, down_ref[...], NT) * slope
    ug = ugf.astype(BF)
    ug_ref[rows, :] = ug
    fng_ref[rows, :] = mm(ug, up_ref[...], NT).astype(BF)
    fo = mm(act, down_ref[...])
    fo_ref[rows, :] = fo.astype(BF)
    ubs = jnp.sum(ugf, axis=0, keepdims=True)
    sums = jnp.concatenate(
        [jnp.sum(seed, axis=0, keepdims=True), jnp.sum(seed * fo, axis=0, keepdims=True)], axis=0
    )

    @pl.when(i == 0)
    def _():
        ubg_ref[...] = ubs
        sums_ref[...] = sums

    @pl.when(i > 0)
    def _():
        ubg_ref[...] += ubs
        sums_ref[...] += sums


def feed(half, lens, tok, own, got, cot, mod, gain, ub, up, down):
    d, f = up.shape
    here = rows_of(d, half * STEPS)
    return pl.pallas_call(
        functools.partial(feed_kernel, first_row=half * HALF),
        grid=(STEPS,),
        in_specs=[
            SMEM, here, VMEM, rows_of(d), here, VMEM, VMEM, VMEM, VMEM, VMEM,
        ],
        out_specs=[VMEM] * 9,
        out_shape=[
            shape((HALF, d)), shape((d, HALF), BF), shape((HALF, f), BF),
            shape((HALF, f), BF), shape((d, HALF), BF), shape((HALF, d), BF),
            shape((HALF, d), BF), shape((1, f)), shape((2, d)),
        ],
        compiler_params=params(16),
        cost_estimate=cost(9),
    )(lens, *hbm(tok), own, got, *hbm(cot), mod, gain, ub, up, down)


def middle_kernel(
    lens, middle_ref, own_ref, got_ref, cot_ref, bown_ref, bgot_ref, mod_ref, gain_ref, w_ref,
    mg_ref, bg_t_ref, do_ref, sums_ref, *, first_row,
):
    i = pl.program_id(0)
    rows = pl.ds(pl.multiple_of(i * RB, RB), RB)
    mod = mod_ref[...]
    xhat, inverse = normalize(middle_ref[rows, :])
    c = own_ref[rows, :].astype(F32) + got_ref[...].astype(F32)
    seed = cot_ref[...].astype(F32) * live_rows(total_of(lens), first_row + i * RB, RB)
    mg = seed + norm_pull(c, xhat, inverse, gain_ref[...].astype(F32) * (1.0 + mod[4:5]))
    mg_ref[...] = mg
    bg = (mod[2:3] * mg).astype(BF)
    bg_t_ref[:, rows] = bg.T
    do_ref[rows, :] = mm(bg, w_ref[...], NT).astype(BF)
    branch = bown_ref[rows, :].astype(F32) + bgot_ref[...].astype(F32)
    sums = jnp.concatenate(
        [
            jnp.sum(mg * branch, axis=0, keepdims=True),
            jnp.sum(c, axis=0, keepdims=True),
            jnp.sum(c * xhat, axis=0, keepdims=True),
        ],
        axis=0,
    )

    @pl.when(i == 0)
    def _():
        sums_ref[...] = sums

    @pl.when(i > 0)
    def _():
        sums_ref[...] += sums


def middle_back(half, lens, middle, own, got, cot, bown, bgot, mod, gain, w):
    inner, d = w.shape
    return pl.pallas_call(
        functools.partial(middle_kernel, first_row=half * HALF),
        grid=(STEPS,),
        in_specs=[
            SMEM, VMEM, VMEM, rows_of(d), rows_of(d, half * STEPS), VMEM, rows_of(d), VMEM, VMEM,
            VMEM,
        ],
        out_specs=[rows_of(d), VMEM, VMEM, VMEM],
        out_shape=[
            pltpu.HBM((HALF, d), F32), shape((d, HALF), BF), shape((HALF, inner), BF), shape((3, d)),
        ],
        compiler_params=params(14),
        cost_estimate=cost(40),
    )(lens, middle, own, got, *hbm(cot), bown, bgot, mod, gain, w)


def weight_grad_kernel(starts, *refs, ins, plan, outs, blocks, chunk):
    out, g = refs[ins : ins + outs], refs[ins + outs]
    j = pl.program_id(0)
    begin = 0
    for chunks, parts in plan:

        @pl.when((j >= begin) & (j < begin + chunks))
        def _(parts=parts, begin=begin):
            cols = pl.ds(pl.multiple_of((j - begin) * chunk, 128), chunk)
            total = None
            for left, column, part in parts:
                size = refs[part].shape[0]
                term = mm(refs[left][:, column : column + size], refs[part][:, cols])
                total = term if total is None else total + term
            g[...] = total

        begin += chunks
    size = out[0].shape[1]
    cols = pl.ds(pl.multiple_of(j * chunk, 128), chunk)
    for k in range(outs):
        for m in range(blocks):
            rows = pl.ds(pl.multiple_of(starts[k * blocks + m], 16), size)
            out[k][m, :, cols] = g[rows, :].astype(BF)


def weight_grad(couples, starts, outs, blocks, size, chunk):
    ins, specs, plan, begin = [], [], [], 0
    for lefts, rights in couples:
        columns = []
        for part in lefts:
            columns += [(len(ins), i) for i in range(0, part.shape[1], HALF)]
            ins.append(part)
            specs.append(VMEM)
        for parts in rights:
            chunks = parts[0].shape[1] // chunk
            entries, row = [], 0
            for part in parts:
                left, column = columns[row // HALF]
                entries.append((left, column, len(ins)))
                row += part.shape[0]
                ins.append(part)
                specs.append(VMEM)
            plan.append((chunks, entries))
            begin += chunks
    d = couples[0][0][0].shape[0]
    return pl.pallas_call(
        functools.partial(
            weight_grad_kernel, ins=len(ins), plan=plan, outs=outs, blocks=blocks, chunk=chunk
        ),
        grid=(begin,),
        in_specs=[SMEM] + specs,
        out_specs=[VMEM] * outs,
        out_shape=[shape((blocks, size, begin * chunk), BF)] * outs,
        scratch_shapes=[pltpu.VMEM((d, chunk), F32)],
        compiler_params=params(12),
        cost_estimate=cost(4),
    )(starts, *ins)


def mix_kernel(side, m0_ref, m1_ref, f0_ref, f1_ref, got_ref, mod_ref, bias_ref, out_ref):
    second = side[0] == 1
    own = jnp.where(second, f1_ref[...], f0_ref[...])
    fo = own.astype(F32) + got_ref[...].astype(F32) + bias_ref[...].astype(F32)
    middle = jnp.where(second, m1_ref[...], m0_ref[...])
    out_ref[...] = (middle + mod_ref[5:6] * fo).astype(BF)


def here_rows(width):
    return pl.BlockSpec((RB, width), lambda i, side: (side[0] * STEPS + i, 0))


def mix(side, middles, outs, got, mod, bias):
    d = got.shape[1]
    return pl.pallas_call(
        mix_kernel,
        grid_spec=pltpu.PrefetchScalarGridSpec(
            num_scalar_prefetch=1,
            grid=(STEPS,),
            in_specs=[rows_of(d)] * 5 + [VMEM, VMEM],
            out_specs=rows_of(d),
        ),
        out_shape=shape((HALF, d), BF),
        compiler_params=params(16),
        cost_estimate=cost(1),
    )(side, *hbm(*middles, *outs), got, mod, bias)


def input_back_kernel(side, q0_ref, q1_ref, k_ref, v_ref, w_ref, out_ref, *, mine):
    second = (side[0] == 1) if mine else (side[0] == 0)
    here = pl.ds(pl.multiple_of(pl.program_id(0) * RB, RB), RB)
    dq = jnp.where(second, q1_ref[here, :], q0_ref[here, :])
    start = (side[0] if mine else 1 - side[0]) * HALF + pl.program_id(0) * RB
    rows = pl.ds(pl.multiple_of(start, RB), RB)
    total = mm(dq, w_ref[0], NT)
    total += mm(k_ref[rows, :], w_ref[1], NT)
    total += mm(v_ref[rows, :], w_ref[2], NT)
    out_ref[here, :] = total.astype(out_ref.dtype)


def input_back(side, dqs, dk, dv, w, mine, kind):
    _, d, inner = w.shape
    return pl.pallas_call(
        functools.partial(input_back_kernel, mine=mine),
        grid_spec=pltpu.PrefetchScalarGridSpec(
            num_scalar_prefetch=1,
            grid=(STEPS,),
            in_specs=[VMEM] * 5,
            out_specs=VMEM,
        ),
        out_shape=shape((HALF, d), kind),
        compiler_params=params(24),
        cost_estimate=cost(1),
    )(side, *dqs, dk, dv, w)


def final_kernel(side, tok_ref, own_ref, got_ref, mg0_ref, mg1_ref, mod_ref, gain_ref, out_ref, sums_ref):
    i = pl.program_id(0)
    xhat, inverse = normalize(tok_ref[...].astype(F32))
    c = own_ref[...] + got_ref[...].astype(F32)
    mg = jnp.where(side[0] == 1, mg1_ref[...], mg0_ref[...])
    out_ref[...] = mg + norm_pull(c, xhat, inverse, gain_ref[...].astype(F32) * (1.0 + mod_ref[1:2]))
    sums = jnp.concatenate(
        [jnp.sum(c, axis=0, keepdims=True), jnp.sum(c * xhat, axis=0, keepdims=True)], axis=0
    )

    @pl.when(i == 0)
    def _():
        sums_ref[...] = sums

    @pl.when(i > 0)
    def _():
        sums_ref[...] += sums


def final(side, tok, own, got, mgs, mod, gain):
    d = tok.shape[1]
    return pl.pallas_call(
        final_kernel,
        grid_spec=pltpu.PrefetchScalarGridSpec(
            num_scalar_prefetch=1,
            grid=(STEPS,),
            in_specs=[here_rows(d)] + [rows_of(d)] * 4 + [whole(6, d), whole(1, d)],
            out_specs=[rows_of(d), constant(2, d)],
        ),
        out_shape=[shape((HALF, d)), shape((2, d))],
        compiler_params=params(24),
        cost_estimate=cost(1),
    )(side, *hbm(tok), own, got, *hbm(*mgs), mod, gain)


def collect_kernel(
    half_ref, got_ref, mid0_ref, mid1_ref, seed0_ref, seed1_ref, mod_ref, ga_ref, gf_ref, db_ref,
    cond_ref, u0_ref, u1_ref, out_ref, all_ref,
):
    half = half_ref[...] + got_ref[...]
    mid = mid0_ref[...] + mid1_ref[...]
    seeds = seed0_ref[0:1, :] + seed1_ref[0:1, :]
    d = half.shape[1]
    s_att, s_feed = half[1:2], mid[2:3]
    all_ref[...] = jnp.zeros_like(all_ref)
    all_ref[0:1, : cond_ref.shape[1]] = cond_ref[...].astype(F32)
    rows = (
        half[0:1], s_att * ga_ref[...].astype(F32), mid[0:1], mid[1:2],
        s_feed * gf_ref[...].astype(F32), half[2:3] + seeds * db_ref[...].astype(F32),
        (1.0 + mod_ref[1:2]) * s_att, (1.0 + mod_ref[4:5]) * s_feed, mod_ref[5:6] * seeds,
    )
    for i, row in enumerate(rows):
        all_ref[i + 1 : i + 2, :] = row
    for i in range(u0_ref.shape[1] // d):
        cols = slice(i * d, (i + 1) * d)
        all_ref[10 + i : 11 + i, :] = u0_ref[:, cols] + u1_ref[:, cols]
    out_ref[...] = all_ref[...].astype(BF)


def collect(half, got, mids, seeds, mod, ga, gf, db, cond, ubs):
    d = half.shape[1]
    rows = -(-(10 + ubs[0].shape[1] // d) // 16) * 16
    return pl.pallas_call(
        collect_kernel,
        in_specs=[VMEM] * 13,
        out_specs=VMEM,
        out_shape=shape((rows, d), BF),
        scratch_shapes=[pltpu.VMEM((rows, d), F32)],
        compiler_params=params(4),
        cost_estimate=cost(1),
    )(half, got, *mids, *seeds, mod, ga, gf, db, cond, *ubs)


def finish_kernel(every_ref, weight_ref, bias_ref, one_ref, two_ref, down_ref, up_ref):
    d = every_ref.shape[2]
    cond = every_ref[:, 0, :]

    def summed(j):
        return jnp.sum(every_ref[:, j, :].astype(F32), axis=0, keepdims=True)

    for j in range(6):
        rows = every_ref[:, 1 + j, :]
        weight_ref[:, j * d : (j + 1) * d] = mm(cond[:, : weight_ref.shape[0]], rows, TN)
        bias_ref[j * d : (j + 1) * d] = summed(1 + j).reshape(d)
    one_ref[...] = summed(7).reshape(d)
    two_ref[...] = summed(8).reshape(d)
    down_ref[...] = summed(9).reshape(d)
    for j in range(up_ref.shape[0] // d):
        up_ref[j * d : (j + 1) * d] = summed(10 + j).reshape(d)


def finish(every, cond_dim, f):
    d = every.shape[2]
    return pl.pallas_call(
        finish_kernel,
        in_specs=[VMEM],
        out_specs=[VMEM] * 6,
        out_shape=[shape((cond_dim, 6 * d)), shape((6 * d,))]
        + [shape((d,))] * 3
        + [shape((f,))],
        compiler_params=params(12),
        cost_estimate=cost(2),
    )(every)


def together(*values):
    return lax.optimization_barrier(values)


def perm(dp_size, move):
    pairs = []
    for index in range(dp_size):
        for y in range(2):
            to = move(index >> 2, (index >> 1) & 1, y, index & 1)
            pairs.append((index * 2 + y, ((to[0] * 2 + to[1]) * 2 + to[3]) * 2 + to[2]))
    return pairs


def xor_order(stack, me, bits):
    for b in range(bits):
        shaped = stack.reshape((-1, 2, 1 << b) + stack.shape[1:])
        flipped = jnp.concatenate([shaped[:, 1:], shaped[:, :1]], axis=1)
        stack = jnp.where(((me >> b) & 1) == 1, flipped, shaped).reshape(stack.shape)
    return stack


def per_device(
    tokens,
    conditioning,
    lengths,
    input_weight,
    output_weight,
    up_weight,
    up_bias,
    down_weight,
    down_bias,
    attention_gain,
    feed_gain,
    adaptive_weight,
    adaptive_bias,
    cotangent,
):
    n, d = tokens.shape
    assert lengths.shape[0] == 1
    inner = input_weight.shape[2]
    f = up_weight.shape[1]
    dp_size = lax.axis_size("dp")
    planes = dp_size // 4
    zbits = planes.bit_length() - 1
    index = lax.axis_index("dp")
    y = lax.axis_index("tensor")
    c = index % 2
    x = (index // 2) % 2
    z = index // 4
    side = y.astype(jnp.int32).reshape(1)

    make = functools.partial(perm, dp_size)
    y_swap = make(lambda z, x, y, c: (z, x, 1 - y, c))
    core_swap = make(lambda z, x, y, c: (z, x, y, 1 - c))
    x_swap = make(lambda z, x, y, c: (z, 1 - x, y, c))

    def send(value, how):
        return lax.ppermute(value, AXES, how)

    gain_a = attention_gain.reshape(1, d)
    gain_f = feed_gain.reshape(1, d)
    up_b = up_bias.reshape(1, f)

    mod, normed_t, q, k, v, cosine, sine = project(
        lengths, tokens, conditioning, adaptive_weight, adaptive_bias, attention_gain,
        input_weight,
    )
    halves = (0, 1)
    att, linv, e, branch, branch_got = [], [], [], [], []
    for h in halves:
        got = attend(h, lengths, q, k, v, output_weight)
        for store, value in zip((att, linv, e, branch), got):
            store.append(value)
        if h == 0:
            branch[0], k = together(branch[0], k)
        branch_got.append(send(branch[h], y_swap))
    fed, fng_got = [], []
    for h in halves:
        fed.append(
            feed(
                h, lengths, tokens, branch[h], branch_got[h], cotangent, mod, gain_f, up_b,
                up_weight, down_weight,
            )
        )
        fng_sent = fed[h][6]
        if h == 0:
            fng_sent, branch_got[1] = together(fng_sent, branch_got[1])
        fng_got.append(send(fng_sent, y_swap))
    middle, fin_t, act, ug, fg_t, fo, fng, ubg, seed_sums = zip(*fed)

    r_out = d // dp_size

    def cut(couples, chunk):
        if r_out % 16 == 0:
            place = [
                (((z ^ m) * 2 + (x ^ dx)) * 2 + (c ^ s)) * r_out
                for s in range(2)
                for dx in range(2)
                for m in range(planes)
            ]
            starts = jnp.stack([p.astype(jnp.int32) for p in place])
            outs = weight_grad(couples, starts, 2, 2 * planes, r_out, chunk)
        else:
            grad = jnp.concatenate(
                [
                    mm(jnp.concatenate(a, axis=1), jnp.concatenate(b)).astype(BF)
                    for a, bs in couples
                    for b in bs
                ],
                axis=1,
            )
            blocks = grad.reshape(planes, 2, 2, r_out, grad.shape[1])
            blocks = xor_order(blocks, z, zbits).transpose(2, 1, 0, 3, 4)
            blocks = xor_order(blocks, c, 1)
            outs = [xor_order(b, x, 1) for b in blocks]
        return [o.reshape(2, planes, r_out, -1) for o in outs]

    def send_z(total):
        return [
            send(total[m].astype(BF), make(lambda z, x, y, c: (z ^ m, x, y, c)))
            for m in range(1, planes)
        ]

    def sum_z(total, got):
        return sum((v.astype(F32) for v in got), total[0])

    feed_own, feed_far = cut([(fg_t, [act]), (fin_t, [ug])], f // 2)
    feed_core_got = send(feed_far, core_swap)
    fng_got[0], feed_own = together(fng_got[0], feed_own)

    mids, backs = [], []
    for h in halves:
        mids.append(
            middle_back(
                h, lengths, middle[h], fng[h], fng_got[h], cotangent, branch[h], branch_got[h],
                mod, gain_f, output_weight,
            )
        )
        if h == 0:
            feed_core_got, do = together(feed_core_got, mids[0][2])
            feed_near = feed_own[0].astype(F32) + feed_core_got[0].astype(F32)
            feed_far = (feed_own[1].astype(F32) + feed_core_got[1].astype(F32)).astype(BF)
            do, feed_far = together(do, feed_far)
            feed_x_got = send(feed_far, x_swap)
        else:
            do = mids[1][2]
        backs.append(
            attend_back(
                h, q, k, v, att[h], linv[h], e[h], do, cosine, sine, backs[0][1:] if h else ()
            )
        )
        if h == 0:
            fng_got[1], fo_sent, _ = together(
                fng_got[1], jnp.where(y == 0, fo[1], fo[0]), backs[0][0]
            )
            fo_got = send(fo_sent, y_swap)
    mg, bg_t, _, mid_sums = zip(*mids)
    dqs, (dk, dv) = (backs[0][0], backs[1][0]), backs[1][1:]

    ang_other = input_back(side, dqs, dk, dv, input_weight, False, BF)
    dk, ang_other, fo_got = together(dk, ang_other, fo_got)
    ang_got = send(ang_other, y_swap)
    attn_own, attn_far = cut([(bg_t, [att]), ([normed_t], [dqs, [dk], [dv]])], inner)
    attn_core_got = send(attn_far, core_swap)
    dk, feed_x_got, attn_own = together(dk, feed_x_got, attn_own)
    feed_total = feed_near + feed_x_got.astype(F32)
    feed_total, attn_core_got = together(feed_total, attn_core_got)
    feed_z_got = send_z(feed_total)
    attn_near = attn_own[0].astype(F32) + attn_core_got[0].astype(F32)
    attn_far = (attn_own[1].astype(F32) + attn_core_got[1].astype(F32)).astype(BF)
    attn_far, dk = together(attn_far, dk)
    attn_x_got = send(attn_far, x_swap)
    ang_own = input_back(side, dqs, dk, dv, input_weight, True, F32)
    mixed = mix(side, middle, fo, fo_got, mod, down_bias.reshape(1, d))
    mixed, ang_got, attn_x_got = together(mixed, ang_got, attn_x_got)
    tok_grad, att_sums = final(side, tokens, ang_own, ang_got, mg, mod, gain_a)

    half_sums = jnp.concatenate([att_sums, seed_sums[0][1:] + seed_sums[1][1:]], axis=0)
    flat = collect(
        half_sums, send(half_sums, y_swap), mid_sums, seed_sums, mod, gain_a, gain_f,
        down_bias.reshape(1, d), conditioning, ubg,
    )
    every = lax.all_to_all(
        jnp.broadcast_to(flat[None], (dp_size,) + flat.shape), "dp", 0, 0, tiled=True
    )
    attn_total = attn_near + attn_x_got.astype(F32)
    attn_z_got = send_z(attn_total)
    joined = together(*attn_z_got, *feed_z_got)
    attn_z_got, feed_z_got = joined[: planes - 1], joined[planes - 1 :]
    feed_grads = sum_z(feed_total, feed_z_got)
    down_grad, up_grad = feed_grads[:, :f], feed_grads[:, f:]
    attn_grads = sum_z(attn_total, attn_z_got)
    out_grad, in_grad = attn_grads[:, :inner], attn_grads[:, inner:]
    (
        adaptive_weight_grad, adaptive_bias_grad, attention_gain_grad, feed_gain_grad,
        down_bias_grad, up_bias_grad,
    ) = finish(every.reshape(dp_size, flat.shape[0], d), conditioning.shape[1], f)
    return (
        mixed,
        tok_grad,
        in_grad.reshape(r_out, 3, inner).transpose(1, 0, 2),
        out_grad.T,
        up_grad,
        up_bias_grad,
        down_grad.T,
        down_bias_grad,
        attention_gain_grad,
        feed_gain_grad,
        adaptive_weight_grad,
        adaptive_bias_grad,
    )


def solution(mesh):
    placed = (
        P("dp", None),
        P("dp", None),
        P("dp", None),
        P(None, None, "tensor"),
        P("tensor", None),
        P(None, "tensor"),
        P("tensor"),
        P("tensor", None),
        P(),
        P(),
        P(),
        P(),
        P(),
        P("dp", None),
    )
    return jax.shard_map(
        per_device,
        mesh=mesh,
        in_specs=placed,
        out_specs=(
            P(("dp", "tensor"), None),
            P(("dp", "tensor"), None),
            P(None, "dp", "tensor"),
            P("tensor", "dp"),
            P("dp", "tensor"),
            P("tensor"),
            P("tensor", "dp"),
            P(),
            P(),
            P(),
            P(),
            P(),
        ),
        check_vma=False,
    )
```
